32 devices in a mesh: dp: 8 (over z, x), expert: 4 (over y, core).
Axes of the slice: x: 2, y: 2, z: 4, core: 2. Of those that a mesh axis runs over, the one named last changes fastest.
Arguments:
- tokens: bfloat16 [32768, 768], P(('dp', 'expert')), may hold values from -6 to 6
- cotangent: bfloat16 [32768, 768], P(('dp', 'expert')), may hold values from -6 to 6
- attention_norm_gain: float32 [768], replicated, may hold values from 0.5 to 1.5
- query_key_value_weight: bfloat16 [768, 2304], replicated, may hold values from -0.21875 to 0.21875
- attention_output_weight: bfloat16 [768, 768], replicated, may hold values from -3 to 3
- adapter_attention_down_maps: bfloat16 [4, 768, 128], replicated, may hold values from -0.21875 to 0.21875
- adapter_query_key_value_up_maps: bfloat16 [3, 128, 768], replicated, may hold values from -0.75 to 0.75
- adapter_output_up_map: bfloat16 [128, 768], replicated, may hold values from -6 to 6
- experts_norm_gain: float32 [768], replicated, may hold values from 0.5 to 1.5
- router_weight: bfloat16 [768, 8], replicated, may hold values from -0.15625 to 0.15625
- constant_expert_mixing: bfloat16 [768, 4], replicated, may hold values from -0.21875 to 0.21875
- constant_expert_vectors: float32 [2, 768], replicated, may hold values from -6 to 6
- expert_gate_up_weight: bfloat16 [4, 768, 4096], P('expert'), may hold values from -0.21875 to 0.21875
- expert_down_weight: bfloat16 [4, 2048, 768], P('expert'), may hold values from -0.125 to 0.125
- adapter_expert_gate_up_down_maps: bfloat16 [4, 2, 768, 128], P('expert'), may hold values from -0.21875 to 0.21875
- adapter_expert_gate_up_up_maps: bfloat16 [4, 2, 128, 2048], P('expert'), may hold values from -0.75 to 0.75
- adapter_expert_down_down_maps: bfloat16 [4, 2048, 128], P('expert'), may hold values from -0.125 to 0.125
- adapter_expert_down_up_maps: bfloat16 [4, 128, 768], P('expert'), may hold values from -0.75 to 0.75
- routes: int32 [32768, 2], P(('dp', 'expert')), may hold values from 0 to 7, all different within a row; in each aligned block of 1024 rows (0 to 1023, 1024 to 2047, ...) at most 512 rows name the same one
- router_logits_carried: float32 [32768, 8], P(('dp', 'expert')), may hold values from -3 to 3
- picture_span_starts: int32 [32, 2], P(('dp', 'expert')), may hold values from 0 to 768, as said below
- sequence_adapter_index: int32 [32], replicated, may hold values from 0 to 7
Outputs:
- result: bfloat16 [32768, 768], P(('dp', 'expert'))
- grad_tokens: bfloat16 [32768, 768], P(('dp', 'expert'))
- grad_lora_a_attn: float32 [4, 768, 128], replicated
- grad_lora_b_qkv: float32 [3, 128, 768], replicated
- grad_lora_b_out: float32 [128, 768], replicated
- grad_lora_a_gate_up: float32 [4, 2, 768, 128], P('expert')
- grad_lora_b_gate_up: float32 [4, 2, 128, 2048], P('expert')
- grad_lora_a_down: float32 [4, 2048, 128], P('expert')
- grad_lora_b_down: float32 [4, 128, 768], P('expert')
The draws below stay inside these ranges and needn't reach their ends.
Inputs may be any that keep to these rules, and one draw needn't show every extreme that they name: `routes`: each token names two different targets. Within the 1024 rows of one sequence no target is named by more than 512 rows, and in some sequences one target is named by exactly 512 rows. `picture_span_starts`: the j-th picture span of a sequence starts within positions j * (512) to (j + 1) * 512 - 256, so spans never intersect and end inside the sequence. Sequence s uses adapter sequence_adapter_index[s].
All inputs are finite; a program needn't handle non-finite values.
Results may differ from the reference program's by a relative error of at most 0.018.
Values may be sent and summed in bfloat16 or wider, within the bound.
A program may use at most 448 MiB of HBM per device.

```python
import math
import jax
import jax.numpy as jnp
import numpy as np
from jax import lax

MODEL_WIDTH = 768
HEADS = 12
HD = 64
EXPERT_HIDDEN = 2048
EXPERT_COUNT = 4
NR = 8
ADAPTER_RANK = 16
NA = 8
ADAPTER_COLUMNS = 128
SEQ = 1024
PIC = 256
NPIC = 2
CAP = 512
SEQS = 32
TOKENS = 32768


def draw_picture_span_starts(key, part):
    stride = SEQ // NPIC
    offsets = jax.random.randint(key, (SEQS, NPIC), 0, stride - PIC + 1)
    offsets = offsets.at[0, NPIC - 1].set(stride - PIC)
    offsets = offsets.at[1, 0].set(0)
    return (offsets + (jnp.arange(NPIC, dtype=jnp.int32) * stride)[None, :]).astype(jnp.int32)


def set_ends(values, rng, low, largest):
    longest = values.shape.index(max(values.shape))
    spots = []
    for shift in (0, 1):
        where = [jax.random.randint(jax.random.fold_in(rng, axis), (), 0, length) for axis, length in enumerate(values.shape)]
        where[longest] = (where[longest] + shift) % values.shape[longest]
        spots.append(tuple(where))
    return values.at[spots[0]].set(low).at[spots[1]].set(largest)


def block_levels(own_key, shape, shards, least, top_value):
    gain = 1.0
    for dim, blocks in shards:
        steps = jax.random.uniform(jax.random.fold_in(jax.random.fold_in(own_key, 6), dim), (blocks,), jnp.float32, least / len(shards), top_value / len(shards))
        gain = gain * jnp.repeat(jnp.exp(steps), shape[dim] // blocks).reshape((-1,) + (1,) * (len(shape) - 1 - dim))
    return gain


def shared_out(key, own, number, rows, count, top, bound, lean):
    sequence = jax.random.permutation(key, count)
    heavy_load, usual = shares(count, rows * top, bound, lean, True), shares(count, rows * top, bound, lean, False)
    places = jnp.arange(count)

    def named(lengths, rotation):
        used = int((lengths > 0).sum())
        fixed = max(1, used // 4)
        passed = fixed + (places - fixed + rotation * (used - fixed)) % max(1, count - fixed)
        return jnp.zeros((count,), jnp.int32).at[sequence[jnp.where(places < fixed, places, passed)]].set(jnp.asarray(lengths, jnp.int32))

    lengths = jnp.where(number % 4 == 0, named(heavy_load, number // 4), named(usual, number - number // 4 - 1))
    mixed = jax.random.permutation(jax.random.fold_in(own, 3), count)
    source_of, taker = mixed[0:count // 2 * 2:2], mixed[1:count // 2 * 2:2]
    margin = jnp.minimum(lengths[source_of] - 1, bound - lengths[taker]) // 2
    margin = jnp.where((source_of == sequence[0]) | (taker == sequence[0]) | (lengths[taker] == 0), 0, jnp.maximum(margin, 0))
    passed = jax.random.randint(jax.random.fold_in(own, 4), (count // 2,), 0, 1 << 20) % (margin + 1)
    lengths = lengths.at[source_of].add(-passed).at[taker].add(passed)
    members = jnp.searchsorted(jnp.cumsum(lengths), jnp.arange(rows * top), side="right").astype(jnp.int32)
    grid = members.reshape(top, rows).T
    grid = grid[jax.random.permutation(jax.random.fold_in(own, 1), rows)]
    rotation = jax.random.randint(jax.random.fold_in(own, 2), (rows, 1), 0, top)
    return jnp.take_along_axis(grid, (jnp.arange(top)[None, :] + rotation) % top, axis=1)


def shares(amount, total, reach, slope, full):
    loads = [(1 << 20) // math.isqrt(grade ** slope) + 1 for grade in range(1, amount + 1)]
    largest = reach if full else min(reach, max(-(-total // amount), total * loads[0] // sum(loads)))
    least = 1 if total - largest >= amount - 1 else 0
    counts, spare = [largest] + [least] * (amount - 1), total - largest - least * (amount - 1)
    while spare > 0:
        candidates = [i for i in range(1, amount) if counts[i] < largest] or [i for i in range(1, amount) if counts[i] < reach]
        whole, remaining = sum([loads[i] for i in candidates]), spare
        for i in candidates:
            more = min(reach - counts[i], max(1, remaining * loads[i] // whole), spare)
            counts[i] = counts[i] + more
            spare = spare - more
    return np.array(counts)


def normal_values(key, extent, spread, reach, cuts=(), kind=jnp.bfloat16):
    drawn = spread * jax.random.normal(key, extent, jnp.float32)
    if cuts:
        drawn = drawn * block_levels(key, extent, cuts, -0.22, 0.18)
    return jnp.clip(drawn, -reach, reach).astype(kind)


def setup_inputs(seed: int = 0) -> dict:
    streams_of = jax.random.split(jax.random.key(seed), 23)
    tokens = normal_values(streams_of[0], (TOKENS, MODEL_WIDTH), 1.0, 6.0, ((0, 32),))
    cotangent = normal_values(streams_of[1], (TOKENS, MODEL_WIDTH), 1.0, 6.0, ((0, 32),))
    attention_norm_gain = jnp.clip(1.0 + 0.1 * jax.random.normal(streams_of[2], (MODEL_WIDTH,), jnp.float32), 0.5, 1.5)
    query_key_value_weight = normal_values(streams_of[3], (MODEL_WIDTH, 3 * MODEL_WIDTH), MODEL_WIDTH ** -0.5, 0.21875)
    attention_output_weight = normal_values(streams_of[4], (MODEL_WIDTH, MODEL_WIDTH), (MODEL_WIDTH // 256 + 1) ** -0.5, 3.0)
    adapter_attention_down_maps = normal_values(streams_of[5], (4, MODEL_WIDTH, ADAPTER_COLUMNS), MODEL_WIDTH ** -0.5, 0.21875)
    adapter_query_key_value_up_maps = normal_values(streams_of[6], (3, ADAPTER_COLUMNS, MODEL_WIDTH), (4 * ADAPTER_RANK) ** -0.5, 0.75)
    adapter_output_up_map = normal_values(streams_of[7], (ADAPTER_COLUMNS, MODEL_WIDTH), 1 ** -0.5, 6.0)
    experts_norm_gain = jnp.clip(1.0 + 0.1 * jax.random.normal(streams_of[8], (MODEL_WIDTH,), jnp.float32), 0.5, 1.5)
    router_weight = normal_values(streams_of[9], (MODEL_WIDTH, NR), (2 * MODEL_WIDTH) ** -0.5, 0.15625)
    constant_expert_mixing = normal_values(streams_of[10], (MODEL_WIDTH, 4), MODEL_WIDTH ** -0.5, 0.21875)
    constant_expert_vectors = normal_values(streams_of[11], (2, MODEL_WIDTH), 1.0, 6.0, (), jnp.float32)
    expert_gate_up_weight = normal_values(streams_of[12], (EXPERT_COUNT, MODEL_WIDTH, 2 * EXPERT_HIDDEN), MODEL_WIDTH ** -0.5, 0.21875, ((0, 4),))
    expert_down_weight = normal_values(streams_of[13], (EXPERT_COUNT, EXPERT_HIDDEN, MODEL_WIDTH), EXPERT_HIDDEN ** -0.5, 0.125, ((0, 4),))
    adapter_expert_gate_up_down_maps = normal_values(streams_of[14], (EXPERT_COUNT, 2, MODEL_WIDTH, ADAPTER_COLUMNS), MODEL_WIDTH ** -0.5, 0.21875, ((0, 4),))
    adapter_expert_gate_up_up_maps = normal_values(streams_of[15], (EXPERT_COUNT, 2, ADAPTER_COLUMNS, EXPERT_HIDDEN), (4 * ADAPTER_RANK) ** -0.5, 0.75, ((0, 4),))
    adapter_expert_down_down_maps = normal_values(streams_of[16], (EXPERT_COUNT, EXPERT_HIDDEN, ADAPTER_COLUMNS), EXPERT_HIDDEN ** -0.5, 0.125, ((0, 4),))
    adapter_expert_down_up_maps = normal_values(streams_of[17], (EXPERT_COUNT, ADAPTER_COLUMNS, MODEL_WIDTH), (4 * ADAPTER_RANK) ** -0.5, 0.75, ((0, 4),))
    routes_keys = jax.random.split(jax.random.fold_in(streams_of[18], 1), TOKENS // SEQ)
    routes_turns = jax.random.permutation(jax.random.fold_in(streams_of[18], 3), TOKENS // SEQ)
    routes = jax.vmap(lambda own, number: shared_out(jax.random.fold_in(streams_of[18], 2), own, number, SEQ, NR, 2, CAP, 1))(routes_keys, routes_turns).reshape((TOKENS, 2))
    router_logits_carried = normal_values(streams_of[19], (TOKENS, NR), 0.5, 3.0, ((0, 32),), jnp.float32)
    picture_span_starts = draw_picture_span_starts(jax.random.fold_in(streams_of[22], 71), 0)
    sequence_adapter_index = set_ends(jax.random.randint(streams_of[21], (SEQS,), 0, NA), jax.random.fold_in(streams_of[21], 1), 0, NA - 1).astype(jnp.int32)
    return {"tokens": tokens, "cotangent": cotangent, "attention_norm_gain": attention_norm_gain, "query_key_value_weight": query_key_value_weight, "attention_output_weight": attention_output_weight, "adapter_attention_down_maps": adapter_attention_down_maps, "adapter_query_key_value_up_maps": adapter_query_key_value_up_maps, "adapter_output_up_map": adapter_output_up_map, "experts_norm_gain": experts_norm_gain, "router_weight": router_weight, "constant_expert_mixing": constant_expert_mixing, "constant_expert_vectors": constant_expert_vectors, "expert_gate_up_weight": expert_gate_up_weight, "expert_down_weight": expert_down_weight, "adapter_expert_gate_up_down_maps": adapter_expert_gate_up_down_maps, "adapter_expert_gate_up_up_maps": adapter_expert_gate_up_up_maps, "adapter_expert_down_down_maps": adapter_expert_down_down_maps, "adapter_expert_down_up_maps": adapter_expert_down_up_maps, "routes": routes, "router_logits_carried": router_logits_carried, "picture_span_starts": picture_span_starts, "sequence_adapter_index": sequence_adapter_index}


HIGH_ACCURACY = lax.Precision.HIGHEST
EPS = 1e-06

@jax.custom_vjp
def low(v):
    return lax.optimization_barrier(v.astype(jnp.bfloat16)).astype(jnp.float32)

@jax.custom_vjp
def low_back(v):
    return v

def low_keep(v):
    return (low(v), None)

def low_pass(kept, grad):
    return (grad,)

def back_keep(v):
    return (v, None)

def back_low(kept, grad):
    return (low(grad),)
low.defvjp(low_keep, low_pass)
low_back.defvjp(back_keep, back_low)

def rms_scale(inputs, weights):
    return inputs * lax.rsqrt(lax.optimization_barrier(jnp.mean(inputs * inputs, axis=-1, keepdims=True)) + EPS) * weights

def rotate(inputs, cosine, sine):
    halfway = inputs.shape[-1] // 2
    turned = jnp.concatenate([-inputs[..., halfway:], inputs[..., :halfway]], axis=-1)
    return inputs * cosine[:, None, :] + turned * sine[:, None, :]

def tables(length):
    positions = jnp.arange(length, dtype=jnp.float32)
    spacing = 10000.0 ** (-jnp.arange(0, HD, 2, dtype=jnp.float32) / HD)
    angles = positions[:, None] * spacing[None, :]
    angles = jnp.concatenate([angles, angles], axis=1)
    return (jnp.cos(angles), jnp.sin(angles))

def span_index(starts, length):
    positions = jnp.arange(length, dtype=jnp.int32)
    inside = (positions[None, :] >= starts[:, None]) & (positions[None, :] < starts[:, None] + PIC)
    labels = jnp.arange(starts.shape[0], dtype=jnp.int32)[:, None] + 1
    return lax.optimization_barrier(jnp.sum(inside.astype(jnp.int32) * labels, axis=0))

def visible(offset, block_rows, labels, length):
    query_pos = offset + jnp.arange(block_rows, dtype=jnp.int32)
    key_pos = jnp.arange(length, dtype=jnp.int32)
    query_lab = lax.dynamic_slice_in_dim(labels, offset, block_rows, 0)
    causal = key_pos[None, :] <= query_pos[:, None]
    return causal | (query_lab[:, None] == labels[None, :]) & (query_lab[:, None] > 0)

def mix_experts(normed, gathered, linear, residual, routes, constant_expert_vectors, experts):
    length = normed.shape[0]
    logits = linear[:, :experts + 4] + residual
    targets = jnp.arange(experts + 4, dtype=jnp.int32)
    picks = (routes[:, :, None] == targets[None, None, :]).astype(jnp.float32)
    chosen = lax.optimization_barrier(jnp.sum(picks * logits[:, None, :], axis=2))
    gates = jax.nn.softmax(chosen, axis=1)
    mixes = jax.nn.softmax(linear[:, experts + 4:].reshape(length, 2, 2), axis=2)
    constant = mixes[:, :, 0:1] * normed[:, None, :] + mixes[:, :, 1:2] * constant_expert_vectors[None, :, :]
    copied = picks[:, :, experts + 1:experts + 2] * normed[:, None, :]
    fixed_out = picks[:, :, experts + 2:experts + 3] * constant[:, 0:1, :] + picks[:, :, experts + 3:experts + 4] * constant[:, 1:2, :]
    return lax.optimization_barrier(jnp.sum(gates[:, :, None] * (gathered + copied + fixed_out), axis=1))

def attend_block(offset, queries, keys_all, values_all, labels, block_rows):
    length = keys_all.shape[0]
    query_blk = lax.dynamic_slice_in_dim(queries, offset, block_rows, 0)
    allowed = visible(offset, block_rows, labels, length)
    raw_scores = jnp.einsum('qhd,khd->hqk', query_blk, keys_all, precision=HIGH_ACCURACY)
    scores = jnp.where(allowed[None], low_back(raw_scores) * 0.125, -1e+30)
    weights = low(jax.nn.softmax(scores, axis=2))
    return jnp.einsum('hqk,khd->qhd', weights, values_all, precision=HIGH_ACCURACY)

def experts_forward(holding_buffer, adapter_select_mask, expert_gate_up_weight, expert_down_weight, gate_up_down_map, gate_up_up_map, a_down, b_down):
    base = jnp.einsum('ecd,edf->ecf', holding_buffer, expert_gate_up_weight, precision=HIGH_ACCURACY)
    adapter_input = low(low_back(jnp.einsum('vfz,vbzy->vbfy', holding_buffer, gate_up_down_map, precision=HIGH_ACCURACY) * adapter_select_mask))
    extra_terms = jnp.einsum('tjid,tjdk->tjik', adapter_input, gate_up_up_map, precision=HIGH_ACCURACY)
    gate_values = low_back(base[:, :, :EXPERT_HIDDEN] + extra_terms[:, 0])
    up_projection_part = low_back(base[:, :, EXPERT_HIDDEN:] + extra_terms[:, 1])
    hidden_state = low(jax.nn.silu(gate_values) * up_projection_part)
    down_projection_input = low(low_back(jnp.einsum('ecf,efr->ecr', hidden_state, a_down, precision=HIGH_ACCURACY) * adapter_select_mask))
    summed = jnp.einsum('ecf,efd->ecd', hidden_state, expert_down_weight, precision=HIGH_ACCURACY) + jnp.einsum('ecr,erd->ecd', down_projection_input, b_down, precision=HIGH_ACCURACY)
    return low(low_back(summed))

def one_sequence(h_start, route, residual, starts, adapter, frozen, trainable_params):
    attention_norm_gain, query_key_value_weight, attention_output_weight, experts_norm_gain, router_weight, constant_expert_mixing, constant_expert_vectors, expert_gate_up_weight, expert_down_weight = frozen
    attention_down_map, query_key_value_up_map, output_up_map, gate_up_down_map, gate_up_up_map, a_down, b_down = trainable_params
    length = h_start.shape[0]
    adapter_select_mask = (jnp.arange(NA * ADAPTER_RANK, dtype=jnp.int32) // ADAPTER_RANK == adapter).astype(jnp.float32)
    attention_input = low(rms_scale(h_start, attention_norm_gain))
    adapter_query_key_value = low(low_back(jnp.einsum('cz,mzg->mcg', attention_input, attention_down_map[:3], precision=HIGH_ACCURACY) * adapter_select_mask))
    linear_output = jnp.dot(attention_input, query_key_value_weight, precision=HIGH_ACCURACY).reshape(length, 3, MODEL_WIDTH)
    linear_output = low_back(linear_output + jnp.einsum('uaj,ujy->auy', adapter_query_key_value, query_key_value_up_map, precision=HIGH_ACCURACY))
    cosine, sine = tables(length)
    queries = low(rotate(linear_output[:, 0].reshape(length, HEADS, HD), cosine, sine))
    keys_all = low(rotate(linear_output[:, 1].reshape(length, HEADS, HD), cosine, sine))
    values_all = low(linear_output[:, 2].reshape(length, HEADS, HD))
    labels = span_index(starts, length)
    block_rows = min(1024, length)

    def one_block(offset):
        return attend_block(offset, queries, keys_all, values_all, labels, block_rows)
    blocks = lax.map(jax.checkpoint(one_block), jnp.arange(0, length, block_rows, dtype=jnp.int32))
    attention_output = low(low_back(blocks.reshape(length, MODEL_WIDTH)))
    adapter_output = low(low_back(jnp.dot(attention_output, attention_down_map[3], precision=HIGH_ACCURACY) * adapter_select_mask))
    branch_output = low_back(jnp.dot(attention_output, attention_output_weight, precision=HIGH_ACCURACY) + jnp.dot(adapter_output, output_up_map, precision=HIGH_ACCURACY))
    h_mid = h_start + branch_output
    normed = rms_scale(h_mid, experts_norm_gain)
    sent = low(normed)
    linear_router = jnp.dot(sent, jnp.concatenate([router_weight, constant_expert_mixing], axis=1), precision=HIGH_ACCURACY)
    targets = route.reshape(-1)
    one_hot = (targets[:, None] == jnp.arange(EXPERT_COUNT, dtype=jnp.int32)[None, :]).astype(jnp.int32)
    slot_index = lax.optimization_barrier(jnp.sum((jnp.cumsum(one_hot, axis=0) - 1) * one_hot, axis=1))
    places = jnp.where(targets < EXPERT_COUNT, targets * CAP + slot_index, EXPERT_COUNT * CAP)
    entries = jnp.stack([low_back(sent), low_back(sent)], axis=1).reshape(2 * length, MODEL_WIDTH)
    holding_buffer = jnp.zeros((EXPERT_COUNT * CAP + 1, MODEL_WIDTH), jnp.float32).at[places].set(entries)[:EXPERT_COUNT * CAP].reshape(EXPERT_COUNT, CAP, MODEL_WIDTH)
    out_rows = experts_forward(holding_buffer, adapter_select_mask, expert_gate_up_weight, expert_down_weight, gate_up_down_map, gate_up_up_map, a_down, b_down)
    padded = jnp.concatenate([out_rows.reshape(EXPERT_COUNT * CAP, MODEL_WIDTH), jnp.zeros((1, MODEL_WIDTH), jnp.float32)], axis=0)
    gathered = padded[places].reshape(length, 2, MODEL_WIDTH)
    return h_mid + mix_experts(normed, gathered, linear_router, residual, route, constant_expert_vectors, EXPERT_COUNT)

def reference(tokens, cotangent, attention_norm_gain, query_key_value_weight, attention_output_weight, adapter_attention_down_maps, adapter_query_key_value_up_maps, adapter_output_up_map, experts_norm_gain, router_weight, constant_expert_mixing, constant_expert_vectors, expert_gate_up_weight, expert_down_weight, adapter_expert_gate_up_down_maps, adapter_expert_gate_up_up_maps, adapter_expert_down_down_maps, adapter_expert_down_up_maps, routes, router_logits_carried, picture_span_starts, sequence_adapter_index):
    frozen = tuple((current_item.astype(jnp.float32) for current_item in (attention_norm_gain, query_key_value_weight, attention_output_weight, experts_norm_gain, router_weight, constant_expert_mixing, constant_expert_vectors, expert_gate_up_weight, expert_down_weight)))
    trainable_params = tuple((current_item.astype(jnp.float32) for current_item in (adapter_attention_down_maps, adapter_query_key_value_up_maps, adapter_output_up_map, adapter_expert_gate_up_down_maps, adapter_expert_gate_up_up_maps, adapter_expert_down_down_maps, adapter_expert_down_up_maps)))
    count = TOKENS // SEQ

    def forward(h_start, weights):

        def per_sequence(current_item):
            return one_sequence(current_item[0], current_item[1], current_item[2], current_item[3], current_item[4], frozen, weights)
        pieces = (h_start.reshape(count, SEQ, MODEL_WIDTH), routes.reshape(count, SEQ, 2), router_logits_carried.reshape(count, SEQ, EXPERT_COUNT + 4), picture_span_starts, sequence_adapter_index)
        return lax.map(jax.checkpoint(per_sequence), pieces).reshape(TOKENS, MODEL_WIDTH)
    output, pull = jax.vjp(forward, tokens.astype(jnp.float32), trainable_params)
    grad_in, grads = pull(cotangent.astype(jnp.float32))
    return (output.astype(jnp.bfloat16), grad_in.astype(jnp.bfloat16), grads[0], grads[1], grads[2], grads[3], grads[4], grads[5], grads[6])
```

```python
import functools

import jax
import jax.numpy as jnp
import numpy as np
from jax import lax
from jax.experimental import pallas as pl
from jax.experimental.pallas import tpu as pltpu
from jax.sharding import PartitionSpec as P

HEADS = 12
HD = 64
RANK = 16
PIC = 256
GROUP = 256
HALF = 512
EPS = 1e-06
NEG = -1e30
BF = jnp.bfloat16
F32 = jnp.float32
MIB = 1024 * 1024


def mm(a, b):
    return jnp.dot(a, b, preferred_element_type=F32)


def mm_t(a, b):
    return lax.dot_general(a, b, (((1,), (1,)), ((), ())), preferred_element_type=F32)


def t_mm(a, b):
    return lax.dot_general(a, b, (((0,), (0,)), ((), ())), preferred_element_type=F32)


def iota(shape, dim):
    return lax.broadcasted_iota(jnp.int32, shape, dim)


def one_hot(condition):
    return jnp.where(condition, 1.0, 0.0).astype(BF)


def picker(adapter, place, rows=128, columns=128):
    row, column = iota((rows, columns), 0), iota((rows, columns), 1)
    return one_hot((row - adapter * RANK == column - place * RANK) & (column // RANK == place))


def placer(adapter, place, rows=128, columns=128):
    row, column = iota((rows, columns), 0), iota((rows, columns), 1)
    return one_hot((column - adapter * RANK == row - place * RANK) & (row // RANK == place))


def head_order(back):
    row, column = iota((GROUP, GROUP), 0), iota((GROUP, GROUP), 1)
    a, b = (column, row) if back else (row, column)
    return one_hot(a == (b % 128 // 32) * 64 + b // 128 * 32 + b % 32)


def rope_tables(length):
    spacing = 10000.0 ** (-np.arange(0, HD, 2, dtype=np.float32) / np.float32(HD))
    angles = np.arange(length, dtype=np.float32)[:, None] * spacing.astype(np.float32)[None, :]
    angles = np.tile(angles, (1, 4))
    return np.cos(angles).astype(np.float32), np.sin(angles).astype(np.float32)


def rope(pair, cosine, sine):
    low, high = pair[:, :128], pair[:, 128:]
    return jnp.concatenate([low * cosine - high * sine, high * cosine + low * sine], axis=1)


def span_bias(start, transposed):
    a, b = iota((HALF, HALF), 0), iota((HALF, HALF), 1)
    query, key = (b, a) if transposed else (a, b)
    inside = (query >= start) & (query < start + PIC) & (key >= start) & (key < start + PIC)
    return jnp.where((key <= query) | inside, 0.0, NEG)


def attention_forward_kernel(
    spans, adapter_ref, tok, gain_a, wqkv, down, up, wo, up_out, gain_m, wr, cos, sin,
    xa_ref, q_ref, k_ref, v_ref, ob_ref, ua_ref, uo_ref, lse_ref, h1_ref, xb_ref, lin_ref, wqk_ref,
    down_ref, up_s,
    bias,
):
    length, width = tok.shape
    groups = width // GROUP
    adapter = adapter_ref[0]
    order = head_order(False)
    down_s = sum(mm(down[p], picker(adapter, p)) for p in range(3)).astype(BF)
    down_o = mm(down[3], picker(adapter, 0)).astype(BF)
    up_o = mm(placer(adapter, 0), up_out[...]).astype(BF)
    down_ref[0] = down_s
    down_ref[1] = down_o
    up_s[:, pl.ds(3 * width, width)] = up_o
    for p in range(3):
        rows = mm(placer(adapter, p), up[p]).astype(BF)
        for g in range(groups):
            block = rows[:, g * GROUP : (g + 1) * GROUP]
            if p < 2:
                block = mm(block, order).astype(BF)
            up_s[:, pl.ds(p * width + g * GROUP, GROUP)] = block
    for g in range(2 * groups):
        at = pl.ds(g * GROUP, GROUP)
        wqk_ref[:, at] = mm(wqkv[:, at], order).astype(BF)
    for half in range(length // HALF):
        bias[half] = span_bias(spans[half] - half * HALF, False)

    def project(block, carry):
        at = pl.ds(pl.multiple_of(block * 256, 256), 256)
        h0 = tok[at, :].astype(F32)
        x = h0 * lax.rsqrt(jnp.mean(h0 * h0, axis=1, keepdims=True) + EPS) * gain_a[...]
        x = x.astype(BF)
        xa_ref[at, :] = x
        u = mm(x, down_s).astype(BF)
        ua_ref[at, :] = u
        c, s = cos[at, :], sin[at, :]
        for p, out in enumerate((q_ref, k_ref)):
            for g in range(groups):
                lanes = pl.ds(p * width + g * GROUP, GROUP)
                lin = mm(x, wqk_ref[:, lanes]) + mm(u, up_s[:, lanes])
                out[at, pl.ds(g * GROUP, GROUP)] = rope(lin, c, s).astype(BF)
        lanes = pl.ds(2 * width, width)
        v_ref[at, :] = (mm(x, wqkv[:, lanes]) + mm(u, up_s[:, lanes])).astype(BF)
        return carry

    lax.fori_loop(0, length // 256, project, 0)

    lane = iota((1, GROUP), 1)
    lse_ref[...] = jnp.zeros(lse_ref.shape, F32)
    ob_f = ob_ref

    def attend(head, carry):
        g, h = head // 4, head % 4
        lanes = pl.ds(pl.multiple_of(g * GROUP, GROUP), GROUP)
        qk_own = jnp.where((lane % 128) // 32 == h, 1.0, 0.0).astype(BF)
        v_own = jnp.where(lane // 64 == h, 1.0, 0.0)
        kh = k_ref[:, lanes] * qk_own
        vh = v_ref[:, lanes] * v_own.astype(BF)
        for half in range(length // HALF):
            at = pl.ds(half * HALF, HALF)
            q = q_ref[at, lanes] * BF(0.125)
            keys = (half + 1) * HALF
            diag = mm_t(q, kh[half * HALF : keys]) + bias[half]
            top = jnp.max(diag, axis=1, keepdims=True)
            if half:
                past = mm_t(q, kh[: half * HALF])
                top = jnp.maximum(top, jnp.max(past, axis=1, keepdims=True))
            e = jnp.exp(diag - top)
            total = jnp.sum(e, axis=1, keepdims=True)
            o = mm(e.astype(BF), vh[half * HALF : keys])
            if half:
                e = jnp.exp(past - top)
                total = total + jnp.sum(e, axis=1, keepdims=True)
                o = o + mm(e.astype(BF), vh[: half * HALF])
            o = o * pl.reciprocal(total, approx=False)
            lse = top + jnp.log(total)
            lse_ref[at, :] = jnp.where(iota((1, 128), 1) == head, lse, lse_ref[at, :])
            old = jnp.where(v_own > 0.5, 0.0, ob_f[at, lanes].astype(F32))
            ob_f[at, lanes] = jnp.where(v_own > 0.5, o, old).astype(BF)
        return carry

    lax.fori_loop(0, HEADS, attend, 0)

    def finish(block, carry):
        at = pl.ds(pl.multiple_of(block * 256, 256), 256)
        o = ob_ref[at, :]
        u = mm(o, down_o).astype(BF)
        uo_ref[at, :] = u
        h1 = tok[at, :].astype(F32) + (mm(o, wo[...]) + mm(u, up_o))
        h1_ref[at, :] = h1
        x = h1 * lax.rsqrt(jnp.mean(h1 * h1, axis=1, keepdims=True) + EPS) * gain_m[...]
        x = x.astype(BF)
        xb_ref[at, :] = x
        lin_ref[at, :] = mm(x, wr[...])
        return carry

    lax.fori_loop(0, length // 256, finish, 0)


def attention_forward(tok, gain_a, wqkv, down, up, wo, up_out, gain_m, wr, spans, adapter):
    length, width = tok.shape
    cos, sin = rope_tables(length)
    shapes = [
        ((length, width), BF),
        ((length, width), BF),
        ((length, width), BF),
        ((length, width), BF),
        ((length, width), BF),
        ((length, 128), BF),
        ((length, 128), BF),
        ((length, 128), F32),
        ((length, width), F32),
        ((length, width), BF),
        ((length, 128), F32),
        ((width, 2 * width), BF),
        ((2, width, 128), BF),
        ((128, 4 * width), BF),
    ]
    vmem, smem = pl.BlockSpec(memory_space=pltpu.VMEM), pl.BlockSpec(memory_space=pltpu.SMEM)
    return pl.pallas_call(
        attention_forward_kernel,
        out_shape=[jax.ShapeDtypeStruct(s, t) for s, t in shapes],
        in_specs=[smem, smem] + [vmem] * 11,
        out_specs=[vmem] * len(shapes),
        scratch_shapes=[pltpu.VMEM((length // HALF, HALF, HALF), F32)],
        compiler_params=pltpu.CompilerParams(vmem_limit_bytes=56 * MIB),
        name="attention_forward",
    )(spans, adapter, tok, gain_a, wqkv, down, up, wo, up_out, gain_m, wr, cos, sin)


def attention_backward_kernel(
    spans, dh1_ref, tok, gain_a, wqkv, wqk, wo, down_ref, up_s, cos, sin,
    xa_ref, q_ref, k_ref, v_ref, ob_ref, ua_ref, uo_ref, lse_ref,
    grad_tok, grad_maps,
    bias, dob, datt, duo, lse_t, center_t, dq, dk, dv, dlin, dua,
):
    length, width = tok.shape
    groups = width // GROUP
    for half in range(length // HALF):
        bias[half] = span_bias(spans[half] - half * HALF, True)
    of_head = one_hot(iota((128, width), 1) // HD == iota((128, width), 0))

    def outer(block, carry):
        at = pl.ds(pl.multiple_of(block * 256, 256), 256)
        d = dh1_ref[at, :].astype(BF)
        datt[at, :] = d
        u = mm_t(d, up_s[:, pl.ds(3 * width, width)]).astype(BF)
        duo[at, :] = u
        do = (mm_t(d, wo[...]) + mm_t(u, down_ref[1])).astype(BF)
        dob[at, :] = do
        both = do.astype(F32) * ob_ref[at, :].astype(F32)
        high = both.astype(BF)
        low = (both - high.astype(F32)).astype(BF)
        center_t[:, at] = mm_t(of_head, high) + mm_t(of_head, low)
        lse_t[:, at] = lse_ref[at, :].T
        return carry

    lax.fori_loop(0, length // 256, outer, 0)
    dq[...] = jnp.zeros(dq.shape, F32)
    dk[...] = jnp.zeros(dk.shape, F32)
    dv[...] = jnp.zeros(dv.shape, F32)
    lane = iota((1, GROUP), 1)

    def attend(head, carry):
        g, h = head // 4, head % 4
        lanes = pl.ds(pl.multiple_of(g * GROUP, GROUP), GROUP)
        qk_own = jnp.where((lane % 128) // 32 == h, 1.0, 0.0).astype(BF)
        v_own = jnp.where(lane // 64 == h, 1.0, 0.0).astype(BF)
        lse = lse_t[pl.ds(head, 1), :]
        center = center_t[pl.ds(head, 1), :]
        for half in range(length // HALF):
            at = pl.ds(half * HALF, HALF)
            late = pl.ds(half * HALF, length - half * HALF)
            kh = k_ref[at, lanes] * qk_own
            vh = v_ref[at, lanes] * v_own
            q = q_ref[late, lanes] * BF(0.125)
            do = dob[late, lanes]
            s = mm_t(kh, q) - lse[:, half * HALF :]
            if half * HALF + HALF < length:
                s = jnp.concatenate([s[:, :HALF] + bias[half], s[:, HALF:]], axis=1)
            else:
                s = s + bias[half]
            prob = jnp.exp(s)
            dp = mm_t(vh, do)
            ds = (prob * (dp - center[:, half * HALF :])).astype(BF)
            dv[at, lanes] += mm(prob.astype(BF), do * v_own)
            dk[at, lanes] += mm(ds, q * qk_own)
            dq[late, lanes] += t_mm(ds, kh)
        return carry

    lax.fori_loop(0, HEADS, attend, 0)

    def inner(block, carry):
        at = pl.ds(pl.multiple_of(block * 256, 256), 256)
        c, s = cos[at, :], -sin[at, :]
        for g in range(groups):
            lanes = pl.ds(g * GROUP, GROUP)
            dlin[at, lanes] = rope(dq[at, lanes] * 0.125, c, s).astype(BF)
            dlin[at, pl.ds(width + g * GROUP, GROUP)] = rope(dk[at, lanes], c, s).astype(BF)
        dlin[at, pl.ds(2 * width, width)] = dv[at, :].astype(BF)
        d = dlin[at, :]
        u = mm_t(d, up_s[:, pl.ds(0, 3 * width)]).astype(BF)
        dua[at, :] = u
        dx = mm_t(d[:, : 2 * width], wqk[...]) + mm_t(d[:, 2 * width :], wqkv[:, pl.ds(2 * width, width)])
        dx = (dx + mm_t(u, down_ref[0])) * gain_a[...]
        h0 = tok[at, :].astype(F32)
        r = lax.rsqrt(jnp.mean(h0 * h0, axis=1, keepdims=True) + EPS)
        pull = r * dx - h0 * (r * r * r * jnp.mean(dx * h0, axis=1, keepdims=True))
        grad_tok[at, :] = (dh1_ref[at, :] + pull).astype(BF)
        return carry

    lax.fori_loop(0, length // 256, inner, 0)
    order = head_order(True)
    grads = t_mm(dua[...], xa_ref[...]).astype(BF)
    for p in range(3):
        grad_maps[p] = grads[p * RANK : (p + 1) * RANK]
    grad_maps[3] = t_mm(duo[...], ob_ref[...]).astype(BF)[:RANK]
    for p in range(3):
        grads = t_mm(ua_ref[...], dlin[:, pl.ds(p * width, width)]).astype(BF)[p * RANK : (p + 1) * RANK]
        if p < 2:
            grads = jnp.concatenate(
                [mm(grads[:, g * GROUP : (g + 1) * GROUP], order) for g in range(groups)], axis=1
            ).astype(BF)
        grad_maps[4 + p] = grads
    grad_maps[7] = t_mm(uo_ref[...], datt[...]).astype(BF)[:RANK]


def attention_backward(spans, dh1, tok, gain_a, wqkv, wqk, wo, down_s, up_s, xa, q, k, v, ob, ua, uo, lse):
    length, width = tok.shape
    cos, sin = rope_tables(length)
    vmem, smem = pl.BlockSpec(memory_space=pltpu.VMEM), pl.BlockSpec(memory_space=pltpu.SMEM)
    return pl.pallas_call(
        attention_backward_kernel,
        out_shape=[
            jax.ShapeDtypeStruct((length, width), BF),
            jax.ShapeDtypeStruct((8, RANK, width), BF),
        ],
        in_specs=[smem] + [vmem] * 18,
        out_specs=[vmem] * 2,
        scratch_shapes=[
            pltpu.VMEM((length // HALF, HALF, HALF), F32),
            pltpu.VMEM((length, width), BF),
            pltpu.VMEM((length, width), BF),
            pltpu.VMEM((length, 128), BF),
            pltpu.VMEM((128, length), F32),
            pltpu.VMEM((128, length), F32),
            pltpu.VMEM((length, width), F32),
            pltpu.VMEM((length, width), F32),
            pltpu.VMEM((length, width), F32),
            pltpu.VMEM((length, 3 * width), BF),
            pltpu.VMEM((length, 128), BF),
        ],
        compiler_params=pltpu.CompilerParams(vmem_limit_bytes=60 * MIB),
        name="attention_backward",
    )(spans, dh1, tok, gain_a, wqkv, wqk, wo, down_s, up_s, cos, sin, xa, q, k, v, ob, ua, uo, lse)


def split(x):
    high = x.astype(BF)
    return high, (x - high.astype(F32)).astype(BF)


def experts_kernel(
    adapter_ref, xb, h1_ref, lin_ref, cot, routes, carried, gain_m, wr, vectors,
    w_gate, w_up, w_down, gu_down, gu_up, dn_down, dn_up,
    result, dh1_ref, grads,
    count, gates, gates_t, place, place_t, both, x_s, c_s, dy_s, g_s, y_acc, dx_acc, ug_s, ud_acc, dud_s, dug_acc,
    a_gu, b_dn, acc,
):
    e, j = pl.program_id(0), pl.program_id(1)
    experts, tiles = pl.num_programs(0), pl.num_programs(1)
    length, width = xb.shape
    kinds = carried.shape[1]
    numbers = kinds - 4
    tile = w_gate.shape[2]
    hidden = grads.shape[2] - 3 * width
    hidden //= 3
    adapter = adapter_ref[0]
    rows_of = 128

    @pl.when((e == 0) & (j == 0))
    def _():
        lane = iota((1, kinds), 1)
        logits = lin_ref[:, :kinds] + carried[...]
        picks = [lane == routes[:, k : k + 1] for k in range(2)]
        chosen = [jnp.sum(jnp.where(p, logits, 0.0), axis=1, keepdims=True) for p in picks]
        top = jnp.maximum(*chosen)
        parts = [jnp.exp(c - top) for c in chosen]
        total = parts[0] + parts[1]
        gates[...] = jnp.zeros(gates.shape, F32)
        gates[:, :kinds] = jnp.where(picks[0], parts[0] / total, jnp.where(picks[1], parts[1] / total, 0.0))
        wide = iota((1, 128), 1)
        named = [(wide == routes[:, k : k + 1]) & (wide < numbers) for k in range(2)]
        member = one_hot(named[0] | named[1])
        for block in range(length // 256):
            before = one_hot(iota((256, length), 1) < iota((256, length), 0) + block * 256)
            place[pl.ds(block * 256, 256), :] = mm(before, member)
        counts = jnp.sum(member.astype(F32), axis=0, keepdims=True)
        padded = jnp.floor((counts + (rows_of - 1)) * (1.0 / rows_of))
        earlier = one_hot(iota((128, 128), 0) < iota((128, 128), 1))
        starts = rows_of * mm(jnp.broadcast_to(padded, (8, 128)).astype(BF), earlier)[:1]
        own = jnp.where(named[0] | named[1], place[...], -1.0)
        place_t[...] = own.T
        gates_t[...] = gates[...].T
        spots = [
            jnp.sum(jnp.where(n, place[...] + starts + 1.0, 0.0), axis=1, keepdims=True) - 1.0 for n in named
        ]
        place[...] = jnp.where(wide == 0, spots[0], spots[1])
        for i in range(numbers):
            mine = wide == i
            count[0, i] = jnp.sum(jnp.where(mine, padded, 0.0)).astype(jnp.int32)
            count[1, i] = jnp.sum(jnp.where(mine, starts, 0.0)).astype(jnp.int32)
        count[1, numbers] = jnp.sum(jnp.where(wide < numbers, padded, 0.0)).astype(jnp.int32) * rows_of

    blocks = count[0, e]
    first = pl.multiple_of(count[1, e], rows_of)

    @pl.when((j == 0) & (blocks > 0))
    def _():
        a_gu[...] = (mm(gu_down[0, 0], picker(adapter, 0)) + mm(gu_down[0, 1], picker(adapter, 1))).astype(BF)
        b_dn[...] = mm(placer(adapter, 0), dn_up[0]).astype(BF)

    @pl.when((j == 0) & (blocks == 0))
    def _():
        grads[...] = jnp.zeros(grads.shape, BF)

    def work(n):
        rows = pl.ds(0, n)

        @pl.when(j == 0)
        def _():
            own = iota((n, length), 0).astype(F32) == place_t[pl.ds(e, 1), :]
            taken = one_hot(own)
            x = mm(taken, xb[...]).astype(BF)
            c = mm(taken, cot[...]).astype(BF)
            g = jnp.sum(jnp.where(own, gates_t[pl.ds(e, 1), :], 0.0), axis=1, keepdims=True)
            dy = (g * c.astype(F32)).astype(BF)
            x_s[rows, :] = x
            c_s[rows, :] = c
            dy_s[rows, :] = dy
            g_s[rows, :] = jnp.broadcast_to(g, (n, 128))
            ug_s[rows, :] = mm(x, a_gu[...]).astype(BF)
            dud_s[rows, :] = mm_t(dy, b_dn[...]).astype(BF)

        x, dy, ug, dud = x_s[rows, :], dy_s[rows, :], ug_s[rows, :], dud_s[rows, :]
        b_gate = mm(placer(adapter, 0), gu_up[0, 0]).astype(BF)
        b_up = mm(placer(adapter, 1), gu_up[0, 1]).astype(BF)
        a_dn = mm(dn_down[0], picker(adapter, 0)).astype(BF)
        gate = mm(x, w_gate[0]) + mm(ug, b_gate)
        up = mm(x, w_up[0]) + mm(ug, b_up)
        sig = 1.0 / (1.0 + jnp.exp(-gate))
        act = gate * sig
        hid = (act * up).astype(BF)
        dhid = mm_t(dy, w_down[0]) + mm_t(dud, a_dn)
        dup = (dhid * act).astype(BF)
        dgate = (dhid * up * (sig + act * (1.0 - sig))).astype(BF)
        y = mm(hid, w_down[0])
        ud = mm(hid, a_dn)
        dx = mm_t(dgate, w_gate[0]) + mm_t(dup, w_up[0])
        dug = mm_t(dgate, b_gate) + mm_t(dup, b_up)
        at = pl.multiple_of(j * tile, tile)
        ug_t = ug.T
        grads[0, :, pl.ds(2 * width + at, tile)] = mm(ug_t[:RANK], dgate).astype(BF)
        grads[0, :, pl.ds(2 * width + hidden + at, tile)] = mm(ug_t[RANK : 2 * RANK], dup).astype(BF)
        grads[0, :, pl.ds(2 * width + 2 * hidden + at, tile)] = mm(dud.T[:RANK], hid).astype(BF)

        @pl.when(j == 0)
        def _():
            y_acc[rows, :] = y
            dx_acc[rows, :] = dx
            ud_acc[rows, :] = ud
            dug_acc[rows, :] = dug

        @pl.when(j > 0)
        def _():
            y_acc[rows, :] += y
            dx_acc[rows, :] += dx
            ud_acc[rows, :] += ud
            dug_acc[rows, :] += dug

        @pl.when(j == tiles - 1)
        def _():
            ud = ud_acc[rows, :].astype(BF)
            dug = dug_acc[rows, :].astype(BF)
            y = y_acc[rows, :] + mm(ud, b_dn[...])
            g = g_s[rows, :][:, :1]
            dg = jnp.sum(c_s[rows, :].astype(F32) * y.astype(BF).astype(F32), axis=1, keepdims=True)
            high, low = split(dg)
            lane = iota((1, 128), 1)
            to = pl.ds(first, n)
            both[to, :width] = (g * y).astype(BF)
            both[to, width : 2 * width] = (dx_acc[rows, :] + mm_t(dug, a_gu[...])).astype(BF)
            both[to, 2 * width :] = jnp.where(
                lane == e, high.astype(F32), jnp.where(lane == e + 64, low.astype(F32), 0.0)
            ).astype(BF)
            x, dy = x_s[rows, :], dy_s[rows, :]
            to_a = mm(dug.T[: 2 * RANK], x).astype(BF)
            grads[0, :, :width] = to_a[:RANK]
            grads[0, :, width : 2 * width] = to_a[RANK:]
            grads[0, :, 2 * width + 3 * hidden :] = mm(ud.T[:RANK], dy).astype(BF)

    for number in range(1, 512 // rows_of + 1):
        pl.when(blocks == number)(functools.partial(work, number * rows_of))

    @pl.when((e == experts - 1) & (j == tiles - 1))
    def _():
        used = count[1, numbers]
        both[pl.ds(pl.multiple_of(used, rows_of), HALF), :] = jnp.zeros((HALF, both.shape[1]), BF)
        lane = iota((1, 128), 1)

        def combine(block, carry):
            at = pl.ds(pl.multiple_of(block * 256, 256), 256)
            acc[...] = jnp.zeros(acc.shape, F32)
            spots = place[at, :]

            def add(part, carry):
                k0 = pl.multiple_of(part * HALF, HALF)
                slot = (iota((256, HALF), 1) + k0).astype(F32)
                taken = one_hot((slot == spots[:, :1]) | (slot == spots[:, 1:2]))
                acc[...] += mm(taken, both[pl.ds(k0, HALF), :])
                return carry

            lax.fori_loop(0, (used + HALF - 1) // HALF, add, 0)
            h1 = h1_ref[at, :]
            ct = cot[at, :].astype(F32)
            r = lax.rsqrt(jnp.mean(h1 * h1, axis=1, keepdims=True) + EPS)
            gain = gain_m[...]
            n2 = h1 * r * gain
            lin = lin_ref[at, :]
            g = gates[at, :]
            gc = g[:, numbers + 1 : numbers + 2]
            g_fix = [g[:, numbers + 2 + i : numbers + 3 + i] for i in range(2)]
            mixes = []
            for i in range(2):
                a, b = lin[:, kinds + 2 * i : kinds + 2 * i + 1], lin[:, kinds + 2 * i + 1 : kinds + 2 * i + 2]
                top = jnp.maximum(a, b)
                a, b = jnp.exp(a - top), jnp.exp(b - top)
                mixes.append((a / (a + b), b / (a + b)))
            vecs = [vectors[i : i + 1, :] for i in range(2)]
            to_n2 = gc + g_fix[0] * mixes[0][0] + g_fix[1] * mixes[1][0]
            out = h1 + acc[:, :width] + to_n2 * n2
            out = out + (g_fix[0] * mixes[0][1]) * vecs[0] + (g_fix[1] * mixes[1][1]) * vecs[1]
            result[at, :] = out.astype(BF)
            a = jnp.sum(ct * n2, axis=1, keepdims=True)
            bs = [jnp.sum(ct * v, axis=1, keepdims=True) for v in vecs]
            packed = acc[:, 2 * width :]
            dg = jnp.where(lane < numbers, packed + pltpu.roll(packed, 64, 1), 0.0)
            dg = jnp.where(lane == numbers + 1, a, dg)
            for i in range(2):
                dg = jnp.where(lane == numbers + 2 + i, mixes[i][0] * a + mixes[i][1] * bs[i], dg)
            dlin = g * (dg - jnp.sum(g * dg, axis=1, keepdims=True))
            for i in range(2):
                pull = mixes[i][0] * mixes[i][1] * (g_fix[i] * (a - bs[i]))
                dlin = jnp.where(lane == kinds + 2 * i, pull, jnp.where(lane == kinds + 2 * i + 1, -pull, dlin))
            high, low = split(dlin)
            dn2 = acc[:, width : 2 * width] + (mm_t(high, wr[...]) + mm_t(low, wr[...])) + ct * to_n2
            dn2 = dn2 * gain
            back = r * dn2 - h1 * (r * r * r * jnp.mean(dn2 * h1, axis=1, keepdims=True))
            dh1_ref[at, :] = ct + back
            return carry

        lax.fori_loop(0, length // 256, combine, 0)


def experts_both_ways(adapter, xb, h1, lin, cot, routes, carried, gain_m, wr, vectors, w_gu, w_dn, gu_down, gu_up, dn_down, dn_up):
    length, width = xb.shape
    experts, hidden = w_dn.shape[0], w_dn.shape[1]
    tile = hidden // 2
    tiles = hidden // tile
    most = 2 * length + experts * 128
    total = 3 * width + 3 * hidden
    smem = pl.BlockSpec(memory_space=pltpu.SMEM)

    def whole(a):
        return pl.BlockSpec(a.shape, lambda e, j: (0,) * a.ndim, pipeline_mode=pl.Buffered(1))

    resident = (xb, h1, lin, cot, routes, carried, gain_m, wr, vectors)
    return pl.pallas_call(
        experts_kernel,
        grid=(experts, tiles),
        out_shape=[
            jax.ShapeDtypeStruct((length, width), BF),
            jax.ShapeDtypeStruct((length, width), F32),
            jax.ShapeDtypeStruct((experts, RANK, total), BF),
        ],
        in_specs=[smem]
        + [whole(a) for a in resident]
        + [
            pl.BlockSpec((1, width, tile), lambda e, j: (e, 0, j)),
            pl.BlockSpec((1, width, tile), lambda e, j: (e, 0, tiles + j)),
            pl.BlockSpec((1, tile, width), lambda e, j: (e, j, 0)),
            pl.BlockSpec((1, 2, width, 128), lambda e, j: (e, 0, 0, 0)),
            pl.BlockSpec((1, 2, 128, tile), lambda e, j: (e, 0, 0, j)),
            pl.BlockSpec((1, tile, 128), lambda e, j: (e, j, 0)),
            pl.BlockSpec((1, 128, width), lambda e, j: (e, 0, 0)),
        ],
        out_specs=[
            pl.BlockSpec((length, width), lambda e, j: (0, 0), pipeline_mode=pl.Buffered(1)),
            pl.BlockSpec((length, width), lambda e, j: (0, 0), pipeline_mode=pl.Buffered(1)),
            pl.BlockSpec((1, RANK, total), lambda e, j: (e, 0, 0)),
        ],
        scratch_shapes=[
            pltpu.SMEM((2, experts + 1), jnp.int32),
            pltpu.VMEM((length, 128), F32),
            pltpu.VMEM((128, length), F32),
            pltpu.VMEM((length, 128), F32),
            pltpu.VMEM((128, length), F32),
            pltpu.VMEM((most + HALF, 2 * width + 128), BF),
            pltpu.VMEM((512, width), BF),
            pltpu.VMEM((512, width), BF),
            pltpu.VMEM((512, width), BF),
            pltpu.VMEM((512, 128), F32),
            pltpu.VMEM((512, width), F32),
            pltpu.VMEM((512, width), F32),
            pltpu.VMEM((512, 128), BF),
            pltpu.VMEM((512, 128), F32),
            pltpu.VMEM((512, 128), BF),
            pltpu.VMEM((512, 128), F32),
            pltpu.VMEM((width, 128), BF),
            pltpu.VMEM((128, width), BF),
            pltpu.VMEM((256, 2 * width + 128), F32),
        ],
        compiler_params=pltpu.CompilerParams(vmem_limit_bytes=60 * MIB),
        name="experts_both_ways",
    )(adapter, *resident, w_gu, w_gu, w_dn, gu_down, gu_up, dn_down, dn_up)


def gather_experts(arrays):
    return [lax.all_gather(a, "expert", axis=0, tiled=True) for a in arrays]


def sum_expert_maps(compact, senders):
    groups = lax.axis_size("expert")
    mine = compact.reshape(groups, -1, *compact.shape[1:])[:, 0]
    got = lax.all_to_all(mine, "expert", split_axis=0, concat_axis=0, tiled=True)
    rows = got.reshape(groups * RANK, -1)
    to = (senders[:, None] * RANK + jnp.arange(RANK)[None, :]).reshape(-1)
    spread = (jnp.arange(128)[:, None] == to[None, :]).astype(BF)
    return lax.psum(mm(spread, rows).astype(BF), "dp").astype(F32)


def sum_attention_maps(compact, adapter):
    maps, _, width = compact.shape
    dense = lax.dynamic_update_slice(jnp.zeros((maps, 128, width), BF), compact, (0, adapter * RANK, 0))
    return lax.psum(dense, ("dp", "expert")).astype(F32)


def body(
    tokens, cotangent, attention_norm_gain, query_key_value_weight, attention_output_weight,
    adapter_attention_down_maps, adapter_query_key_value_up_maps, adapter_output_up_map,
    experts_norm_gain, router_weight, constant_expert_mixing, constant_expert_vectors,
    expert_gate_up_weight, expert_down_weight, adapter_expert_gate_up_down_maps, adapter_expert_gate_up_up_maps,
    adapter_expert_down_down_maps, adapter_expert_down_up_maps,
    routes, router_logits_carried, picture_span_starts, sequence_adapter_index,
):
    groups = lax.axis_size("expert")
    width = tokens.shape[1]
    hidden = expert_down_weight.shape[1]
    first = lax.axis_index("dp") * groups
    senders = lax.dynamic_slice_in_dim(sequence_adapter_index, first, groups, 0)
    adapter = lax.dynamic_slice_in_dim(senders, lax.axis_index("expert"), 1, 0)
    gain_a, gain_m = attention_norm_gain[None], experts_norm_gain[None]
    spans = picture_span_starts.reshape(-1)
    router = jnp.concatenate([router_weight, constant_expert_mixing], axis=1)
    router = jnp.pad(router, ((0, 0), (0, 128 - router.shape[1])))
    weights = gather_experts([
        expert_gate_up_weight, expert_down_weight, adapter_expert_gate_up_down_maps,
        adapter_expert_gate_up_up_maps, adapter_expert_down_down_maps, adapter_expert_down_up_maps,
    ])
    xa, q, k, v, ob, ua, uo, lse, h1, xb, lin, wqk, down_s, up_s = attention_forward(
        tokens, gain_a, query_key_value_weight, adapter_attention_down_maps, adapter_query_key_value_up_maps,
        attention_output_weight, adapter_output_up_map, gain_m, router, spans, adapter,
    )
    result, dh1, expert_maps = experts_both_ways(
        adapter, xb, h1, lin, cotangent, routes, router_logits_carried, gain_m, router, constant_expert_vectors, *weights
    )
    grad_tokens, attention_maps = attention_backward(
        spans, dh1, tokens, gain_a, query_key_value_weight, wqk, attention_output_weight, down_s, up_s,
        xa, q, k, v, ob, ua, uo, lse,
    )
    of_expert = sum_expert_maps(expert_maps, senders)
    of_attention = sum_attention_maps(attention_maps, adapter[0])
    cuts = [width, 2 * width, 2 * width + hidden, 2 * width + 2 * hidden, 2 * width + 3 * hidden]
    gud0, gud1, guu0, guu1, dnd, dnu = jnp.split(of_expert, cuts, axis=1)
    return (
        result,
        grad_tokens,
        of_attention[:4].transpose(0, 2, 1),
        of_attention[4:7],
        of_attention[7],
        jnp.stack([gud0.T, gud1.T])[None],
        jnp.stack([guu0, guu1])[None],
        dnd.T[None],
        dnu[None],
    )


def solution(mesh):
    tokens, own = P(("dp", "expert"), None), P("expert", None, None)
    own4 = P("expert", None, None, None)
    in_specs = (tokens, tokens) + (P(),) * 10 + (own, own, own4, own4, own, own) + (tokens,) * 3 + (P(),)
    out_specs = (tokens, tokens, P(), P(), P(), own4, own4, own, own)
    return jax.shard_map(body, mesh=mesh, in_specs=in_specs, out_specs=out_specs, check_vma=False)
```

```python
import functools

import jax
import jax.numpy as jnp
import numpy as np
from jax import lax
from jax.experimental import pallas as pl
from jax.experimental.pallas import tpu as pltpu
from jax.sharding import PartitionSpec as P

HEADS = 12
HD = 64
RANK = 16
PIC = 256
GROUP = 256
HALF = 512
EPS = 1e-06
NEG = -1e30
BF = jnp.bfloat16
F32 = jnp.float32
MIB = 1024 * 1024


def mm(a, b):
    return jnp.dot(a, b, preferred_element_type=F32)


def mm_t(a, b):
    return lax.dot_general(a, b, (((1,), (1,)), ((), ())), preferred_element_type=F32)


def t_mm(a, b):
    return lax.dot_general(a, b, (((0,), (0,)), ((), ())), preferred_element_type=F32)


def iota(shape, dim):
    return lax.broadcasted_iota(jnp.int32, shape, dim)


def one_hot(condition):
    return jnp.where(condition, 1.0, 0.0).astype(BF)


def picker(adapter, place, rows=128, columns=128):
    row, column = iota((rows, columns), 0), iota((rows, columns), 1)
    return one_hot((row - adapter * RANK == column - place * RANK) & (column // RANK == place))


def placer(adapter, place, rows=128, columns=128):
    row, column = iota((rows, columns), 0), iota((rows, columns), 1)
    return one_hot((column - adapter * RANK == row - place * RANK) & (row // RANK == place))


def head_order(back):
    row, column = iota((GROUP, GROUP), 0), iota((GROUP, GROUP), 1)
    a, b = (column, row) if back else (row, column)
    return one_hot(a == (b % 128 // 32) * 64 + b // 128 * 32 + b % 32)


def rope_tables(length):
    spacing = 10000.0 ** (-np.arange(0, HD, 2, dtype=np.float32) / np.float32(HD))
    angles = np.arange(length, dtype=np.float32)[:, None] * spacing.astype(np.float32)[None, :]
    angles = np.tile(angles, (1, 4))
    return np.cos(angles).astype(np.float32), np.sin(angles).astype(np.float32)


def rope(pair, cosine, sine):
    low, high = pair[:, :128], pair[:, 128:]
    return jnp.concatenate([low * cosine - high * sine, high * cosine + low * sine], axis=1)


def span_bias(start, transposed):
    a, b = iota((HALF, HALF), 0), iota((HALF, HALF), 1)
    query, key = (b, a) if transposed else (a, b)
    inside = (query >= start) & (query < start + PIC) & (key >= start) & (key < start + PIC)
    return jnp.where((key <= query) | inside, 0.0, NEG)


UNITS = 32
CHUNKS = ((0, 1), (1, 2), (3, 1), (4, 2))
EXTRA = ((0, 2), (2, 2))
MESH = pl.DeviceIdType.MESH


def other(index, step):
    return index + step - 2 * step * ((index // step) % 2)


def sending_steps(own, outs, scratch):
    senders, w_gu, w_dn, gu_down, gu_up, dn_down, dn_up = own
    all_gu, all_dn, all_maps = outs
    bounce_gu, bounce_dn, compact, send, recv, local = scratch
    sources, targets, bounce = (w_gu, w_dn), (all_gu, all_dn), (bounce_gu, bounce_dn)
    dp, ex = lax.axis_index("dp"), lax.axis_index("expert")
    sibling, far = other(ex, 1), other(ex, 2)
    peers = {
        "x": (other(dp, 1), ex), "z": (other(dp, 2), ex), "y": (dp, far), "s": (dp, sibling), "d": (dp, other(far, 1)),
    }
    x, z = dp % 2, (dp // 2) % 2
    quarter = {"y": z * 2 + x, "x": z * 2 + 1 - x, "z": (1 - z) * 2 + x, "d": (1 - z) * 2 + 1 - x}
    kind = (x + z) % 2
    slots = {}
    for name in ("y", "x", "z", "d"):
        for chunk in CHUNKS:
            slots[name, chunk] = len(slots)
    for name in ("e", "o"):
        for chunk in EXTRA:
            slots[name, chunk] = len(slots)
    count = len(slots)
    started = []

    def views(refs, expert, key):
        name, (first, number) = key
        if name in quarter:
            first = quarter[name] * 6 + first
        else:
            first = 24 + 4 * (kind if name == "e" else 1 - kind) + first
        columns, rows = refs[0].shape[-1] // UNITS, refs[1].shape[-2] // UNITS
        return (
            refs[0].at[expert, :, pl.ds(pl.multiple_of(first * columns, columns), number * columns)],
            refs[1].at[expert, pl.ds(pl.multiple_of(first * rows, rows), number * rows), :],
        )

    def copies(source, target, peer, slot):
        for i in range(len(source())):
            number = len(started)

            def made(i=i, number=number):
                return pltpu.make_async_remote_copy(
                    src_ref=source()[i], dst_ref=target()[i], send_sem=send.at[number], recv_sem=recv.at[slot, i],
                    device_id=peers[peer], device_id_type=MESH,
                )

            made().start()
            started.append(made)

    def arrived(view, slot, i):
        pltpu.make_async_remote_copy(
            src_ref=view, dst_ref=view, send_sem=send.at[0], recv_sem=recv.at[slot, i],
            device_id=peers["s"], device_id_type=MESH,
        ).wait_recv()

    def begin():
        barrier = pltpu.get_barrier_semaphore()
        for peer in peers.values():
            pl.semaphore_signal(barrier, inc=1, device_id=peer, device_id_type=MESH)
        pl.semaphore_wait(barrier, len(peers))
        for name, chunks in (("y", CHUNKS), ("e", EXTRA)):
            for chunk in chunks:
                key = name, chunk
                copies(
                    functools.partial(views, sources, 0, key), functools.partial(views, targets, ex, key), "y", slots[key]
                )
        copies(lambda: [s.at[0] for s in sources], lambda: [t.at[ex] for t in targets], "s", 2 * count)
        for i in range(2):
            pltpu.make_async_copy(sources[i].at[0], bounce[i], local.at[i]).start()

    def select():
        row, column = iota((64, 128), 0), iota((64, 128), 1)
        first = sum(jnp.where(row // RANK == i, senders[i], 0) for i in range(4))
        rows = one_hot(column == first * RANK + row % RANK)
        width, hidden = gu_down.shape[2], dn_down.shape[1]
        parts = [
            (0, mm_t(rows, gu_down[0, 0])),
            (width, mm_t(rows, gu_down[0, 1])),
            (2 * width, mm(rows, gu_up[0, 0])),
            (2 * width + hidden, mm(rows, gu_up[0, 1])),
            (2 * width + 2 * hidden, mm_t(rows, dn_down[0])),
            (2 * width + 3 * hidden, mm(rows, dn_up[0])),
        ]
        for at, part in parts:
            for i in range(4):
                compact[i, :, pl.ds(at, part.shape[1])] = part[i * RANK : (i + 1) * RANK].astype(BF)
        for i, (peer, to) in enumerate((("s", sibling), ("y", far), ("d", other(far, 1)))):
            copies(lambda to=to: [compact.at[to]], lambda: [all_maps.at[ex]], peer, 2 * count + 1 + i)
        pltpu.make_async_copy(compact.at[ex], all_maps.at[ex], local.at[2]).start()

    def turn():
        for i in range(2):
            pltpu.make_async_copy(sources[i].at[0], bounce[i], local.at[i]).wait()
            pltpu.make_async_copy(bounce[i], targets[i].at[ex], local.at[i]).start()

    along_x = (CHUNKS[0], CHUNKS[3])

    def got(name, chunk):
        key = name, chunk
        to = []
        if name == "y":
            to = [("x", slots["x", chunk]), ("z", slots["z", chunk])]
        if name == "x" and chunk not in along_x:
            to = [("z", slots["d", chunk])]
        if name == "z" and chunk in along_x:
            to = [("x", slots["d", chunk])]
        if name == "e":
            to = [("x" if chunk == EXTRA[0] else "z", slots["o", chunk])]

        def step():
            mine = functools.partial(views, targets, far, key)
            for i in range(2):
                arrived(mine()[i], slots[key], i)
            for peer, slot in to:
                copies(mine, mine, peer, slot)
            copies(mine, mine, "s", count + slots[key])

        return step

    def end():
        for made in started:
            made().wait_send()
        for i in range(2):
            pltpu.make_async_copy(bounce[i], targets[i].at[ex], local.at[i]).wait()
            arrived(targets[i].at[sibling], 2 * count, i)
        pltpu.make_async_copy(compact.at[ex], all_maps.at[ex], local.at[2]).wait()
        for i, source in enumerate((sibling, far, other(far, 1))):
            arrived(all_maps.at[source], 2 * count + 1 + i, 0)
        for key, slot in slots.items():
            view = views(targets, other(far, 1), key)
            for i in range(2):
                arrived(view[i], count + slot, i)

    c, e = CHUNKS, EXTRA
    return {
        "begin": [begin, select],
        "ready": [turn],
        "projected": [got("y", c[0])],
        2: [got("x", c[0]), got("z", c[0])],
        4: [got("y", c[1])],
        6: [got("y", c[2]), got("d", c[0])],
        9: [got("x", c[1]), got("z", c[1])],
        "end": [
            got("y", c[3]), got("x", c[2]), got("z", c[2]), got("e", e[0]), got("x", c[3]), got("z", c[3]), got("e", e[1]),
            got("d", c[1]), got("d", c[2]), got("o", e[0]), got("d", c[3]), got("o", e[1]), end,
        ],
    }


def attention_forward_kernel(exchange, *refs):
    spans, adapter_ref, tok, gain_a, wqkv, down, up, wo, up_out, gain_m, wr, cos, sin = refs[:13]
    refs = refs[13:]
    own = ()
    if exchange:
        own, refs = refs[:7], refs[7:]
    xa_ref, q_ref, k_ref, v_ref, ob_ref, ua_ref, uo_ref, lse_ref, h1_ref, xb_ref, lin_ref, wqk_ref, down_ref, up_s = refs[:14]
    refs = refs[14:]
    steps = {}
    if exchange:
        steps = sending_steps(own, refs[:3], refs[4:])
        bias = refs[3]
    else:
        (bias,) = refs
    length, width = tok.shape
    groups = width // GROUP
    adapter = adapter_ref[0]

    def run(point):
        for step in steps.get(point, ()):
            step()

    run("begin")
    order = head_order(False)
    down_s = sum(mm(down[p], picker(adapter, p)) for p in range(3)).astype(BF)
    down_o = mm(down[3], picker(adapter, 0)).astype(BF)
    up_o = mm(placer(adapter, 0), up_out[...]).astype(BF)
    down_ref[0] = down_s
    down_ref[1] = down_o
    up_s[:, pl.ds(3 * width, width)] = up_o
    for p in range(3):
        rows = mm(placer(adapter, p), up[p]).astype(BF)
        for g in range(groups):
            block = rows[:, g * GROUP : (g + 1) * GROUP]
            if p < 2:
                block = mm(block, order).astype(BF)
            up_s[:, pl.ds(p * width + g * GROUP, GROUP)] = block
    for g in range(2 * groups):
        at = pl.ds(g * GROUP, GROUP)
        wqk_ref[:, at] = mm(wqkv[:, at], order).astype(BF)
    for half in range(length // HALF):
        bias[half] = span_bias(spans[half] - half * HALF, False)
    run("ready")

    def project(block, carry):
        at = pl.ds(pl.multiple_of(block * 256, 256), 256)
        h0 = tok[at, :].astype(F32)
        x = h0 * lax.rsqrt(jnp.mean(h0 * h0, axis=1, keepdims=True) + EPS) * gain_a[...]
        x = x.astype(BF)
        xa_ref[at, :] = x
        u = mm(x, down_s).astype(BF)
        ua_ref[at, :] = u
        c, s = cos[at, :], sin[at, :]
        for p, out in enumerate((q_ref, k_ref)):
            for g in range(groups):
                lanes = pl.ds(p * width + g * GROUP, GROUP)
                lin = mm(x, wqk_ref[:, lanes]) + mm(u, up_s[:, lanes])
                out[at, pl.ds(g * GROUP, GROUP)] = rope(lin, c, s).astype(BF)
        lanes = pl.ds(2 * width, width)
        v_ref[at, :] = (mm(x, wqkv[:, lanes]) + mm(u, up_s[:, lanes])).astype(BF)
        return carry

    lax.fori_loop(0, length // 256, project, 0)
    run("projected")

    lane = iota((1, GROUP), 1)
    lse_ref[...] = jnp.zeros(lse_ref.shape, F32)
    ob_f = ob_ref

    def attend(head, carry):
        g, h = head // 4, head % 4
        lanes = pl.ds(pl.multiple_of(g * GROUP, GROUP), GROUP)
        qk_own = jnp.where((lane % 128) // 32 == h, 1.0, 0.0).astype(BF)
        v_own = jnp.where(lane // 64 == h, 1.0, 0.0)
        kh = k_ref[:, lanes] * qk_own
        vh = v_ref[:, lanes] * v_own.astype(BF)
        for half in range(length // HALF):
            at = pl.ds(half * HALF, HALF)
            q = q_ref[at, lanes] * BF(0.125)
            keys = (half + 1) * HALF
            diag = mm_t(q, kh[half * HALF : keys]) + bias[half]
            top = jnp.max(diag, axis=1, keepdims=True)
            if half:
                past = mm_t(q, kh[: half * HALF])
                top = jnp.maximum(top, jnp.max(past, axis=1, keepdims=True))
            e = jnp.exp(diag - top)
            total = jnp.sum(e, axis=1, keepdims=True)
            o = mm(e.astype(BF), vh[half * HALF : keys])
            if half:
                e = jnp.exp(past - top)
                total = total + jnp.sum(e, axis=1, keepdims=True)
                o = o + mm(e.astype(BF), vh[: half * HALF])
            o = o * pl.reciprocal(total, approx=False)
            lse = top + jnp.log(total)
            lse_ref[at, :] = jnp.where(iota((1, 128), 1) == head, lse, lse_ref[at, :])
            old = jnp.where(v_own > 0.5, 0.0, ob_f[at, lanes].astype(F32))
            ob_f[at, lanes] = jnp.where(v_own > 0.5, o, old).astype(BF)
        for point in steps:
            if isinstance(point, int):
                pl.when(head == point)(functools.partial(run, point))
        return carry

    lax.fori_loop(0, HEADS, attend, 0)

    def finish(block, carry):
        at = pl.ds(pl.multiple_of(block * 256, 256), 256)
        o = ob_ref[at, :]
        u = mm(o, down_o).astype(BF)
        uo_ref[at, :] = u
        h1 = tok[at, :].astype(F32) + (mm(o, wo[...]) + mm(u, up_o))
        h1_ref[at, :] = h1
        x = h1 * lax.rsqrt(jnp.mean(h1 * h1, axis=1, keepdims=True) + EPS) * gain_m[...]
        x = x.astype(BF)
        xb_ref[at, :] = x
        lin_ref[at, :] = mm(x, wr[...])
        return carry

    lax.fori_loop(0, length // 256, finish, 0)
    run("end")


def attention_forward(tok, gain_a, wqkv, down, up, wo, up_out, gain_m, wr, spans, adapter, own=(), senders=None):
    length, width = tok.shape
    cos, sin = rope_tables(length)
    shapes = [
        ((length, width), BF),
        ((length, width), BF),
        ((length, width), BF),
        ((length, width), BF),
        ((length, width), BF),
        ((length, 128), BF),
        ((length, 128), BF),
        ((length, 128), F32),
        ((length, width), F32),
        ((length, width), BF),
        ((length, 128), F32),
        ((width, 2 * width), BF),
        ((2, width, 128), BF),
        ((128, 4 * width), BF),
    ]
    vmem, smem = pl.BlockSpec(memory_space=pltpu.VMEM), pl.BlockSpec(memory_space=pltpu.SMEM)
    anys = pl.BlockSpec(memory_space=pl.ANY)
    in_specs, out_specs = [smem, smem] + [vmem] * 11, [vmem] * len(shapes)
    scratch = [pltpu.VMEM((length // HALF, HALF, HALF), F32)]
    params = dict(vmem_limit_bytes=60 * MIB)
    args = (spans, adapter, tok, gain_a, wqkv, down, up, wo, up_out, gain_m, wr, cos, sin)
    if own:
        w_gu, w_dn = own[:2]
        columns = 3 * width + 3 * w_dn.shape[1]
        in_specs += [smem, anys, anys] + [vmem] * 4
        args += (senders, *own)
        shapes += [((4, *w_gu.shape[1:]), BF), ((4, *w_dn.shape[1:]), BF), ((4, RANK, columns), BF)]
        out_specs += [anys] * 3
        scratch += [
            pltpu.VMEM(w_gu.shape[1:], BF),
            pltpu.VMEM(w_dn.shape[1:], BF),
            pltpu.VMEM((4, RANK, columns), BF),
            pltpu.SemaphoreType.DMA((96,)),
            pltpu.SemaphoreType.DMA((48, 2)),
            pltpu.SemaphoreType.DMA((3,)),
        ]
        params.update(collective_id=0, has_side_effects=True)
    return pl.pallas_call(
        functools.partial(attention_forward_kernel, bool(own)),
        out_shape=[jax.ShapeDtypeStruct(s, t) for s, t in shapes],
        in_specs=in_specs,
        out_specs=out_specs,
        scratch_shapes=scratch,
        compiler_params=pltpu.CompilerParams(**params),
        name="attention_forward",
    )(*args)


def attention_backward_kernel(
    spans, dh1_ref, tok, gain_a, wqkv, wqk, wo, down_ref, up_s, cos, sin,
    xa_ref, q_ref, k_ref, v_ref, ob_ref, ua_ref, uo_ref, lse_ref,
    grad_tok, grad_maps,
    bias, dob, datt, duo, lse_t, center_t, dq, dk, dv, dlin, dua,
):
    length, width = tok.shape
    groups = width // GROUP
    for half in range(length // HALF):
        bias[half] = span_bias(spans[half] - half * HALF, True)
    of_head = one_hot(iota((128, width), 1) // HD == iota((128, width), 0))

    def outer(block, carry):
        at = pl.ds(pl.multiple_of(block * 256, 256), 256)
        d = dh1_ref[at, :].astype(BF)
        datt[at, :] = d
        u = mm_t(d, up_s[:, pl.ds(3 * width, width)]).astype(BF)
        duo[at, :] = u
        do = (mm_t(d, wo[...]) + mm_t(u, down_ref[1])).astype(BF)
        dob[at, :] = do
        both = do.astype(F32) * ob_ref[at, :].astype(F32)
        high = both.astype(BF)
        low = (both - high.astype(F32)).astype(BF)
        center_t[:, at] = mm_t(of_head, high) + mm_t(of_head, low)
        lse_t[:, at] = lse_ref[at, :].T
        return carry

    lax.fori_loop(0, length // 256, outer, 0)
    dq[...] = jnp.zeros(dq.shape, F32)
    dk[...] = jnp.zeros(dk.shape, F32)
    dv[...] = jnp.zeros(dv.shape, F32)
    lane = iota((1, GROUP), 1)

    def attend(head, carry):
        g, h = head // 4, head % 4
        lanes = pl.ds(pl.multiple_of(g * GROUP, GROUP), GROUP)
        qk_own = jnp.where((lane % 128) // 32 == h, 1.0, 0.0).astype(BF)
        v_own = jnp.where(lane // 64 == h, 1.0, 0.0).astype(BF)
        lse = lse_t[pl.ds(head, 1), :]
        center = center_t[pl.ds(head, 1), :]
        for half in range(length // HALF):
            at = pl.ds(half * HALF, HALF)
            late = pl.ds(half * HALF, length - half * HALF)
            kh = k_ref[at, lanes] * qk_own
            vh = v_ref[at, lanes] * v_own
            q = q_ref[late, lanes] * BF(0.125)
            do = dob[late, lanes]
            s = mm_t(kh, q) - lse[:, half * HALF :]
            if half * HALF + HALF < length:
                s = jnp.concatenate([s[:, :HALF] + bias[half], s[:, HALF:]], axis=1)
            else:
                s = s + bias[half]
            prob = jnp.exp(s)
            dp = mm_t(vh, do)
            ds = (prob * (dp - center[:, half * HALF :])).astype(BF)
            dv[at, lanes] += mm(prob.astype(BF), do * v_own)
            dk[at, lanes] += mm(ds, q * qk_own)
            dq[late, lanes] += t_mm(ds, kh)
        return carry

    lax.fori_loop(0, HEADS, attend, 0)

    def inner(block, carry):
        at = pl.ds(pl.multiple_of(block * 256, 256), 256)
        c, s = cos[at, :], -sin[at, :]
        for g in range(groups):
            lanes = pl.ds(g * GROUP, GROUP)
            dlin[at, lanes] = rope(dq[at, lanes] * 0.125, c, s).astype(BF)
            dlin[at, pl.ds(width + g * GROUP, GROUP)] = rope(dk[at, lanes], c, s).astype(BF)
        dlin[at, pl.ds(2 * width, width)] = dv[at, :].astype(BF)
        d = dlin[at, :]
        u = mm_t(d, up_s[:, pl.ds(0, 3 * width)]).astype(BF)
        dua[at, :] = u
        dx = mm_t(d[:, : 2 * width], wqk[...]) + mm_t(d[:, 2 * width :], wqkv[:, pl.ds(2 * width, width)])
        dx = (dx + mm_t(u, down_ref[0])) * gain_a[...]
        h0 = tok[at, :].astype(F32)
        r = lax.rsqrt(jnp.mean(h0 * h0, axis=1, keepdims=True) + EPS)
        pull = r * dx - h0 * (r * r * r * jnp.mean(dx * h0, axis=1, keepdims=True))
        grad_tok[at, :] = (dh1_ref[at, :] + pull).astype(BF)
        return carry

    lax.fori_loop(0, length // 256, inner, 0)
    order = head_order(True)
    grads = t_mm(dua[...], xa_ref[...]).astype(BF)
    for p in range(3):
        grad_maps[p] = grads[p * RANK : (p + 1) * RANK]
    grad_maps[3] = t_mm(duo[...], ob_ref[...]).astype(BF)[:RANK]
    for p in range(3):
        grads = t_mm(ua_ref[...], dlin[:, pl.ds(p * width, width)]).astype(BF)[p * RANK : (p + 1) * RANK]
        if p < 2:
            grads = jnp.concatenate(
                [mm(grads[:, g * GROUP : (g + 1) * GROUP], order) for g in range(groups)], axis=1
            ).astype(BF)
        grad_maps[4 + p] = grads
    grad_maps[7] = t_mm(uo_ref[...], datt[...]).astype(BF)[:RANK]


def attention_backward(spans, dh1, tok, gain_a, wqkv, wqk, wo, down_s, up_s, xa, q, k, v, ob, ua, uo, lse):
    length, width = tok.shape
    cos, sin = rope_tables(length)
    vmem, smem = pl.BlockSpec(memory_space=pltpu.VMEM), pl.BlockSpec(memory_space=pltpu.SMEM)
    return pl.pallas_call(
        attention_backward_kernel,
        out_shape=[
            jax.ShapeDtypeStruct((length, width), BF),
            jax.ShapeDtypeStruct((8, RANK, width), BF),
        ],
        in_specs=[smem] + [vmem] * 18,
        out_specs=[vmem] * 2,
        scratch_shapes=[
            pltpu.VMEM((length // HALF, HALF, HALF), F32),
            pltpu.VMEM((length, width), BF),
            pltpu.VMEM((length, width), BF),
            pltpu.VMEM((length, 128), BF),
            pltpu.VMEM((128, length), F32),
            pltpu.VMEM((128, length), F32),
            pltpu.VMEM((length, width), F32),
            pltpu.VMEM((length, width), F32),
            pltpu.VMEM((length, width), F32),
            pltpu.VMEM((length, 3 * width), BF),
            pltpu.VMEM((length, 128), BF),
        ],
        compiler_params=pltpu.CompilerParams(vmem_limit_bytes=60 * MIB),
        name="attention_backward",
    )(spans, dh1, tok, gain_a, wqkv, wqk, wo, down_s, up_s, cos, sin, xa, q, k, v, ob, ua, uo, lse)


def split(x):
    high = x.astype(BF)
    return high, (x - high.astype(F32)).astype(BF)


def experts_kernel(
    xb, h1_ref, lin_ref, cot, routes, carried, gain_m, wr, vectors,
    w_gate, w_up, w_down, maps,
    result, dh1_ref, grads,
    count, gates, gates_t, place, place_t, both, x_s, c_s, dy_s, g_s, y_acc, dx_acc, ug_s, ud_acc, dud_s, dug_acc,
    a_gu, b_dn, acc,
):
    e, j = pl.program_id(0), pl.program_id(1)
    experts, tiles = pl.num_programs(0), pl.num_programs(1)
    length, width = xb.shape
    kinds = carried.shape[1]
    numbers = kinds - 4
    tile = w_gate.shape[2]
    hidden = (grads.shape[2] - 3 * width) // 3
    rows_of = 128

    def padded_rows(start, number, before=0):
        part = maps[0, :, pl.ds(start, number)]
        parts = [jnp.zeros((before, number), BF), part, jnp.zeros((128 - RANK - before, number), BF)]
        return jnp.concatenate(parts if before else parts[1:], axis=0)

    @pl.when((e == 0) & (j == 0))
    def _():
        lane = iota((1, kinds), 1)
        logits = lin_ref[:, :kinds] + carried[...]
        picks = [lane == routes[:, k : k + 1] for k in range(2)]
        chosen = [jnp.sum(jnp.where(p, logits, 0.0), axis=1, keepdims=True) for p in picks]
        top = jnp.maximum(*chosen)
        parts = [jnp.exp(c - top) for c in chosen]
        total = parts[0] + parts[1]
        gates[...] = jnp.zeros(gates.shape, F32)
        gates[:, :kinds] = jnp.where(picks[0], parts[0] / total, jnp.where(picks[1], parts[1] / total, 0.0))
        wide = iota((1, 128), 1)
        named = [(wide == routes[:, k : k + 1]) & (wide < numbers) for k in range(2)]
        member = one_hot(named[0] | named[1])
        for block in range(length // 256):
            before = one_hot(iota((256, length), 1) < iota((256, length), 0) + block * 256)
            place[pl.ds(block * 256, 256), :] = mm(before, member)
        counts = jnp.sum(member.astype(F32), axis=0, keepdims=True)
        padded = jnp.floor((counts + (rows_of - 1)) * (1.0 / rows_of))
        earlier = one_hot(iota((128, 128), 0) < iota((128, 128), 1))
        starts = rows_of * mm(jnp.broadcast_to(padded, (8, 128)).astype(BF), earlier)[:1]
        own = jnp.where(named[0] | named[1], place[...], -1.0)
        place_t[...] = own.T
        gates_t[...] = gates[...].T
        spots = [
            jnp.sum(jnp.where(n, place[...] + starts + 1.0, 0.0), axis=1, keepdims=True) - 1.0 for n in named
        ]
        place[...] = jnp.where(wide == 0, spots[0], spots[1])
        for i in range(numbers):
            mine = wide == i
            count[0, i] = jnp.sum(jnp.where(mine, padded, 0.0)).astype(jnp.int32)
            count[1, i] = jnp.sum(jnp.where(mine, starts, 0.0)).astype(jnp.int32)
        count[1, numbers] = jnp.sum(jnp.where(wide < numbers, padded, 0.0)).astype(jnp.int32) * rows_of

    blocks = count[0, e]
    first = pl.multiple_of(count[1, e], rows_of)

    @pl.when((j == 0) & (blocks > 0))
    def _():
        a_gu[...] = padded_rows(0, width) + padded_rows(width, width, RANK)
        b_dn[...] = padded_rows(2 * width + 3 * hidden, width)

    @pl.when((j == 0) & (blocks == 0))
    def _():
        grads[...] = jnp.zeros(grads.shape, BF)

    def work(n):
        rows = pl.ds(0, n)

        @pl.when(j == 0)
        def _():
            own = iota((n, length), 0).astype(F32) == place_t[pl.ds(e, 1), :]
            taken = one_hot(own)
            x = mm(taken, xb[...]).astype(BF)
            c = mm(taken, cot[...]).astype(BF)
            g = jnp.sum(jnp.where(own, gates_t[pl.ds(e, 1), :], 0.0), axis=1, keepdims=True)
            dy = (g * c.astype(F32)).astype(BF)
            x_s[rows, :] = x
            c_s[rows, :] = c
            dy_s[rows, :] = dy
            g_s[rows, :] = jnp.broadcast_to(g, (n, 128))
            ug_s[rows, :] = mm_t(x, a_gu[...]).astype(BF)
            dud_s[rows, :] = mm_t(dy, b_dn[...]).astype(BF)

        x, dy, ug, dud = x_s[rows, :], dy_s[rows, :], ug_s[rows, :], dud_s[rows, :]
        at = pl.multiple_of(j * tile, tile)
        b_gate = padded_rows(2 * width + at, tile)
        b_up = padded_rows(2 * width + hidden + at, tile, RANK)
        a_dn = padded_rows(2 * width + 2 * hidden + at, tile)
        gate = mm(x, w_gate[0]) + mm(ug, b_gate)
        up = mm(x, w_up[0]) + mm(ug, b_up)
        sig = 1.0 / (1.0 + jnp.exp(-gate))
        act = gate * sig
        hid = (act * up).astype(BF)
        dhid = mm_t(dy, w_down[0]) + mm(dud, a_dn)
        dup = (dhid * act).astype(BF)
        dgate = (dhid * up * (sig + act * (1.0 - sig))).astype(BF)
        y = mm(hid, w_down[0])
        ud = mm_t(hid, a_dn)
        dx = mm_t(dgate, w_gate[0]) + mm_t(dup, w_up[0])
        dug = mm_t(dgate, b_gate) + mm_t(dup, b_up)
        ug_t = ug.T
        grads[0, :, pl.ds(2 * width + at, tile)] = mm(ug_t[:RANK], dgate).astype(BF)
        grads[0, :, pl.ds(2 * width + hidden + at, tile)] = mm(ug_t[RANK : 2 * RANK], dup).astype(BF)
        grads[0, :, pl.ds(2 * width + 2 * hidden + at, tile)] = mm(dud.T[:RANK], hid).astype(BF)

        @pl.when(j == 0)
        def _():
            y_acc[rows, :] = y
            dx_acc[rows, :] = dx
            ud_acc[rows, :] = ud
            dug_acc[rows, :] = dug

        @pl.when(j > 0)
        def _():
            y_acc[rows, :] += y
            dx_acc[rows, :] += dx
            ud_acc[rows, :] += ud
            dug_acc[rows, :] += dug

        @pl.when(j == tiles - 1)
        def _():
            ud = ud_acc[rows, :].astype(BF)
            dug = dug_acc[rows, :].astype(BF)
            y = y_acc[rows, :] + mm(ud, b_dn[...])
            g = g_s[rows, :][:, :1]
            dg = jnp.sum(c_s[rows, :].astype(F32) * y.astype(BF).astype(F32), axis=1, keepdims=True)
            high, low = split(dg)
            lane = iota((1, 128), 1)
            to = pl.ds(first, n)
            both[to, :width] = (g * y).astype(BF)
            both[to, width : 2 * width] = (dx_acc[rows, :] + mm(dug, a_gu[...])).astype(BF)
            both[to, 2 * width :] = jnp.where(
                lane == e, high.astype(F32), jnp.where(lane == e + 64, low.astype(F32), 0.0)
            ).astype(BF)
            x, dy = x_s[rows, :], dy_s[rows, :]
            to_a = mm(dug.T[: 2 * RANK], x).astype(BF)
            grads[0, :, :width] = to_a[:RANK]
            grads[0, :, width : 2 * width] = to_a[RANK:]
            grads[0, :, 2 * width + 3 * hidden :] = mm(ud.T[:RANK], dy).astype(BF)

    for number in range(1, 512 // rows_of + 1):
        pl.when(blocks == number)(functools.partial(work, number * rows_of))

    @pl.when((e == experts - 1) & (j == tiles - 1))
    def _():
        used = count[1, numbers]
        both[pl.ds(pl.multiple_of(used, rows_of), HALF), :] = jnp.zeros((HALF, both.shape[1]), BF)
        lane = iota((1, 128), 1)

        def combine(block, carry):
            at = pl.ds(pl.multiple_of(block * 256, 256), 256)
            acc[...] = jnp.zeros(acc.shape, F32)
            spots = place[at, :]

            def add(part, carry):
                k0 = pl.multiple_of(part * HALF, HALF)
                slot = (iota((256, HALF), 1) + k0).astype(F32)
                taken = one_hot((slot == spots[:, :1]) | (slot == spots[:, 1:2]))
                acc[...] += mm(taken, both[pl.ds(k0, HALF), :])
                return carry

            lax.fori_loop(0, (used + HALF - 1) // HALF, add, 0)
            h1 = h1_ref[at, :]
            ct = cot[at, :].astype(F32)
            r = lax.rsqrt(jnp.mean(h1 * h1, axis=1, keepdims=True) + EPS)
            gain = gain_m[...]
            n2 = h1 * r * gain
            lin = lin_ref[at, :]
            g = gates[at, :]
            gc = g[:, numbers + 1 : numbers + 2]
            g_fix = [g[:, numbers + 2 + i : numbers + 3 + i] for i in range(2)]
            mixes = []
            for i in range(2):
                a, b = lin[:, kinds + 2 * i : kinds + 2 * i + 1], lin[:, kinds + 2 * i + 1 : kinds + 2 * i + 2]
                top = jnp.maximum(a, b)
                a, b = jnp.exp(a - top), jnp.exp(b - top)
                mixes.append((a / (a + b), b / (a + b)))
            vecs = [vectors[i : i + 1, :] for i in range(2)]
            to_n2 = gc + g_fix[0] * mixes[0][0] + g_fix[1] * mixes[1][0]
            out = h1 + acc[:, :width] + to_n2 * n2
            out = out + (g_fix[0] * mixes[0][1]) * vecs[0] + (g_fix[1] * mixes[1][1]) * vecs[1]
            result[at, :] = out.astype(BF)
            a = jnp.sum(ct * n2, axis=1, keepdims=True)
            bs = [jnp.sum(ct * v, axis=1, keepdims=True) for v in vecs]
            packed = acc[:, 2 * width :]
            dg = jnp.where(lane < numbers, packed + pltpu.roll(packed, 64, 1), 0.0)
            dg = jnp.where(lane == numbers + 1, a, dg)
            for i in range(2):
                dg = jnp.where(lane == numbers + 2 + i, mixes[i][0] * a + mixes[i][1] * bs[i], dg)
            dlin = g * (dg - jnp.sum(g * dg, axis=1, keepdims=True))
            for i in range(2):
                pull = mixes[i][0] * mixes[i][1] * (g_fix[i] * (a - bs[i]))
                dlin = jnp.where(lane == kinds + 2 * i, pull, jnp.where(lane == kinds + 2 * i + 1, -pull, dlin))
            high, low = split(dlin)
            dn2 = acc[:, width : 2 * width] + (mm_t(high, wr[...]) + mm_t(low, wr[...])) + ct * to_n2
            dn2 = dn2 * gain
            back = r * dn2 - h1 * (r * r * r * jnp.mean(dn2 * h1, axis=1, keepdims=True))
            dh1_ref[at, :] = ct + back
            return carry

        lax.fori_loop(0, length // 256, combine, 0)


def experts_both_ways(xb, h1, lin, cot, routes, carried, gain_m, wr, vectors, w_gu, w_dn, maps):
    length, width = xb.shape
    experts, hidden = w_dn.shape[0], w_dn.shape[1]
    tile = hidden // 2
    tiles = hidden // tile
    most = 2 * length + experts * 128
    total = 3 * width + 3 * hidden

    def whole(a):
        return pl.BlockSpec(a.shape, lambda e, j: (0,) * a.ndim, pipeline_mode=pl.Buffered(1))

    resident = (xb, h1, lin, cot, routes, carried, gain_m, wr, vectors)
    return pl.pallas_call(
        experts_kernel,
        grid=(experts, tiles),
        out_shape=[
            jax.ShapeDtypeStruct((length, width), BF),
            jax.ShapeDtypeStruct((length, width), F32),
            jax.ShapeDtypeStruct((experts, RANK, total), BF),
        ],
        in_specs=[whole(a) for a in resident]
        + [
            pl.BlockSpec((1, width, tile), lambda e, j: (e, 0, j)),
            pl.BlockSpec((1, width, tile), lambda e, j: (e, 0, tiles + j)),
            pl.BlockSpec((1, tile, width), lambda e, j: (e, j, 0)),
            pl.BlockSpec((1, RANK, total), lambda e, j: (e, 0, 0)),
        ],
        out_specs=[
            pl.BlockSpec((length, width), lambda e, j: (0, 0), pipeline_mode=pl.Buffered(1)),
            pl.BlockSpec((length, width), lambda e, j: (0, 0), pipeline_mode=pl.Buffered(1)),
            pl.BlockSpec((1, RANK, total), lambda e, j: (e, 0, 0)),
        ],
        scratch_shapes=[
            pltpu.SMEM((2, experts + 1), jnp.int32),
            pltpu.VMEM((length, 128), F32),
            pltpu.VMEM((128, length), F32),
            pltpu.VMEM((length, 128), F32),
            pltpu.VMEM((128, length), F32),
            pltpu.VMEM((most + HALF, 2 * width + 128), BF),
            pltpu.VMEM((512, width), BF),
            pltpu.VMEM((512, width), BF),
            pltpu.VMEM((512, width), BF),
            pltpu.VMEM((512, 128), F32),
            pltpu.VMEM((512, width), F32),
            pltpu.VMEM((512, width), F32),
            pltpu.VMEM((512, 128), BF),
            pltpu.VMEM((512, 128), F32),
            pltpu.VMEM((512, 128), BF),
            pltpu.VMEM((512, 128), F32),
            pltpu.VMEM((128, width), BF),
            pltpu.VMEM((128, width), BF),
            pltpu.VMEM((256, 2 * width + 128), F32),
        ],
        compiler_params=pltpu.CompilerParams(vmem_limit_bytes=60 * MIB),
        name="experts_both_ways",
    )(*resident, w_gu, w_gu, w_dn, maps)


def gather_experts(weights, senders):
    w_gu, w_dn, gu_down, gu_up, dn_down, dn_up = weights
    maps = jnp.concatenate(
        [gu_down[0, 0].T, gu_down[0, 1].T, gu_up[0, 0], gu_up[0, 1], dn_down[0].T, dn_up[0]], axis=1
    )
    to = (senders[:, None] * RANK + jnp.arange(RANK)[None, :]).reshape(-1)
    rows = mm((to[:, None] == jnp.arange(128)[None, :]).astype(BF), maps).astype(BF)
    rows = rows.reshape(senders.shape[0], RANK, -1)
    return (
        lax.all_gather(w_gu, "expert", axis=0, tiled=True),
        lax.all_gather(w_dn, "expert", axis=0, tiled=True),
        lax.all_to_all(rows, "expert", split_axis=0, concat_axis=0, tiled=True),
    )


BOTH = ("dp", "expert")


def sum_expert_maps(compact, spread):
    copies = lax.axis_size("dp")
    experts, rank, columns = compact.shape
    each = -(-columns // (copies * 128)) * 128
    parts = jnp.pad(compact, ((0, 0), (0, 0), (0, copies * each - columns)))
    parts = parts.reshape(experts, rank, copies, each).transpose(2, 0, 1, 3).reshape(copies * experts, rank, each)
    got = lax.all_to_all(parts, BOTH, split_axis=0, concat_axis=0, tiled=True)
    own = mm(spread, got.reshape(-1, each)).astype(BF)
    return lax.all_gather(own, "dp", axis=1, tiled=True)


def sum_attention_maps(compact, spread):
    devices = lax.axis_size("dp") * lax.axis_size("expert")
    maps, rank, width = compact.shape
    cuts = devices // maps
    parts = compact.reshape(maps, rank, cuts, width // cuts).transpose(0, 2, 1, 3).reshape(devices, rank, width // cuts)
    got = lax.all_to_all(parts, BOTH, split_axis=0, concat_axis=0, tiled=True)
    own = mm(spread, got.reshape(devices * rank, width // cuts)).astype(BF)
    whole = lax.all_gather(own[None], BOTH, axis=0, tiled=True)
    return whole.reshape(maps, cuts, 128, width // cuts).transpose(0, 2, 1, 3).reshape(maps, 128, width).astype(F32)


def body(
    exchange,
    tokens, cotangent, attention_norm_gain, query_key_value_weight, attention_output_weight,
    adapter_attention_down_maps, adapter_query_key_value_up_maps, adapter_output_up_map,
    experts_norm_gain, router_weight, constant_expert_mixing, constant_expert_vectors,
    expert_gate_up_weight, expert_down_weight, adapter_expert_gate_up_down_maps, adapter_expert_gate_up_up_maps,
    adapter_expert_down_down_maps, adapter_expert_down_up_maps,
    routes, router_logits_carried, picture_span_starts, sequence_adapter_index,
):
    groups = lax.axis_size("expert")
    width = tokens.shape[1]
    hidden = expert_down_weight.shape[1]
    first = lax.axis_index("dp") * groups
    senders = lax.dynamic_slice_in_dim(sequence_adapter_index, first, groups, 0)
    adapter = lax.dynamic_slice_in_dim(senders, lax.axis_index("expert"), 1, 0)
    gain_a, gain_m = attention_norm_gain[None], experts_norm_gain[None]
    spans = picture_span_starts.reshape(-1)
    router = jnp.concatenate([router_weight, constant_expert_mixing], axis=1)
    router = jnp.pad(router, ((0, 0), (0, 128 - router.shape[1])))
    own = (
        expert_gate_up_weight, expert_down_weight, adapter_expert_gate_up_down_maps,
        adapter_expert_gate_up_up_maps, adapter_expert_down_down_maps, adapter_expert_down_up_maps,
    )
    outs = attention_forward(
        tokens, gain_a, query_key_value_weight, adapter_attention_down_maps, adapter_query_key_value_up_maps,
        attention_output_weight, adapter_output_up_map, gain_m, router, spans, adapter,
        *((own, senders) if exchange else ()),
    )
    xa, q, k, v, ob, ua, uo, lse, h1, xb, lin, wqk, down_s, up_s = outs[:14]
    weights = outs[14:] if exchange else gather_experts(own, senders)
    result, dh1, expert_maps = experts_both_ways(
        xb, h1, lin, cotangent, routes, router_logits_carried, gain_m, router, constant_expert_vectors, *weights
    )
    grad_tokens, attention_maps = attention_backward(
        spans, dh1, tokens, gain_a, query_key_value_weight, wqk, attention_output_weight, down_s, up_s,
        xa, q, k, v, ob, ua, uo, lse,
    )
    to = (sequence_adapter_index[:, None] * RANK + jnp.arange(RANK)[None, :]).reshape(-1)
    spread = (jnp.arange(128)[:, None] == to[None, :]).astype(BF)
    of_expert = sum_expert_maps(expert_maps, spread)[:, : expert_maps.shape[2]].astype(F32)
    of_attention = sum_attention_maps(attention_maps, spread)
    cuts = [width, 2 * width, 2 * width + hidden, 2 * width + 2 * hidden, 2 * width + 3 * hidden]
    gud0, gud1, guu0, guu1, dnd, dnu = jnp.split(of_expert, cuts, axis=1)
    return (
        result,
        grad_tokens,
        of_attention[:4].transpose(0, 2, 1),
        of_attention[4:7],
        of_attention[7],
        jnp.stack([gud0.T, gud1.T])[None],
        jnp.stack([guu0, guu1])[None],
        dnd.T[None],
        dnu[None],
    )


def solution(mesh):
    tokens, own = P(("dp", "expert"), None), P("expert", None, None)
    own4 = P("expert", None, None, None)
    in_specs = (tokens, tokens) + (P(),) * 10 + (own, own, own4, own4, own, own) + (tokens,) * 3 + (P(),)
    out_specs = (tokens, tokens, P(), P(), P(), own4, own4, own, own)
    exchange = dict(mesh.shape) == {"dp": 8, "expert": 4}
    return jax.shard_map(functools.partial(body, exchange), mesh=mesh, in_specs=in_specs, out_specs=out_specs, check_vma=False)
```

```python
import functools

import jax
import jax.numpy as jnp
import numpy as np
from jax import lax
from jax.experimental import pallas as pl
from jax.experimental.pallas import tpu as pltpu
from jax.sharding import PartitionSpec as P

HEADS = 12
HD = 64
RANK = 16
PIC = 256
GROUP = 256
HALF = 512
EPS = 1e-06
NEG = -1e30
BF = jnp.bfloat16
F32 = jnp.float32
MIB = 1024 * 1024


def mm(a, b):
    return jnp.dot(a, b, preferred_element_type=F32)


def mm_t(a, b):
    return lax.dot_general(a, b, (((1,), (1,)), ((), ())), preferred_element_type=F32)


def t_mm(a, b):
    return lax.dot_general(a, b, (((0,), (0,)), ((), ())), preferred_element_type=F32)


def iota(shape, dim):
    return lax.broadcasted_iota(jnp.int32, shape, dim)


def one_hot(condition):
    return jnp.where(condition, 1.0, 0.0).astype(BF)


def picker(adapter, place, rows=128, columns=128):
    row, column = iota((rows, columns), 0), iota((rows, columns), 1)
    return one_hot((row - adapter * RANK == column - place * RANK) & (column // RANK == place))


def placer(adapter, place, rows=128, columns=128):
    row, column = iota((rows, columns), 0), iota((rows, columns), 1)
    return one_hot((column - adapter * RANK == row - place * RANK) & (row // RANK == place))


def head_order(back):
    row, column = iota((GROUP, GROUP), 0), iota((GROUP, GROUP), 1)
    a, b = (column, row) if back else (row, column)
    return one_hot(a == (b % 128 // 32) * 64 + b // 128 * 32 + b % 32)


def rope_tables(length):
    spacing = 10000.0 ** (-np.arange(0, HD, 2, dtype=np.float32) / np.float32(HD))
    angles = np.arange(length, dtype=np.float32)[:, None] * spacing.astype(np.float32)[None, :]
    angles = np.tile(angles, (1, 4))
    return np.cos(angles).astype(np.float32), np.sin(angles).astype(np.float32)


def rope(pair, cosine, sine):
    low, high = pair[:, :128], pair[:, 128:]
    return jnp.concatenate([low * cosine - high * sine, high * cosine + low * sine], axis=1)


def span_bias(start, transposed):
    a, b = iota((HALF, HALF), 0), iota((HALF, HALF), 1)
    query, key = (b, a) if transposed else (a, b)
    inside = (query >= start) & (query < start + PIC) & (key >= start) & (key < start + PIC)
    return jnp.where((key <= query) | inside, 0.0, NEG)


UNITS = 32
CHUNKS = ((0, 1), (1, 2), (3, 1), (4, 2))
EXTRA = ((0, 2), (2, 2))
MESH = pl.DeviceIdType.MESH


def other(index, step):
    return index + step - 2 * step * ((index // step) % 2)


def sending_steps(own, outs, scratch):
    senders, w_gu, w_dn, gu_down, gu_up, dn_down, dn_up = own
    all_gu, all_dn, all_maps = outs
    bounce_gu, bounce_dn, compact, send, recv, local = scratch
    sources, targets, bounce = (w_gu, w_dn), (all_gu, all_dn), (bounce_gu, bounce_dn)
    dp, ex = lax.axis_index("dp"), lax.axis_index("expert")
    sibling, far = other(ex, 1), other(ex, 2)
    peers = {
        "x": (other(dp, 1), ex), "z": (other(dp, 2), ex), "y": (dp, far), "s": (dp, sibling), "d": (dp, other(far, 1)),
    }
    x, z = dp % 2, (dp // 2) % 2
    quarter = {"y": z * 2 + x, "x": z * 2 + 1 - x, "z": (1 - z) * 2 + x, "d": (1 - z) * 2 + 1 - x}
    kind = (x + z) % 2
    slots = {}
    for name in ("y", "x", "z", "d"):
        for chunk in CHUNKS:
            slots[name, chunk] = len(slots)
    for name in ("e", "o"):
        for chunk in EXTRA:
            slots[name, chunk] = len(slots)
    count = len(slots)
    started = []

    def views(refs, expert, key):
        name, (first, number) = key
        if name in quarter:
            first = quarter[name] * 6 + first
        else:
            first = 24 + 4 * (kind if name == "e" else 1 - kind) + first
        columns, rows = refs[0].shape[-1] // UNITS, refs[1].shape[-2] // UNITS
        return (
            refs[0].at[expert, :, pl.ds(pl.multiple_of(first * columns, columns), number * columns)],
            refs[1].at[expert, pl.ds(pl.multiple_of(first * rows, rows), number * rows), :],
        )

    def copies(source, target, peer, slot):
        for i in range(len(source())):
            number = len(started)

            def made(i=i, number=number):
                return pltpu.make_async_remote_copy(
                    src_ref=source()[i], dst_ref=target()[i], send_sem=send.at[number], recv_sem=recv.at[slot, i],
                    device_id=peers[peer], device_id_type=MESH,
                )

            made().start()
            started.append(made)

    def arrived(view, slot, i):
        pltpu.make_async_remote_copy(
            src_ref=view, dst_ref=view, send_sem=send.at[0], recv_sem=recv.at[slot, i],
            device_id=peers["s"], device_id_type=MESH,
        ).wait_recv()

    def begin():
        barrier = pltpu.get_barrier_semaphore()
        for peer in peers.values():
            pl.semaphore_signal(barrier, inc=1, device_id=peer, device_id_type=MESH)
        pl.semaphore_wait(barrier, len(peers))
        for name, chunks in (("y", CHUNKS), ("e", EXTRA)):
            for chunk in chunks:
                key = name, chunk
                copies(
                    functools.partial(views, sources, 0, key), functools.partial(views, targets, ex, key), "y", slots[key]
                )
        copies(lambda: [s.at[0] for s in sources], lambda: [t.at[ex] for t in targets], "s", 2 * count)
        for i in range(2):
            pltpu.make_async_copy(sources[i].at[0], bounce[i], local.at[i]).start()

    def select():
        row, column = iota((64, 128), 0), iota((64, 128), 1)
        first = sum(jnp.where(row // RANK == i, senders[i], 0) for i in range(4))
        rows = one_hot(column == first * RANK + row % RANK)
        width, hidden = gu_down.shape[2], dn_down.shape[1]
        parts = [
            (0, mm_t(rows, gu_down[0, 0])),
            (width, mm_t(rows, gu_down[0, 1])),
            (2 * width, mm(rows, gu_up[0, 0])),
            (2 * width + hidden, mm(rows, gu_up[0, 1])),
            (2 * width + 2 * hidden, mm_t(rows, dn_down[0])),
            (2 * width + 3 * hidden, mm(rows, dn_up[0])),
        ]
        for at, part in parts:
            for i in range(4):
                compact[i, :, pl.ds(at, part.shape[1])] = part[i * RANK : (i + 1) * RANK].astype(BF)
        for i, (peer, to) in enumerate((("s", sibling), ("y", far), ("d", other(far, 1)))):
            copies(lambda to=to: [compact.at[to]], lambda: [all_maps.at[ex]], peer, 2 * count + 1 + i)
        pltpu.make_async_copy(compact.at[ex], all_maps.at[ex], local.at[2]).start()

    def turn():
        for i in range(2):
            pltpu.make_async_copy(sources[i].at[0], bounce[i], local.at[i]).wait()
            pltpu.make_async_copy(bounce[i], targets[i].at[ex], local.at[i]).start()

    along_x = (CHUNKS[0], CHUNKS[3])

    def got(name, chunk):
        key = name, chunk
        to = []
        if name == "y":
            to = [("x", slots["x", chunk]), ("z", slots["z", chunk])]
        if name == "x" and chunk not in along_x:
            to = [("z", slots["d", chunk])]
        if name == "z" and chunk in along_x:
            to = [("x", slots["d", chunk])]
        if name == "e":
            to = [("x" if chunk == EXTRA[0] else "z", slots["o", chunk])]

        def step():
            mine = functools.partial(views, targets, far, key)
            for i in range(2):
                arrived(mine()[i], slots[key], i)
            for peer, slot in to:
                copies(mine, mine, peer, slot)
            copies(mine, mine, "s", count + slots[key])

        return step

    def end():
        for made in started:
            made().wait_send()
        for i in range(2):
            pltpu.make_async_copy(bounce[i], targets[i].at[ex], local.at[i]).wait()
            arrived(targets[i].at[sibling], 2 * count, i)
        pltpu.make_async_copy(compact.at[ex], all_maps.at[ex], local.at[2]).wait()
        for i, source in enumerate((sibling, far, other(far, 1))):
            arrived(all_maps.at[source], 2 * count + 1 + i, 0)
        for key, slot in slots.items():
            view = views(targets, other(far, 1), key)
            for i in range(2):
                arrived(view[i], count + slot, i)

    c, e = CHUNKS, EXTRA
    return {
        "begin": [begin, select],
        "ready": [turn],
        "projected": [got("y", c[0])],
        2: [got("x", c[0]), got("z", c[0])],
        4: [got("y", c[1])],
        6: [got("y", c[2]), got("d", c[0])],
        9: [got("x", c[1]), got("z", c[1])],
        "end": [
            got("y", c[3]), got("x", c[2]), got("z", c[2]), got("e", e[0]), got("x", c[3]), got("z", c[3]), got("e", e[1]),
            got("d", c[1]), got("d", c[2]), got("o", e[0]), got("d", c[3]), got("o", e[1]), end,
        ],
    }


def attention_forward_kernel(exchange, *refs):
    spans, adapter_ref, tok, gain_a, wqkv, down, up, wo, up_out, gain_m, wr, cos, sin = refs[:13]
    refs = refs[13:]
    own = ()
    if exchange:
        own, refs = refs[:7], refs[7:]
    xa_ref, q_ref, k_ref, v_ref, ob_ref, ua_ref, uo_ref, lse_ref, h1_ref, xb_ref, lin_ref, wqk_ref, down_ref, up_s = refs[:14]
    refs = refs[14:]
    steps = {}
    if exchange:
        steps = sending_steps(own, refs[:3], refs[4:])
        bias = refs[3]
    else:
        (bias,) = refs
    length, width = tok.shape
    groups = width // GROUP
    adapter = adapter_ref[0]

    def run(point):
        for step in steps.get(point, ()):
            step()

    run("begin")
    order = head_order(False)
    down_s = sum(mm(down[p], picker(adapter, p)) for p in range(3)).astype(BF)
    down_o = mm(down[3], picker(adapter, 0)).astype(BF)
    up_o = mm(placer(adapter, 0), up_out[...]).astype(BF)
    down_ref[0] = down_s
    down_ref[1] = down_o
    up_s[:, pl.ds(3 * width, width)] = up_o
    for p in range(3):
        rows = mm(placer(adapter, p), up[p]).astype(BF)
        for g in range(groups):
            block = rows[:, g * GROUP : (g + 1) * GROUP]
            if p < 2:
                block = mm(block, order).astype(BF)
            up_s[:, pl.ds(p * width + g * GROUP, GROUP)] = block
    for g in range(2 * groups):
        at = pl.ds(g * GROUP, GROUP)
        wqk_ref[:, at] = mm(wqkv[:, at], order).astype(BF)
    for half in range(length // HALF):
        bias[half] = span_bias(spans[half] - half * HALF, False)
    run("ready")

    def project(block, carry):
        at = pl.ds(pl.multiple_of(block * 256, 256), 256)
        h0 = tok[at, :].astype(F32)
        x = h0 * lax.rsqrt(jnp.mean(h0 * h0, axis=1, keepdims=True) + EPS) * gain_a[...]
        x = x.astype(BF)
        xa_ref[at, :] = x
        u = mm(x, down_s).astype(BF)
        ua_ref[at, :] = u
        c, s = cos[at, :], sin[at, :]
        for p, out in enumerate((q_ref, k_ref)):
            for g in range(groups):
                lanes = pl.ds(p * width + g * GROUP, GROUP)
                lin = mm(x, wqk_ref[:, lanes]) + mm(u, up_s[:, lanes])
                out[at, pl.ds(g * GROUP, GROUP)] = rope(lin, c, s).astype(BF)
        lanes = pl.ds(2 * width, width)
        v_ref[at, :] = (mm(x, wqkv[:, lanes]) + mm(u, up_s[:, lanes])).astype(BF)
        return carry

    lax.fori_loop(0, length // 256, project, 0)
    run("projected")

    lane = iota((1, GROUP), 1)
    lse_ref[...] = jnp.zeros(lse_ref.shape, F32)
    ob_f = ob_ref

    def attend(head, carry):
        g, h = head // 4, head % 4
        lanes = pl.ds(pl.multiple_of(g * GROUP, GROUP), GROUP)
        qk_own = jnp.where((lane % 128) // 32 == h, 1.0, 0.0).astype(BF)
        v_own = jnp.where(lane // 64 == h, 1.0, 0.0)
        kh = k_ref[:, lanes] * qk_own
        vh = v_ref[:, lanes] * v_own.astype(BF)
        for half in range(length // HALF):
            at = pl.ds(half * HALF, HALF)
            q = q_ref[at, lanes] * BF(0.125)
            keys = (half + 1) * HALF
            diag = mm_t(q, kh[half * HALF : keys]) + bias[half]
            top = jnp.max(diag, axis=1, keepdims=True)
            if half:
                past = mm_t(q, kh[: half * HALF])
                top = jnp.maximum(top, jnp.max(past, axis=1, keepdims=True))
            e = jnp.exp(diag - top)
            total = jnp.sum(e, axis=1, keepdims=True)
            o = mm(e.astype(BF), vh[half * HALF : keys])
            if half:
                e = jnp.exp(past - top)
                total = total + jnp.sum(e, axis=1, keepdims=True)
                o = o + mm(e.astype(BF), vh[: half * HALF])
            o = o * pl.reciprocal(total, approx=False)
            lse = top + jnp.log(total)
            lse_ref[at, :] = jnp.where(iota((1, 128), 1) == head, lse, lse_ref[at, :])
            old = jnp.where(v_own > 0.5, 0.0, ob_f[at, lanes].astype(F32))
            ob_f[at, lanes] = jnp.where(v_own > 0.5, o, old).astype(BF)
        for point in steps:
            if isinstance(point, int):
                pl.when(head == point)(functools.partial(run, point))
        return carry

    lax.fori_loop(0, HEADS, attend, 0)

    def finish(block, carry):
        at = pl.ds(pl.multiple_of(block * 256, 256), 256)
        o = ob_ref[at, :]
        u = mm(o, down_o).astype(BF)
        uo_ref[at, :] = u
        h1 = tok[at, :].astype(F32) + (mm(o, wo[...]) + mm(u, up_o))
        h1_ref[at, :] = h1
        x = h1 * lax.rsqrt(jnp.mean(h1 * h1, axis=1, keepdims=True) + EPS) * gain_m[...]
        x = x.astype(BF)
        xb_ref[at, :] = x
        lin_ref[at, :] = mm(x, wr[...])
        return carry

    lax.fori_loop(0, length // 256, finish, 0)
    run("end")


def attention_forward(tok, gain_a, wqkv, down, up, wo, up_out, gain_m, wr, spans, adapter, own=(), senders=None):
    length, width = tok.shape
    cos, sin = rope_tables(length)
    shapes = [
        ((length, width), BF),
        ((length, width), BF),
        ((length, width), BF),
        ((length, width), BF),
        ((length, width), BF),
        ((length, 128), BF),
        ((length, 128), BF),
        ((length, 128), F32),
        ((length, width), F32),
        ((length, width), BF),
        ((length, 128), F32),
        ((width, 2 * width), BF),
        ((2, width, 128), BF),
        ((128, 4 * width), BF),
    ]
    vmem, smem = pl.BlockSpec(memory_space=pltpu.VMEM), pl.BlockSpec(memory_space=pltpu.SMEM)
    anys = pl.BlockSpec(memory_space=pl.ANY)
    in_specs, out_specs = [smem, smem] + [vmem] * 11, [vmem] * len(shapes)
    scratch = [pltpu.VMEM((length // HALF, HALF, HALF), F32)]
    params = dict(vmem_limit_bytes=60 * MIB)
    args = (spans, adapter, tok, gain_a, wqkv, down, up, wo, up_out, gain_m, wr, cos, sin)
    if own:
        w_gu, w_dn = own[:2]
        columns = 3 * width + 3 * w_dn.shape[1]
        in_specs += [smem, anys, anys] + [vmem] * 4
        args += (senders, *own)
        shapes += [((4, *w_gu.shape[1:]), BF), ((4, *w_dn.shape[1:]), BF), ((4, RANK, columns), BF)]
        out_specs += [anys] * 3
        scratch += [
            pltpu.VMEM(w_gu.shape[1:], BF),
            pltpu.VMEM(w_dn.shape[1:], BF),
            pltpu.VMEM((4, RANK, columns), BF),
            pltpu.SemaphoreType.DMA((96,)),
            pltpu.SemaphoreType.DMA((48, 2)),
            pltpu.SemaphoreType.DMA((3,)),
        ]
        params.update(collective_id=0, has_side_effects=True)
    return pl.pallas_call(
        functools.partial(attention_forward_kernel, bool(own)),
        out_shape=[jax.ShapeDtypeStruct(s, t) for s, t in shapes],
        in_specs=in_specs,
        out_specs=out_specs,
        scratch_shapes=scratch,
        compiler_params=pltpu.CompilerParams(**params),
        name="attention_forward",
    )(*args)


class Mail:
    def __init__(self, send, recv):
        self.send, self.recv, self.started = send, recv, []

    def post(self, source, target, peer, slot):
        number = len(self.started)

        def made():
            return pltpu.make_async_remote_copy(
                src_ref=source(), dst_ref=target(), send_sem=self.send.at[number], recv_sem=self.recv.at[slot],
                device_id=peer, device_id_type=MESH,
            )

        made().start()
        self.started.append(made)

    def arrived(self, view, slot, peer):
        pltpu.make_async_remote_copy(
            src_ref=view, dst_ref=view, send_sem=self.send.at[0], recv_sem=self.recv.at[slot],
            device_id=peer, device_id_type=MESH,
        ).wait_recv()

    def finish(self):
        for made in self.started:
            made().wait_send()


def meet(peers):
    barrier = pltpu.get_barrier_semaphore()
    for peer in peers:
        pl.semaphore_signal(barrier, inc=1, device_id=peer, device_id_type=MESH)
    pl.semaphore_wait(barrier, len(peers))


def summing_steps(refs, grad_maps):
    maps_in, takers, all_e, all_a, e_got, e_two, e_own, a_in, a_part, a_z, a_own, send, recv, local = refs
    mail = Mail(send, recv)
    dp, ex = lax.axis_index("dp"), lax.axis_index("expert")
    x, z = dp % 2, dp // 2
    share = e_two.shape[3]
    group = {k: (ex + k) % 4 for k in range(1, 4)}
    later = {k: (z + k) % 4 for k in range(1, 4)}
    along = {k: (dp + k) % 8 for k in range(1, 8)}
    along_z = {k: ((z + k) % 4) * 2 + x for k in range(1, 4)}
    plane = {(a, k): (other(dp, 1) if a else dp, (ex + k) % 4) for a in range(2) for k in range(4) if (a, k) != (0, 0)}
    x_peer, y_peer, s_peer = (other(dp, 1), ex), (dp, other(ex, 2)), (dp, other(ex, 1))
    free = [0]

    def slots(n):
        free[0] += n
        return free[0] - n

    first = {n: slots(c) for n, c in dict(e1=4, e2=8, e3=4, e4=4, a1=8, a2=4, a3=4, ay=1, ax=2, a_s=4).items()}

    def begin():
        meet([(dp, group[k]) for k in group] + [(along[k], ex) for k in along] + [plane[1, k] for k in range(1, 4)])
        for k, to in group.items():
            mail.post(lambda to=to: maps_in.at[to], lambda: e_got.at[ex], (dp, to), first["e1"] + k)
        pltpu.make_async_copy(maps_in.at[ex], e_got.at[ex], local.at[0]).start()

    def spread_out():
        for k in group:
            source = (ex + 4 - k) % 4
            mail.arrived(e_got.at[source], first["e1"] + k, (dp, source))
        pltpu.make_async_copy(maps_in.at[ex], e_got.at[ex], local.at[0]).wait()

        def columns(to):
            return e_got.at[:, :, pl.ds(pl.multiple_of(to * share, 128), share)]

        for k, to in along.items():
            mail.post(lambda to=to: columns(to), lambda: e_two.at[dp], (to, ex), first["e2"] + k)
        e_two[dp] = e_got[:, :, pl.ds(pl.multiple_of(dp * share, 128), share)]

    def placed(sender, columns):
        row, column = iota((128, columns), 0), iota((128, columns), 1)
        return one_hot(row - sender * RANK == column % RANK)

    def add_up():
        for k in along:
            source = (dp + 8 - k) % 8
            mail.arrived(e_two.at[source], first["e2"] + k, (source, ex))
        rows = e_two[...].reshape(-1, share)
        e_own[...] = mm(placed(takers[...], rows.shape[0]), rows).astype(BF)
        for k, to in along_z.items():
            mail.post(lambda: e_own, lambda: all_e.at[dp], (to, ex), first["e3"] + k)
        mail.post(lambda: e_own, lambda: all_e.at[dp], x_peer, first["e4"])
        pltpu.make_async_copy(e_own, all_e.at[dp], local.at[1]).start()

    def e_forward():
        for k in along_z:
            source = ((z + 4 - k) % 4) * 2 + x
            mail.arrived(all_e.at[source], first["e3"] + k, (source, ex))
            here = functools.partial(lambda source: all_e.at[source], source)
            mail.post(here, here, x_peer, first["e4"] + k)

    def a_share():
        for (a, k), to in plane.items():
            number = 2 * to[1] + to[0] % 2
            mail.post(
                lambda number=number: grad_maps.at[number], lambda: a_in.at[x * 4 + ex], to, first["a1"] + a * 4 + k
            )
        a_in[x * 4 + ex] = grad_maps[2 * ex + x]

    def a_partial():
        for a, k in plane:
            source = (other(dp, 1) if a else dp, (ex + 4 - k) % 4)
            at = (source[0] % 2) * 4 + source[1]
            mail.arrived(a_in.at[at], first["a1"] + a * 4 + k, source)
        rows = a_in[...].reshape(128, -1)
        senders = takers[:, pl.ds(pl.multiple_of(z * 128, 128), 128)]
        a_part[...] = mm(placed(senders, 128), rows).astype(BF)
        for k, to in later.items():
            mail.post(
                lambda to=to: a_part.at[pl.ds(pl.multiple_of(to * 32, 32), 32)], lambda: a_z.at[z],
                (along_z[k], ex), first["a2"] + k,
            )
        a_z[z] = a_part[pl.ds(pl.multiple_of(z * 32, 32), 32), :]

    def piece(number, place):
        return all_a.at[number, pl.ds(pl.multiple_of(place * 32, 32), 32)]

    mine = 2 * ex + x

    def a_total():
        for k in range(1, 4):
            source = (z + 4 - k) % 4
            mail.arrived(a_z.at[source], first["a2"] + k, (source * 2 + x, ex))
        a_own[...] = sum(a_z[i].astype(F32) for i in range(4)).astype(BF)
        for k in range(1, 4):
            mail.post(lambda: a_own, lambda: piece(mine, z), (along_z[k], ex), first["a3"] + k)
        pltpu.make_async_copy(a_own, piece(mine, z), local.at[2]).start()

    def a_gather():
        pltpu.make_async_copy(a_own, piece(mine, z), local.at[2]).wait()
        for k in range(1, 4):
            source = (z + 4 - k) % 4
            mail.arrived(piece(mine, source), first["a3"] + k, (source * 2 + x, ex))

        def send(number, peer, slot):
            here = functools.partial(lambda number: all_a.at[number], number)
            mail.post(here, here, peer, slot)

        of_y, of_x = 2 * other(ex, 2) + x, 2 * ex + 1 - x
        of_xy = 2 * other(ex, 2) + 1 - x
        send(mine, y_peer, first["ay"])
        send(mine, x_peer, first["ax"])
        send(mine, s_peer, first["a_s"])
        mail.arrived(all_a.at[of_y], first["ay"], y_peer)
        send(of_y, x_peer, first["ax"] + 1)
        send(of_y, s_peer, first["a_s"] + 1)
        mail.arrived(all_a.at[of_x], first["ax"], x_peer)
        send(of_x, s_peer, first["a_s"] + 2)
        mail.arrived(all_a.at[of_xy], first["ax"] + 1, x_peer)
        send(of_xy, s_peer, first["a_s"] + 3)

    def end():
        sib = other(ex, 1)
        numbers = (2 * sib + x, 2 * other(sib, 2) + x, 2 * sib + 1 - x, 2 * other(sib, 2) + 1 - x)
        for i, number in enumerate(numbers):
            mail.arrived(all_a.at[number], first["a_s"] + i, s_peer)
        for k in range(4):
            source = ((z + 4 - k) % 4) * 2 + 1 - x
            mail.arrived(all_e.at[source], first["e4"] + k, x_peer)
        pltpu.make_async_copy(e_own, all_e.at[dp], local.at[1]).wait()
        mail.finish()

    return {
        "begin": [begin], 1: [spread_out], 10: [add_up], "maps": [a_share, e_forward], "half": [a_partial],
        "end": [a_total, a_gather, end],
    }


def attention_backward_kernel(exchange, *refs):
    spans, dh1_ref, tok, gain_a, wqkv, wqk, wo, down_ref, up_s, cos, sin = refs[:11]
    xa_ref, q_ref, k_ref, v_ref, ob_ref, ua_ref, uo_ref, lse_ref = refs[11:19]
    steps = {}
    if exchange:
        grad_tok, grad_maps, own = refs[21], refs[24], refs[36:]
        steps = summing_steps((*refs[19:21], *refs[22:24], *own), grad_maps)
        bias, dob, datt, duo, lse_t, center_t, dq, dk, dv, dlin, dua = refs[25:36]
    else:
        grad_tok, grad_maps = refs[19:21]
        bias, dob, datt, duo, lse_t, center_t, dq, dk, dv, dlin, dua = refs[21:]
    length, width = tok.shape
    groups = width // GROUP

    def run(point):
        for step in steps.get(point, ()):
            step()

    run("begin")
    for half in range(length // HALF):
        bias[half] = span_bias(spans[half] - half * HALF, True)
    of_head = one_hot(iota((128, width), 1) // HD == iota((128, width), 0))

    def outer(block, carry):
        at = pl.ds(pl.multiple_of(block * 256, 256), 256)
        d = dh1_ref[at, :].astype(BF)
        datt[at, :] = d
        u = mm_t(d, up_s[:, pl.ds(3 * width, width)]).astype(BF)
        duo[at, :] = u
        do = (mm_t(d, wo[...]) + mm_t(u, down_ref[1])).astype(BF)
        dob[at, :] = do
        both = do.astype(F32) * ob_ref[at, :].astype(F32)
        high = both.astype(BF)
        low = (both - high.astype(F32)).astype(BF)
        center_t[:, at] = mm_t(of_head, high) + mm_t(of_head, low)
        lse_t[:, at] = lse_ref[at, :].T
        return carry

    lax.fori_loop(0, length // 256, outer, 0)
    dq[...] = jnp.zeros(dq.shape, F32)
    dk[...] = jnp.zeros(dk.shape, F32)
    dv[...] = jnp.zeros(dv.shape, F32)
    lane = iota((1, GROUP), 1)

    def attend(head, carry):
        g, h = head // 4, head % 4
        lanes = pl.ds(pl.multiple_of(g * GROUP, GROUP), GROUP)
        qk_own = jnp.where((lane % 128) // 32 == h, 1.0, 0.0).astype(BF)
        v_own = jnp.where(lane // 64 == h, 1.0, 0.0).astype(BF)
        lse = lse_t[pl.ds(head, 1), :]
        center = center_t[pl.ds(head, 1), :]
        for half in range(length // HALF):
            at = pl.ds(half * HALF, HALF)
            late = pl.ds(half * HALF, length - half * HALF)
            kh = k_ref[at, lanes] * qk_own
            vh = v_ref[at, lanes] * v_own
            q = q_ref[late, lanes] * BF(0.125)
            do = dob[late, lanes]
            s = mm_t(kh, q) - lse[:, half * HALF :]
            if half * HALF + HALF < length:
                s = jnp.concatenate([s[:, :HALF] + bias[half], s[:, HALF:]], axis=1)
            else:
                s = s + bias[half]
            prob = jnp.exp(s)
            dp = mm_t(vh, do)
            ds = (prob * (dp - center[:, half * HALF :])).astype(BF)
            dv[at, lanes] += mm(prob.astype(BF), do * v_own)
            dk[at, lanes] += mm(ds, q * qk_own)
            dq[late, lanes] += t_mm(ds, kh)
        for point in steps:
            if isinstance(point, int):
                pl.when(head == point)(functools.partial(run, point))
        return carry

    lax.fori_loop(0, HEADS, attend, 0)

    def turn_back(block, carry):
        at = pl.ds(pl.multiple_of(block * 256, 256), 256)
        c, s = cos[at, :], -sin[at, :]
        for g in range(groups):
            lanes = pl.ds(g * GROUP, GROUP)
            dlin[at, lanes] = rope(dq[at, lanes] * 0.125, c, s).astype(BF)
            dlin[at, pl.ds(width + g * GROUP, GROUP)] = rope(dk[at, lanes], c, s).astype(BF)
        dlin[at, pl.ds(2 * width, width)] = dv[at, :].astype(BF)
        dua[at, :] = mm_t(dlin[at, :], up_s[:, pl.ds(0, 3 * width)]).astype(BF)
        return carry

    lax.fori_loop(0, length // 256, turn_back, 0)
    order = head_order(True)
    grads = t_mm(dua[...], xa_ref[...]).astype(BF)
    for p in range(3):
        grad_maps[p] = grads[p * RANK : (p + 1) * RANK]
    grad_maps[3] = t_mm(duo[...], ob_ref[...]).astype(BF)[:RANK]
    for p in range(3):
        grads = t_mm(ua_ref[...], dlin[:, pl.ds(p * width, width)]).astype(BF)[p * RANK : (p + 1) * RANK]
        if p < 2:
            grads = jnp.concatenate(
                [mm(grads[:, g * GROUP : (g + 1) * GROUP], order) for g in range(groups)], axis=1
            ).astype(BF)
        grad_maps[4 + p] = grads
    grad_maps[7] = t_mm(uo_ref[...], datt[...]).astype(BF)[:RANK]
    run("maps")

    def inner(block, carry):
        at = pl.ds(pl.multiple_of(block * 256, 256), 256)
        d, u = dlin[at, :], dua[at, :]
        dx = mm_t(d[:, : 2 * width], wqk[...]) + mm_t(d[:, 2 * width :], wqkv[:, pl.ds(2 * width, width)])
        dx = (dx + mm_t(u, down_ref[0])) * gain_a[...]
        h0 = tok[at, :].astype(F32)
        r = lax.rsqrt(jnp.mean(h0 * h0, axis=1, keepdims=True) + EPS)
        pull = r * dx - h0 * (r * r * r * jnp.mean(dx * h0, axis=1, keepdims=True))
        grad_tok[at, :] = (dh1_ref[at, :] + pull).astype(BF)
        if "half" in steps:
            pl.when(block == 1)(functools.partial(run, "half"))
        return carry

    lax.fori_loop(0, length // 256, inner, 0)
    run("end")


def attention_backward(
    spans, dh1, tok, gain_a, wqkv, wqk, wo, down_s, up_s, xa, q, k, v, ob, ua, uo, lse, maps=None, takers=None
):
    length, width = tok.shape
    cos, sin = rope_tables(length)
    vmem, smem = pl.BlockSpec(memory_space=pltpu.VMEM), pl.BlockSpec(memory_space=pltpu.SMEM)
    anys = pl.BlockSpec(memory_space=pl.ANY)
    args = (spans, dh1, tok, gain_a, wqkv, wqk, wo, down_s, up_s, cos, sin, xa, q, k, v, ob, ua, uo, lse)
    in_specs = [smem] + [vmem] * 18
    compact = ((8, RANK, width), BF)
    shapes, out_specs, scratch = [((length, width), BF)], [vmem], []
    if maps is None:
        shapes.append(compact)
        out_specs.append(vmem)
    else:
        share = maps.shape[2] // 8
        in_specs += [anys, vmem]
        args += (maps, takers)
        shapes += [((8, 128, share), BF), ((8, 128, width), BF)]
        out_specs += [anys] * 2
        scratch.append(compact)
    scratch += [
        ((length // HALF, HALF, HALF), F32),
        ((length, width), BF),
        ((length, width), BF),
        ((length, 128), BF),
        ((128, length), F32),
        ((128, length), F32),
        ((length, width), F32),
        ((length, width), F32),
        ((length, width), F32),
        ((length, 3 * width), BF),
        ((length, 128), BF),
    ]
    params = dict(vmem_limit_bytes=62 * MIB)
    semaphores = []
    if maps is not None:
        scratch += [
            (maps.shape, BF),
            ((8, 4, RANK, share), BF),
            ((128, share), BF),
            ((8, RANK, width), BF),
            ((128, width), BF),
            ((4, 32, width), BF),
            ((32, width), BF),
        ]
        semaphores = [pltpu.SemaphoreType.DMA((48,)), pltpu.SemaphoreType.DMA((48,)), pltpu.SemaphoreType.DMA((3,))]
        params.update(collective_id=1, has_side_effects=True)
    return pl.pallas_call(
        functools.partial(attention_backward_kernel, maps is not None),
        out_shape=[jax.ShapeDtypeStruct(s, t) for s, t in shapes],
        in_specs=in_specs,
        out_specs=out_specs,
        scratch_shapes=[pltpu.VMEM(s, t) for s, t in scratch] + semaphores,
        compiler_params=pltpu.CompilerParams(**params),
        name="attention_backward",
    )(*args)


def unpack_kernel(all_e, all_a, a_attention, b_qkv, b_out, a_gate_up, b_gate_up, a_down, b_down):
    width, hidden, share = b_out.shape[1], a_down.shape[1], all_e.shape[2]
    for p in range(4):
        a_attention[p] = all_a[p].astype(F32).T
    for p in range(3):
        b_qkv[p] = all_a[4 + p].astype(F32)
    b_out[...] = all_a[7].astype(F32)

    def pieces(start, number):
        at = start
        while at < start + number:
            stop = min(start + number, (at // share + 1) * share)
            part = all_e[at // share, :, at % share : at % share + stop - at]
            yield at - start, part.astype(F32)
            at = stop

    for p in range(2):
        for at, part in pieces(p * width, width):
            a_gate_up[0, p, pl.ds(at, part.shape[1]), :] = part.T
        for at, part in pieces(2 * width + p * hidden, hidden):
            b_gate_up[0, p, :, pl.ds(at, part.shape[1])] = part
    for at, part in pieces(2 * width + 2 * hidden, hidden):
        a_down[0, pl.ds(at, part.shape[1]), :] = part.T
    for at, part in pieces(2 * width + 3 * hidden, width):
        b_down[0, :, pl.ds(at, part.shape[1])] = part


def unpack(all_e, all_a, hidden):
    width = all_a.shape[2]
    shapes = [
        (4, width, 128), (3, 128, width), (128, width),
        (1, 2, width, 128), (1, 2, 128, hidden), (1, hidden, 128), (1, 128, width),
    ]
    return pl.pallas_call(
        unpack_kernel,
        out_shape=[jax.ShapeDtypeStruct(s, F32) for s in shapes],
        in_specs=[pl.BlockSpec(memory_space=pltpu.VMEM)] * 2,
        out_specs=[pl.BlockSpec(memory_space=pltpu.VMEM)] * 7,
        compiler_params=pltpu.CompilerParams(vmem_limit_bytes=40 * MIB),
        name="unpack",
    )(all_e, all_a)


def split(x):
    high = x.astype(BF)
    return high, (x - high.astype(F32)).astype(BF)


def experts_kernel(
    xb, h1_ref, lin_ref, cot, routes, carried, gain_m, wr, vectors,
    w_gate, w_up, w_down, maps,
    result, dh1_ref, grads,
    count, gates, gates_t, place, place_t, both, x_s, c_s, dy_s, g_s, y_acc, dx_acc, ug_s, ud_acc, dud_s, dug_acc,
    a_gu, b_dn, acc,
):
    e, j = pl.program_id(0), pl.program_id(1)
    experts, tiles = pl.num_programs(0), pl.num_programs(1)
    length, width = xb.shape
    kinds = carried.shape[1]
    numbers = kinds - 4
    tile = w_gate.shape[2]
    hidden = (maps.shape[2] - 3 * width) // 3
    rows_of = 128

    def padded_rows(start, number, before=0):
        part = maps[0, :, pl.ds(start, number)]
        parts = [jnp.zeros((before, number), BF), part, jnp.zeros((128 - RANK - before, number), BF)]
        return jnp.concatenate(parts if before else parts[1:], axis=0)

    @pl.when((e == 0) & (j == 0))
    def _():
        lane = iota((1, kinds), 1)
        logits = lin_ref[:, :kinds] + carried[...]
        picks = [lane == routes[:, k : k + 1] for k in range(2)]
        chosen = [jnp.sum(jnp.where(p, logits, 0.0), axis=1, keepdims=True) for p in picks]
        top = jnp.maximum(*chosen)
        parts = [jnp.exp(c - top) for c in chosen]
        total = parts[0] + parts[1]
        gates[...] = jnp.zeros(gates.shape, F32)
        gates[:, :kinds] = jnp.where(picks[0], parts[0] / total, jnp.where(picks[1], parts[1] / total, 0.0))
        wide = iota((1, 128), 1)
        named = [(wide == routes[:, k : k + 1]) & (wide < numbers) for k in range(2)]
        member = one_hot(named[0] | named[1])
        for block in range(length // 256):
            before = one_hot(iota((256, length), 1) < iota((256, length), 0) + block * 256)
            place[pl.ds(block * 256, 256), :] = mm(before, member)
        counts = jnp.sum(member.astype(F32), axis=0, keepdims=True)
        padded = jnp.floor((counts + (rows_of - 1)) * (1.0 / rows_of))
        earlier = one_hot(iota((128, 128), 0) < iota((128, 128), 1))
        starts = rows_of * mm(jnp.broadcast_to(padded, (8, 128)).astype(BF), earlier)[:1]
        own = jnp.where(named[0] | named[1], place[...], -1.0)
        place_t[...] = own.T
        gates_t[...] = gates[...].T
        spots = [
            jnp.sum(jnp.where(n, place[...] + starts + 1.0, 0.0), axis=1, keepdims=True) - 1.0 for n in named
        ]
        place[...] = jnp.where(wide == 0, spots[0], spots[1])
        for i in range(numbers):
            mine = wide == i
            count[0, i] = jnp.sum(jnp.where(mine, padded, 0.0)).astype(jnp.int32)
            count[1, i] = jnp.sum(jnp.where(mine, starts, 0.0)).astype(jnp.int32)
        count[1, numbers] = jnp.sum(jnp.where(wide < numbers, padded, 0.0)).astype(jnp.int32) * rows_of

    blocks = count[0, e]
    first = pl.multiple_of(count[1, e], rows_of)

    @pl.when((j == 0) & (blocks > 0))
    def _():
        a_gu[...] = padded_rows(0, width) + padded_rows(width, width, RANK)
        b_dn[...] = padded_rows(2 * width + 3 * hidden, width)

    @pl.when((j == 0) & (blocks == 0))
    def _():
        grads[...] = jnp.zeros(grads.shape, BF)

    if grads.shape[2] > maps.shape[2]:
        grads[0, :, maps.shape[2] :] = jnp.zeros((RANK, grads.shape[2] - maps.shape[2]), BF)

    def work(n):
        rows = pl.ds(0, n)

        @pl.when(j == 0)
        def _():
            own = iota((n, length), 0).astype(F32) == place_t[pl.ds(e, 1), :]
            taken = one_hot(own)
            x = mm(taken, xb[...]).astype(BF)
            c = mm(taken, cot[...]).astype(BF)
            g = jnp.sum(jnp.where(own, gates_t[pl.ds(e, 1), :], 0.0), axis=1, keepdims=True)
            dy = (g * c.astype(F32)).astype(BF)
            x_s[rows, :] = x
            c_s[rows, :] = c
            dy_s[rows, :] = dy
            g_s[rows, :] = jnp.broadcast_to(g, (n, 128))
            ug_s[rows, :] = mm_t(x, a_gu[...]).astype(BF)
            dud_s[rows, :] = mm_t(dy, b_dn[...]).astype(BF)

        x, dy, ug, dud = x_s[rows, :], dy_s[rows, :], ug_s[rows, :], dud_s[rows, :]
        at = pl.multiple_of(j * tile, tile)
        b_gate = padded_rows(2 * width + at, tile)
        b_up = padded_rows(2 * width + hidden + at, tile, RANK)
        a_dn = padded_rows(2 * width + 2 * hidden + at, tile)
        gate = mm(x, w_gate[0]) + mm(ug, b_gate)
        up = mm(x, w_up[0]) + mm(ug, b_up)
        sig = 1.0 / (1.0 + jnp.exp(-gate))
        act = gate * sig
        hid = (act * up).astype(BF)
        dhid = mm_t(dy, w_down[0]) + mm(dud, a_dn)
        dup = (dhid * act).astype(BF)
        dgate = (dhid * up * (sig + act * (1.0 - sig))).astype(BF)
        y = mm(hid, w_down[0])
        ud = mm_t(hid, a_dn)
        dx = mm_t(dgate, w_gate[0]) + mm_t(dup, w_up[0])
        dug = mm_t(dgate, b_gate) + mm_t(dup, b_up)
        ug_t = ug.T
        grads[0, :, pl.ds(2 * width + at, tile)] = mm(ug_t[:RANK], dgate).astype(BF)
        grads[0, :, pl.ds(2 * width + hidden + at, tile)] = mm(ug_t[RANK : 2 * RANK], dup).astype(BF)
        grads[0, :, pl.ds(2 * width + 2 * hidden + at, tile)] = mm(dud.T[:RANK], hid).astype(BF)

        @pl.when(j == 0)
        def _():
            y_acc[rows, :] = y
            dx_acc[rows, :] = dx
            ud_acc[rows, :] = ud
            dug_acc[rows, :] = dug

        @pl.when(j > 0)
        def _():
            y_acc[rows, :] += y
            dx_acc[rows, :] += dx
            ud_acc[rows, :] += ud
            dug_acc[rows, :] += dug

        @pl.when(j == tiles - 1)
        def _():
            ud = ud_acc[rows, :].astype(BF)
            dug = dug_acc[rows, :].astype(BF)
            y = y_acc[rows, :] + mm(ud, b_dn[...])
            g = g_s[rows, :][:, :1]
            dg = jnp.sum(c_s[rows, :].astype(F32) * y.astype(BF).astype(F32), axis=1, keepdims=True)
            high, low = split(dg)
            lane = iota((1, 128), 1)
            to = pl.ds(first, n)
            both[to, :width] = (g * y).astype(BF)
            both[to, width : 2 * width] = (dx_acc[rows, :] + mm(dug, a_gu[...])).astype(BF)
            both[to, 2 * width :] = jnp.where(
                lane == e, high.astype(F32), jnp.where(lane == e + 64, low.astype(F32), 0.0)
            ).astype(BF)
            x, dy = x_s[rows, :], dy_s[rows, :]
            to_a = mm(dug.T[: 2 * RANK], x).astype(BF)
            grads[0, :, :width] = to_a[:RANK]
            grads[0, :, width : 2 * width] = to_a[RANK:]
            grads[0, :, 2 * width + 3 * hidden : 3 * width + 3 * hidden] = mm(ud.T[:RANK], dy).astype(BF)

    for number in range(1, 512 // rows_of + 1):
        pl.when(blocks == number)(functools.partial(work, number * rows_of))

    @pl.when((e == experts - 1) & (j == tiles - 1))
    def _():
        used = count[1, numbers]
        both[pl.ds(pl.multiple_of(used, rows_of), HALF), :] = jnp.zeros((HALF, both.shape[1]), BF)
        lane = iota((1, 128), 1)

        def combine(block, carry):
            at = pl.ds(pl.multiple_of(block * 256, 256), 256)
            acc[...] = jnp.zeros(acc.shape, F32)
            spots = place[at, :]

            def add(part, carry):
                k0 = pl.multiple_of(part * HALF, HALF)
                slot = (iota((256, HALF), 1) + k0).astype(F32)
                taken = one_hot((slot == spots[:, :1]) | (slot == spots[:, 1:2]))
                acc[...] += mm(taken, both[pl.ds(k0, HALF), :])
                return carry

            lax.fori_loop(0, (used + HALF - 1) // HALF, add, 0)
            h1 = h1_ref[at, :]
            ct = cot[at, :].astype(F32)
            r = lax.rsqrt(jnp.mean(h1 * h1, axis=1, keepdims=True) + EPS)
            gain = gain_m[...]
            n2 = h1 * r * gain
            lin = lin_ref[at, :]
            g = gates[at, :]
            gc = g[:, numbers + 1 : numbers + 2]
            g_fix = [g[:, numbers + 2 + i : numbers + 3 + i] for i in range(2)]
            mixes = []
            for i in range(2):
                a, b = lin[:, kinds + 2 * i : kinds + 2 * i + 1], lin[:, kinds + 2 * i + 1 : kinds + 2 * i + 2]
                top = jnp.maximum(a, b)
                a, b = jnp.exp(a - top), jnp.exp(b - top)
                mixes.append((a / (a + b), b / (a + b)))
            vecs = [vectors[i : i + 1, :] for i in range(2)]
            to_n2 = gc + g_fix[0] * mixes[0][0] + g_fix[1] * mixes[1][0]
            out = h1 + acc[:, :width] + to_n2 * n2
            out = out + (g_fix[0] * mixes[0][1]) * vecs[0] + (g_fix[1] * mixes[1][1]) * vecs[1]
            result[at, :] = out.astype(BF)
            a = jnp.sum(ct * n2, axis=1, keepdims=True)
            bs = [jnp.sum(ct * v, axis=1, keepdims=True) for v in vecs]
            packed = acc[:, 2 * width :]
            dg = jnp.where(lane < numbers, packed + pltpu.roll(packed, 64, 1), 0.0)
            dg = jnp.where(lane == numbers + 1, a, dg)
            for i in range(2):
                dg = jnp.where(lane == numbers + 2 + i, mixes[i][0] * a + mixes[i][1] * bs[i], dg)
            dlin = g * (dg - jnp.sum(g * dg, axis=1, keepdims=True))
            for i in range(2):
                pull = mixes[i][0] * mixes[i][1] * (g_fix[i] * (a - bs[i]))
                dlin = jnp.where(lane == kinds + 2 * i, pull, jnp.where(lane == kinds + 2 * i + 1, -pull, dlin))
            high, low = split(dlin)
            dn2 = acc[:, width : 2 * width] + (mm_t(high, wr[...]) + mm_t(low, wr[...])) + ct * to_n2
            dn2 = dn2 * gain
            back = r * dn2 - h1 * (r * r * r * jnp.mean(dn2 * h1, axis=1, keepdims=True))
            dh1_ref[at, :] = ct + back
            return carry

        lax.fori_loop(0, length // 256, combine, 0)


def experts_both_ways(xb, h1, lin, cot, routes, carried, gain_m, wr, vectors, w_gu, w_dn, maps, copies):
    length, width = xb.shape
    experts, hidden = w_dn.shape[0], w_dn.shape[1]
    tile = hidden // 2
    tiles = hidden // tile
    most = 2 * length + experts * 128
    total = 3 * width + 3 * hidden
    padded = -(-total // (copies * 128)) * copies * 128

    def whole(a):
        return pl.BlockSpec(a.shape, lambda e, j: (0,) * a.ndim, pipeline_mode=pl.Buffered(1))

    resident = (xb, h1, lin, cot, routes, carried, gain_m, wr, vectors)
    return pl.pallas_call(
        experts_kernel,
        grid=(experts, tiles),
        out_shape=[
            jax.ShapeDtypeStruct((length, width), BF),
            jax.ShapeDtypeStruct((length, width), F32),
            jax.ShapeDtypeStruct((experts, RANK, padded), BF),
        ],
        in_specs=[whole(a) for a in resident]
        + [
            pl.BlockSpec((1, width, tile), lambda e, j: (e, 0, j)),
            pl.BlockSpec((1, width, tile), lambda e, j: (e, 0, tiles + j)),
            pl.BlockSpec((1, tile, width), lambda e, j: (e, j, 0)),
            pl.BlockSpec((1, RANK, total), lambda e, j: (e, 0, 0)),
        ],
        out_specs=[
            pl.BlockSpec((length, width), lambda e, j: (0, 0), pipeline_mode=pl.Buffered(1)),
            pl.BlockSpec((length, width), lambda e, j: (0, 0), pipeline_mode=pl.Buffered(1)),
            pl.BlockSpec((1, RANK, padded), lambda e, j: (e, 0, 0)),
        ],
        scratch_shapes=[
            pltpu.SMEM((2, experts + 1), jnp.int32),
            pltpu.VMEM((length, 128), F32),
            pltpu.VMEM((128, length), F32),
            pltpu.VMEM((length, 128), F32),
            pltpu.VMEM((128, length), F32),
            pltpu.VMEM((most + HALF, 2 * width + 128), BF),
            pltpu.VMEM((512, width), BF),
            pltpu.VMEM((512, width), BF),
            pltpu.VMEM((512, width), BF),
            pltpu.VMEM((512, 128), F32),
            pltpu.VMEM((512, width), F32),
            pltpu.VMEM((512, width), F32),
            pltpu.VMEM((512, 128), BF),
            pltpu.VMEM((512, 128), F32),
            pltpu.VMEM((512, 128), BF),
            pltpu.VMEM((512, 128), F32),
            pltpu.VMEM((128, width), BF),
            pltpu.VMEM((128, width), BF),
            pltpu.VMEM((256, 2 * width + 128), F32),
        ],
        compiler_params=pltpu.CompilerParams(vmem_limit_bytes=60 * MIB),
        name="experts_both_ways",
    )(*resident, w_gu, w_gu, w_dn, maps)


def gather_experts(weights, senders):
    w_gu, w_dn, gu_down, gu_up, dn_down, dn_up = weights
    maps = jnp.concatenate(
        [gu_down[0, 0].T, gu_down[0, 1].T, gu_up[0, 0], gu_up[0, 1], dn_down[0].T, dn_up[0]], axis=1
    )
    to = (senders[:, None] * RANK + jnp.arange(RANK)[None, :]).reshape(-1)
    rows = mm((to[:, None] == jnp.arange(128)[None, :]).astype(BF), maps).astype(BF)
    rows = rows.reshape(senders.shape[0], RANK, -1)
    return (
        lax.all_gather(w_gu, "expert", axis=0, tiled=True),
        lax.all_gather(w_dn, "expert", axis=0, tiled=True),
        lax.all_to_all(rows, "expert", split_axis=0, concat_axis=0, tiled=True),
    )


BOTH = ("dp", "expert")


def sum_expert_maps(compact, spread):
    copies = lax.axis_size("dp")
    experts, rank, columns = compact.shape
    each = columns // copies
    parts = compact.reshape(experts, rank, copies, each).transpose(2, 0, 1, 3).reshape(copies * experts, rank, each)
    got = lax.all_to_all(parts, BOTH, split_axis=0, concat_axis=0, tiled=True)
    own = mm(spread, got.reshape(-1, each)).astype(BF)
    return lax.all_gather(own, "dp", axis=1, tiled=True)


def sum_attention_maps(compact, spread):
    devices = lax.axis_size("dp") * lax.axis_size("expert")
    maps, rank, width = compact.shape
    cuts = devices // maps
    parts = compact.reshape(maps, rank, cuts, width // cuts).transpose(0, 2, 1, 3).reshape(devices, rank, width // cuts)
    got = lax.all_to_all(parts, BOTH, split_axis=0, concat_axis=0, tiled=True)
    own = mm(spread, got.reshape(devices * rank, width // cuts)).astype(BF)
    whole = lax.all_gather(own[None], BOTH, axis=0, tiled=True)
    return whole.reshape(maps, cuts, 128, width // cuts).transpose(0, 2, 1, 3).reshape(maps, 128, width).astype(F32)


def body(
    exchange,
    tokens, cotangent, attention_norm_gain, query_key_value_weight, attention_output_weight,
    adapter_attention_down_maps, adapter_query_key_value_up_maps, adapter_output_up_map,
    experts_norm_gain, router_weight, constant_expert_mixing, constant_expert_vectors,
    expert_gate_up_weight, expert_down_weight, adapter_expert_gate_up_down_maps, adapter_expert_gate_up_up_maps,
    adapter_expert_down_down_maps, adapter_expert_down_up_maps,
    routes, router_logits_carried, picture_span_starts, sequence_adapter_index,
):
    groups = lax.axis_size("expert")
    width = tokens.shape[1]
    hidden = expert_down_weight.shape[1]
    first = lax.axis_index("dp") * groups
    senders = lax.dynamic_slice_in_dim(sequence_adapter_index, first, groups, 0)
    adapter = lax.dynamic_slice_in_dim(senders, lax.axis_index("expert"), 1, 0)
    gain_a, gain_m = attention_norm_gain[None], experts_norm_gain[None]
    spans = picture_span_starts.reshape(-1)
    router = jnp.concatenate([router_weight, constant_expert_mixing], axis=1)
    router = jnp.pad(router, ((0, 0), (0, 128 - router.shape[1])))
    own = (
        expert_gate_up_weight, expert_down_weight, adapter_expert_gate_up_down_maps,
        adapter_expert_gate_up_up_maps, adapter_expert_down_down_maps, adapter_expert_down_up_maps,
    )
    outs = attention_forward(
        tokens, gain_a, query_key_value_weight, adapter_attention_down_maps, adapter_query_key_value_up_maps,
        attention_output_weight, adapter_output_up_map, gain_m, router, spans, adapter,
        *((own, senders) if exchange else ()),
    )
    xa, q, k, v, ob, ua, uo, lse, h1, xb, lin, wqk, down_s, up_s = outs[:14]
    weights = outs[14:] if exchange else gather_experts(own, senders)
    result, dh1, expert_maps = experts_both_ways(
        xb, h1, lin, cotangent, routes, router_logits_carried, gain_m, router, constant_expert_vectors, *weights,
        lax.axis_size("dp"),
    )
    backward = functools.partial(
        attention_backward, spans, dh1, tokens, gain_a, query_key_value_weight, wqk, attention_output_weight, down_s, up_s,
        xa, q, k, v, ob, ua, uo, lse,
    )
    if exchange:
        takers = jnp.repeat(sequence_adapter_index, RANK)[None]
        grad_tokens, all_e, all_a = backward(expert_maps, takers)
        return (result, grad_tokens, *unpack(all_e, all_a, hidden))
    grad_tokens, attention_maps = backward()
    to = (sequence_adapter_index[:, None] * RANK + jnp.arange(RANK)[None, :]).reshape(-1)
    spread = (jnp.arange(128)[:, None] == to[None, :]).astype(BF)
    of_expert = sum_expert_maps(expert_maps, spread).astype(F32)
    of_attention = sum_attention_maps(attention_maps, spread)
    ends = [0, width, 2 * width, 2 * width + hidden, 2 * width + 2 * hidden, 2 * width + 3 * hidden, 3 * width + 3 * hidden]
    gud0, gud1, guu0, guu1, dnd, dnu = (of_expert[:, a:b] for a, b in zip(ends, ends[1:]))
    return (
        result,
        grad_tokens,
        of_attention[:4].transpose(0, 2, 1),
        of_attention[4:7],
        of_attention[7],
        jnp.stack([gud0.T, gud1.T])[None],
        jnp.stack([guu0, guu1])[None],
        dnd.T[None],
        dnu[None],
    )


def solution(mesh):
    tokens, own = P(("dp", "expert"), None), P("expert", None, None)
    own4 = P("expert", None, None, None)
    in_specs = (tokens, tokens) + (P(),) * 10 + (own, own, own4, own4, own, own) + (tokens,) * 3 + (P(),)
    out_specs = (tokens, tokens, P(), P(), P(), own4, own4, own, own)
    exchange = dict(mesh.shape) == {"dp": 8, "expert": 4}
    return jax.shard_map(functools.partial(body, exchange), mesh=mesh, in_specs=in_specs, out_specs=out_specs, check_vma=False)
```

```python
import functools

import jax
import jax.numpy as jnp
import numpy as np
from jax import lax
from jax.experimental import pallas as pl
from jax.experimental.pallas import tpu as pltpu
from jax.sharding import PartitionSpec as P

HEADS = 12
HD = 64
RANK = 16
PIC = 256
GROUP = 256
HALF = 512
EPS = 1e-06
NEG = -1e30
BF = jnp.bfloat16
F32 = jnp.float32
MIB = 1024 * 1024


def mm(a, b):
    return jnp.dot(a, b, preferred_element_type=F32)


def mm_t(a, b):
    return lax.dot_general(a, b, (((1,), (1,)), ((), ())), preferred_element_type=F32)


def t_mm(a, b):
    return lax.dot_general(a, b, (((0,), (0,)), ((), ())), preferred_element_type=F32)


def iota(shape, dim):
    return lax.broadcasted_iota(jnp.int32, shape, dim)


def one_hot(condition):
    return jnp.where(condition, 1.0, 0.0).astype(BF)


def picker(adapter, place, rows=128, columns=128):
    row, column = iota((rows, columns), 0), iota((rows, columns), 1)
    return one_hot((row - adapter * RANK == column - place * RANK) & (column // RANK == place))


def placer(adapter, place, rows=128, columns=128):
    row, column = iota((rows, columns), 0), iota((rows, columns), 1)
    return one_hot((column - adapter * RANK == row - place * RANK) & (row // RANK == place))


def head_order(back):
    row, column = iota((GROUP, GROUP), 0), iota((GROUP, GROUP), 1)
    a, b = (column, row) if back else (row, column)
    return one_hot(a == (b % 128 // 32) * 64 + b // 128 * 32 + b % 32)


def rope_tables(length):
    spacing = 10000.0 ** (-np.arange(0, HD, 2, dtype=np.float32) / np.float32(HD))
    angles = np.arange(length, dtype=np.float32)[:, None] * spacing.astype(np.float32)[None, :]
    angles = np.tile(angles, (1, 4))
    return np.cos(angles).astype(np.float32), np.sin(angles).astype(np.float32)


def rope(pair, cosine, sine):
    low, high = pair[:, :128], pair[:, 128:]
    return jnp.concatenate([low * cosine - high * sine, high * cosine + low * sine], axis=1)


def span_bias(start, transposed):
    a, b = iota((HALF, HALF), 0), iota((HALF, HALF), 1)
    query, key = (b, a) if transposed else (a, b)
    inside = (query >= start) & (query < start + PIC) & (key >= start) & (key < start + PIC)
    return jnp.where((key <= query) | inside, 0.0, NEG)


UNITS = 32
CHUNKS = ((0, 1), (1, 2), (3, 1), (4, 2))
EXTRA = ((0, 2), (2, 2))
MESH = pl.DeviceIdType.MESH


def other(index, step):
    return index + step - 2 * step * ((index // step) % 2)


def sending_steps(own, outs, scratch):
    adapters, w_gu, w_dn, gu_down, gu_up, dn_down, dn_up = own
    all_gu, all_dn, all_maps = outs
    bounce_gu, bounce_dn, compact, send, recv, local = scratch
    sources, targets, bounce = (w_gu, w_dn), (all_gu, all_dn), (bounce_gu, bounce_dn)
    dp, ex = lax.axis_index("dp"), lax.axis_index("expert")
    sibling, far = other(ex, 1), other(ex, 2)
    peers = {
        "x": (other(dp, 1), ex), "z": (other(dp, 2), ex), "y": (dp, far), "s": (dp, sibling), "d": (dp, other(far, 1)),
    }
    x, z = dp % 2, (dp // 2) % 2
    quarter = {"y": z * 2 + x, "x": z * 2 + 1 - x, "z": (1 - z) * 2 + x, "d": (1 - z) * 2 + 1 - x}
    kind = (x + z) % 2
    slots = {}
    for name in ("y", "x", "z", "d"):
        for chunk in CHUNKS:
            slots[name, chunk] = len(slots)
    for name in ("e", "o"):
        for chunk in EXTRA:
            slots[name, chunk] = len(slots)
    count = len(slots)
    started = []

    def views(refs, expert, key):
        name, (first, number) = key
        if name in quarter:
            first = quarter[name] * 6 + first
        else:
            first = 24 + 4 * (kind if name == "e" else 1 - kind) + first
        columns, rows = refs[0].shape[-1] // UNITS, refs[1].shape[-2] // UNITS
        return (
            refs[0].at[expert, :, pl.ds(pl.multiple_of(first * columns, columns), number * columns)],
            refs[1].at[expert, pl.ds(pl.multiple_of(first * rows, rows), number * rows), :],
        )

    def copies(source, target, peer, slot):
        for i in range(len(source())):
            number = len(started)

            def made(i=i, number=number):
                return pltpu.make_async_remote_copy(
                    src_ref=source()[i], dst_ref=target()[i], send_sem=send.at[number], recv_sem=recv.at[slot, i],
                    device_id=peers[peer], device_id_type=MESH,
                )

            made().start()
            started.append(made)

    def arrived(view, slot, i):
        pltpu.make_async_remote_copy(
            src_ref=view, dst_ref=view, send_sem=send.at[0], recv_sem=recv.at[slot, i],
            device_id=peers["s"], device_id_type=MESH,
        ).wait_recv()

    def begin():
        barrier = pltpu.get_barrier_semaphore()
        for peer in peers.values():
            pl.semaphore_signal(barrier, inc=1, device_id=peer, device_id_type=MESH)
        pl.semaphore_wait(barrier, len(peers))
        for name, chunks in (("y", CHUNKS), ("e", EXTRA)):
            for chunk in chunks:
                key = name, chunk
                copies(
                    functools.partial(views, sources, 0, key), functools.partial(views, targets, ex, key), "y", slots[key]
                )
        copies(lambda: [s.at[0] for s in sources], lambda: [t.at[ex] for t in targets], "s", 2 * count)
        for i in range(2):
            pltpu.make_async_copy(sources[i].at[0], bounce[i], local.at[i]).start()

    def select():
        row, column = iota((64, 128), 0), iota((64, 128), 1)
        first = sum(jnp.where(row // RANK == i, adapters[dp * 4 + i], 0) for i in range(4))
        rows = one_hot(column == first * RANK + row % RANK)
        width, hidden = gu_down.shape[2], dn_down.shape[1]
        parts = [
            (0, mm_t(rows, gu_down[0, 0])),
            (width, mm_t(rows, gu_down[0, 1])),
            (2 * width, mm(rows, gu_up[0, 0])),
            (2 * width + hidden, mm(rows, gu_up[0, 1])),
            (2 * width + 2 * hidden, mm_t(rows, dn_down[0])),
            (2 * width + 3 * hidden, mm(rows, dn_up[0])),
        ]
        for at, part in parts:
            for i in range(4):
                compact[i, :, pl.ds(at, part.shape[1])] = part[i * RANK : (i + 1) * RANK].astype(BF)
        for i, (peer, to) in enumerate((("s", sibling), ("y", far), ("d", other(far, 1)))):
            copies(lambda to=to: [compact.at[to]], lambda: [all_maps.at[ex]], peer, 2 * count + 1 + i)
        pltpu.make_async_copy(compact.at[ex], all_maps.at[ex], local.at[2]).start()

    def turn():
        for i in range(2):
            pltpu.make_async_copy(sources[i].at[0], bounce[i], local.at[i]).wait()
            pltpu.make_async_copy(bounce[i], targets[i].at[ex], local.at[i]).start()

    along_x = (CHUNKS[0], CHUNKS[3])

    def got(name, chunk):
        key = name, chunk
        to = []
        if name == "y":
            to = [("x", slots["x", chunk]), ("z", slots["z", chunk])]
        if name == "x" and chunk not in along_x:
            to = [("z", slots["d", chunk])]
        if name == "z" and chunk in along_x:
            to = [("x", slots["d", chunk])]
        if name == "e":
            to = [("x" if chunk == EXTRA[0] else "z", slots["o", chunk])]

        def step():
            mine = functools.partial(views, targets, far, key)
            for i in range(2):
                arrived(mine()[i], slots[key], i)
            for peer, slot in to:
                copies(mine, mine, peer, slot)
            copies(mine, mine, "s", count + slots[key])

        return step

    def end():
        for made in started:
            made().wait_send()
        for i in range(2):
            pltpu.make_async_copy(bounce[i], targets[i].at[ex], local.at[i]).wait()
            arrived(targets[i].at[sibling], 2 * count, i)
        pltpu.make_async_copy(compact.at[ex], all_maps.at[ex], local.at[2]).wait()
        for i, source in enumerate((sibling, far, other(far, 1))):
            arrived(all_maps.at[source], 2 * count + 1 + i, 0)
        for key, slot in slots.items():
            view = views(targets, other(far, 1), key)
            for i in range(2):
                arrived(view[i], count + slot, i)

    c, e = CHUNKS, EXTRA
    return {
        "begin": [begin],
        "loaded": [select],
        "ready": [turn, got("y", c[0])],
        "projected": [got("x", c[0]), got("z", c[0]), got("y", c[1])],
        3: [got("y", c[2])],
        6: [got("z", c[1]), got("x", c[1])],
        8: [got("y", c[3]), got("d", c[0])],
        10: [got("x", c[2]), got("z", c[2])],
        "finished": [got("z", c[3]), got("e", e[0])],
        200: [got("x", c[3])],
        201: [got("e", e[1])],
        202: [got("d", c[1])],
        203: [got("d", c[2])],
        "end": [got("o", e[0]), got("d", c[3]), got("o", e[1]), end],
    }


def attention_forward_kernel(exchange, *refs):
    spans, adapters, tok, gain_a, wqkv, down, up, wo, up_out, gain_m, router, mixing, cos, sin = refs[:14]
    refs = refs[14:]
    own = ()
    if exchange:
        own, refs = (adapters, *refs[:9]), refs[9:]
    xa_ref, q_ref, k_ref, v_ref, ob_ref, ua_ref, uo_ref, lse_ref, h1_ref, xb_ref, lin_ref, wqk_ref, down_ref, up_s, wr = refs[:15]
    refs = refs[15:]
    steps = {}
    if exchange:
        cot, routes, carried = own[-3:]
        own_outs, semaphores = refs[:3], refs[6:12]
        own_both, own_grads, bias = refs[3:6]
        bounce_gu, bounce_dn, compact = refs[6:9]
        info_t, place_t, x_s, c_s, dy_s, y_acc, ud_acc, dx_acc, dug_acc = refs[12:21]
        held, refs = refs[21:], ()
        loads = (tok, down, up, up_out, *own[3:7], wqkv, cos, sin, wo, cot)
        load = Staged(list(zip(loads, held)), held[-2])
        tok, down, up, up_out, *maps, wqkv, cos, sin, wo, cot = held[: len(loads)]
        outs = (xa_ref, q_ref, k_ref, v_ref, ob_ref, ua_ref, uo_ref, lse_ref, h1_ref, xb_ref, lin_ref, wqk_ref, down_ref, up_s, wr)
        kept_outs = held[len(loads) : len(loads) + len(outs)]
        store = Staged(list(zip(kept_outs, outs)), held[-1])
        xa_ref, q_ref, k_ref, v_ref, ob_ref, ua_ref, uo_ref, lse_ref, h1_ref, xb_ref, lin_ref, wqk_ref, down_ref, up_s, wr = kept_outs
        steps = sending_steps((*own[:3], *maps), own_outs, semaphores)
    else:
        (bias,) = refs
    length, width = tok.shape
    groups = width // GROUP
    adapter = adapters[lax.axis_index("dp") * lax.axis_size("expert") + lax.axis_index("expert")]

    def run(point):
        for step in steps.get(point, ()):
            step()

    run("begin")
    if exchange:
        load.start()
        load.wait()
        run("loaded")
    order = head_order(False)
    down_s = sum(mm(down[p], picker(adapter, p)) for p in range(3)).astype(BF)
    down_o = mm(down[3], picker(adapter, 0)).astype(BF)
    up_o = mm(placer(adapter, 0), up_out[...]).astype(BF)
    row, column = iota((128, router.shape[0]), 0), iota((128, router.shape[0]), 1)
    wr[...] = mm(one_hot(row == column), router[...]).astype(BF)
    row, column = iota((128, mixing.shape[0]), 0), iota((128, mixing.shape[0]), 1)
    wr[...] += mm(one_hot(row == column + router.shape[0]), mixing[...]).astype(BF)
    down_ref[0] = down_s
    down_ref[1] = down_o
    up_s[:, pl.ds(3 * width, width)] = up_o
    for p in range(3):
        rows = mm(placer(adapter, p), up[p]).astype(BF)
        for g in range(groups):
            block = rows[:, g * GROUP : (g + 1) * GROUP]
            if p < 2:
                block = mm(block, order).astype(BF)
            up_s[:, pl.ds(p * width + g * GROUP, GROUP)] = block
    for g in range(2 * groups):
        at = pl.ds(g * GROUP, GROUP)
        wqk_ref[:, at] = mm(wqkv[:, at], order).astype(BF)
    for half in range(length // HALF):
        bias[half] = span_bias(spans[half] - half * HALF, False)
    run("ready")

    def project(block, carry):
        at = pl.ds(pl.multiple_of(block * 256, 256), 256)
        h0 = tok[at, :].astype(F32)
        x = h0 * lax.rsqrt(jnp.mean(h0 * h0, axis=1, keepdims=True) + EPS) * gain_a[...][None]
        x = x.astype(BF)
        xa_ref[at, :] = x
        u = mm(x, down_s).astype(BF)
        ua_ref[at, :] = u
        c, s = cos[at, :], sin[at, :]
        for p, out in enumerate((q_ref, k_ref)):
            for g in range(groups):
                lanes = pl.ds(p * width + g * GROUP, GROUP)
                lin = mm(x, wqk_ref[:, lanes]) + mm(u, up_s[:, lanes])
                out[at, pl.ds(g * GROUP, GROUP)] = rope(lin, c, s).astype(BF)
        lanes = pl.ds(2 * width, width)
        v_ref[at, :] = (mm(x, wqkv[:, lanes]) + mm(u, up_s[:, lanes])).astype(BF)
        return carry

    lax.fori_loop(0, length // 256, project, 0)
    run("projected")

    lane = iota((1, GROUP), 1)
    lse_ref[...] = jnp.zeros(lse_ref.shape, F32)
    ob_f = ob_ref

    def attend(head, carry):
        g, h = head // 4, head % 4
        lanes = pl.ds(pl.multiple_of(g * GROUP, GROUP), GROUP)
        qk_own = jnp.where((lane % 128) // 32 == h, 1.0, 0.0).astype(BF)
        v_own = jnp.where(lane // 64 == h, 1.0, 0.0)
        kh = k_ref[:, lanes] * qk_own
        vh = v_ref[:, lanes] * v_own.astype(BF)
        for half in range(length // HALF):
            at = pl.ds(half * HALF, HALF)
            q = q_ref[at, lanes] * BF(0.125)
            keys = (half + 1) * HALF
            diag = mm_t(q, kh[half * HALF : keys]) + bias[half]
            top = jnp.max(diag, axis=1, keepdims=True)
            if half:
                past = mm_t(q, kh[: half * HALF])
                top = jnp.maximum(top, jnp.max(past, axis=1, keepdims=True))
            e = jnp.exp(diag - top)
            total = jnp.sum(e, axis=1, keepdims=True)
            o = mm(e.astype(BF), vh[half * HALF : keys])
            if half:
                e = jnp.exp(past - top)
                total = total + jnp.sum(e, axis=1, keepdims=True)
                o = o + mm(e.astype(BF), vh[: half * HALF])
            o = o * pl.reciprocal(total, approx=False)
            lse = top + jnp.log(total)
            lse_ref[at, :] = jnp.where(iota((1, 128), 1) == head, lse, lse_ref[at, :])
            old = jnp.where(v_own > 0.5, 0.0, ob_f[at, lanes].astype(F32))
            ob_f[at, lanes] = jnp.where(v_own > 0.5, o, old).astype(BF)
        for point in steps:
            if isinstance(point, int) and point < 100:
                pl.when(head == point)(functools.partial(run, point))
        return carry

    lax.fori_loop(0, HEADS, attend, 0)

    def finish(block, carry):
        at = pl.ds(pl.multiple_of(block * 256, 256), 256)
        o = ob_ref[at, :]
        u = mm(o, down_o).astype(BF)
        uo_ref[at, :] = u
        h1 = tok[at, :].astype(F32) + (mm(o, wo[...]) + mm(u, up_o))
        h1_ref[at, :] = h1
        x = h1 * lax.rsqrt(jnp.mean(h1 * h1, axis=1, keepdims=True) + EPS) * gain_m[...][None]
        x = x.astype(BF)
        xb_ref[at, :] = x
        lin_ref[at, :] = mm_t(x, wr[...])
        return carry

    lax.fori_loop(0, length // 256, finish, 0)
    if exchange:
        store.start()
        run("finished")
        ex = lax.axis_index("expert")
        hidden = bounce_dn.shape[0]
        own_grads[:, 3 * width + 3 * hidden :] = jnp.zeros((RANK, own_grads.shape[1] - 3 * width - 3 * hidden), BF)
        route(lin_ref, carried, routes, carried.shape[0] - 4, info_t, place_t)
        x, c, g, dy = take_rows(x_s.shape[0], place_t[pl.ds(ex, 1), :], info_t[pl.ds(ex, 1), :], xb_ref, cot)
        x_s[...], c_s[...], dy_s[...] = x, c, dy
        a_gu = padded_rows(compact[ex, :, :width]) + padded_rows(compact[ex, :, width : 2 * width], RANK)
        b_dn = padded_rows(compact[ex, :, 2 * width + 3 * hidden :])
        ug, dud = mm_t(x, a_gu).astype(BF), mm_t(dy, b_dn).astype(BF)
        kept = (y_acc, ud_acc, dx_acc, dug_acc)
        for ref in kept:
            ref[...] = jnp.zeros(ref.shape, F32)
        run(200)
        tile = 512

        def one_tile(j, carry):
            at = pl.multiple_of(j * tile, tile)
            starts = [2 * width + i * hidden + at for i in range(3)]
            sums, parts = hidden_tile(
                x_s[...], dy_s[...], ug, dud,
                bounce_gu[:, pl.ds(at, tile)], bounce_gu[:, pl.ds(hidden + at, tile)], bounce_dn[pl.ds(at, tile), :],
                padded_rows(compact[ex, :, pl.ds(starts[0], tile)]),
                padded_rows(compact[ex, :, pl.ds(starts[1], tile)], RANK),
                padded_rows(compact[ex, :, pl.ds(starts[2], tile)]),
            )
            for start, part in zip(starts, parts):
                own_grads[:, pl.ds(start, tile)] = part
            for ref, value in zip(kept, sums):
                ref[...] += value
            for point in steps:
                if isinstance(point, int) and point > 200:
                    pl.when(j == point - 201)(functools.partial(run, point))
            return carry

        lax.fori_loop(0, hidden // tile, one_tile, 0)
        out, parts = close_rows(ex, [ref[...] for ref in kept], x_s[...], c_s[...], g, dy_s[...], a_gu, b_dn)
        own_both[:, :width], own_both[:, width : 2 * width], own_both[:, 2 * width :] = out
        own_grads[:, :width], own_grads[:, width : 2 * width] = parts[:2]
        own_grads[:, 2 * width + 3 * hidden : 3 * width + 3 * hidden] = parts[2]
        store.wait()
    run("end")


def attention_forward(tok, gain_a, wqkv, down, up, wo, up_out, gain_m, router, mixing, spans, adapters, own=()):
    length, width = tok.shape
    cos, sin = rope_tables(length)
    shapes = [
        ((length, width), BF),
        ((length, width), BF),
        ((length, width), BF),
        ((length, width), BF),
        ((length, width), BF),
        ((length, 128), BF),
        ((length, 128), BF),
        ((length, 128), F32),
        ((length, width), F32),
        ((length, width), BF),
        ((length, 128), F32),
        ((width, 2 * width), BF),
        ((2, width, 128), BF),
        ((128, 4 * width), BF),
        ((128, width), BF),
    ]
    vmem, smem = pl.BlockSpec(memory_space=pltpu.VMEM), pl.BlockSpec(memory_space=pltpu.SMEM)
    anys = pl.BlockSpec(memory_space=pl.ANY)
    in_specs, out_specs = [smem, smem] + [vmem] * 12, [vmem] * len(shapes)
    scratch = [pltpu.VMEM((length // HALF, HALF, HALF), F32)]
    params = dict(vmem_limit_bytes=60 * MIB)
    args = (spans, adapters, tok, gain_a, wqkv, down, up, wo, up_out, gain_m, router, mixing, cos, sin)
    if own:
        w_gu, w_dn = own[:2]
        columns = 3 * width + 3 * w_dn.shape[1]
        in_specs = [smem, smem] + [vmem if i in (1, 7, 8, 9) else anys for i in range(12)]
        in_specs += [anys] * 7 + [vmem] * 2
        args += own
        held = [args[i] for i in (2, 5, 6, 8, 16, 17, 18, 19, 4, 12, 13, 7, 20)]
        held = [pltpu.VMEM(a.shape, a.dtype) for a in held] + [pltpu.VMEM(a, t) for a, t in shapes]
        padded = -(-columns // 1024) * 1024
        shapes += [
            ((4, *w_gu.shape[1:]), BF),
            ((4, *w_dn.shape[1:]), BF),
            ((4, RANK, columns), BF),
            ((HALF, 2 * width + 128), BF),
            ((RANK, padded), BF),
        ]
        out_specs = [anys] * (len(out_specs) + 3) + [vmem] * 2
        scratch += [
            pltpu.VMEM(w_gu.shape[1:], BF),
            pltpu.VMEM(w_dn.shape[1:], BF),
            pltpu.VMEM((4, RANK, columns), BF),
            pltpu.SemaphoreType.DMA((96,)),
            pltpu.SemaphoreType.DMA((48, 2)),
            pltpu.SemaphoreType.DMA((3,)),
            pltpu.VMEM((128, length), F32),
            pltpu.VMEM((128, length), F32),
            pltpu.VMEM((HALF, width), BF),
            pltpu.VMEM((HALF, width), BF),
            pltpu.VMEM((HALF, width), BF),
            pltpu.VMEM((HALF, width), F32),
            pltpu.VMEM((HALF, 128), F32),
            pltpu.VMEM((HALF, width), F32),
            pltpu.VMEM((HALF, 128), F32),
        ]
        scratch += held + [pltpu.SemaphoreType.DMA((16,)), pltpu.SemaphoreType.DMA((16,))]
        params.update(collective_id=0, has_side_effects=True)
    return pl.pallas_call(
        functools.partial(attention_forward_kernel, bool(own)),
        out_shape=[jax.ShapeDtypeStruct(s, t) for s, t in shapes],
        in_specs=in_specs,
        out_specs=out_specs,
        scratch_shapes=scratch,
        compiler_params=pltpu.CompilerParams(**params),
        name="attention_forward",
    )(*args)


class Staged:
    def __init__(self, pairs, sems):
        self.pairs, self.sems = pairs, sems

    def copy(self, i):
        return pltpu.make_async_copy(self.pairs[i][0], self.pairs[i][1], self.sems.at[i])

    def start(self, numbers=None):
        for i in range(len(self.pairs)) if numbers is None else numbers:
            self.copy(i).start()

    def wait(self, numbers=None):
        for i in range(len(self.pairs)) if numbers is None else numbers:
            self.copy(i).wait()


class Mail:
    def __init__(self, send, recv):
        self.send, self.recv, self.started = send, recv, []

    def post(self, source, target, peer, slot, when=None):
        number = len(self.started)

        def made():
            return pltpu.make_async_remote_copy(
                src_ref=source(), dst_ref=target(), send_sem=self.send.at[number],
                recv_sem=self.recv.at[slot() if callable(slot) else slot],
                device_id=peer, device_id_type=MESH,
            )

        self.only(when, lambda: made().start())
        self.started.append((made, when))

    def only(self, when, do):
        if when is None:
            do()
        else:
            pl.when(when())(do)

    def arrived(self, view, slot, peer):
        pltpu.make_async_remote_copy(
            src_ref=view, dst_ref=view, send_sem=self.send.at[0], recv_sem=self.recv.at[slot],
            device_id=peer, device_id_type=MESH,
        ).wait_recv()

    def finish(self):
        for made, when in self.started:
            self.only(when, lambda made=made: made().wait_send())


def meet(peers):
    barrier = pltpu.get_barrier_semaphore()
    for peer in peers:
        pl.semaphore_signal(barrier, inc=1, device_id=peer, device_id_type=MESH)
    pl.semaphore_wait(barrier, len(peers))


def summing_steps(refs, grad_maps):
    maps_in, own_maps, takers, all_e, all_a, e_got, e_two, e_own, a_in, a_part, a_z, a_own, send, recv, local = refs
    mail = Mail(send, recv)
    dp, ex = lax.axis_index("dp"), lax.axis_index("expert")
    x, z = dp % 2, dp // 2
    share = e_two.shape[3]
    group = {k: (ex + k) % 4 for k in range(1, 4)}
    later = {k: (z + k) % 4 for k in range(1, 4)}
    along = {k: (dp + k) % 8 for k in range(1, 8)}
    along_z = {k: ((z + k) % 4) * 2 + x for k in range(1, 4)}
    plane = {(a, k): (other(dp, 1) if a else dp, (ex + k) % 4) for a in range(2) for k in range(4) if (a, k) != (0, 0)}
    x_peer, y_peer, s_peer = (other(dp, 1), ex), (dp, other(ex, 2)), (dp, other(ex, 1))
    others = (other(ex, 1), other(ex, 2), other(other(ex, 1), 2))
    spots = {(up, k): ((z + 4 - k) if up else (z + k)) % 4 for up in (True, False) for k in range(1, 4)}
    reach = {(up, k): (z >= k) if up else (z + k < 4) for up in (True, False) for k in range(1, 4)}
    above, below = (((z + 1) % 4) * 2 + x, ex), (((z + 3) % 4) * 2 + x, ex)
    near = 2 * (ex // 2)
    away = 2 - near
    free = [0]

    def slots(n):
        free[0] += n
        return free[0] - n

    first = {n: slots(c) for n, c in dict(e1=4, e2=8, e5=8, e3=4, e4=4, a1=8, a2=4, a3=4, ay=2, ax=1, a_s=4).items()}

    def begin():
        meet([(dp, group[k]) for k in group] + [(along[k], ex) for k in along] + [plane[1, k] for k in range(1, 4)])
        for i, to in enumerate(others):
            mail.post(lambda to=to: maps_in.at[to], lambda: e_got.at[ex], (dp, to), first["e1"] + i)
        pltpu.make_async_copy(own_maps, e_got.at[ex], local.at[0]).start()

    def columns(refs, pair, to):
        return refs.at[pl.ds(pair, 2), :, pl.ds(pl.multiple_of(to * share, 128), share)]

    def spread_out(pair, slot):
        for k, to in along.items():
            mail.post(
                lambda to=to: columns(e_got, pair, to), lambda: e_two.at[dp, pl.ds(pair, 2)], (to, ex), first[slot] + k
            )
        e_two[dp, pl.ds(pair, 2)] = e_got[pl.ds(pair, 2), :, pl.ds(pl.multiple_of(dp * share, 128), share)]

    def spread_near():
        mail.arrived(e_got.at[others[0]], first["e1"], s_peer)
        pltpu.make_async_copy(own_maps, e_got.at[ex], local.at[0]).wait()
        spread_out(near, "e2")

    def spread_far():
        for i in (1, 2):
            mail.arrived(e_got.at[others[i]], first["e1"] + i, (dp, others[i]))
        spread_out(away, "e5")

    def placed(sender, columns):
        row, column = iota((128, columns), 0), iota((128, columns), 1)
        return one_hot(row - sender * RANK == column % RANK)

    def add_up():
        for k in along:
            source = (dp + 8 - k) % 8
            mail.arrived(e_two.at[source, pl.ds(near, 2)], first["e2"] + k, (source, ex))
            mail.arrived(e_two.at[source, pl.ds(away, 2)], first["e5"] + k, (source, ex))
        rows = e_two[...].reshape(-1, share)
        e_own[...] = mm(placed(takers[...], rows.shape[0]), rows).astype(BF)
        mail.post(lambda: e_own, lambda: all_e.at[dp], above, lambda: first["e3"] + z, lambda: z < 3)
        mail.post(lambda: e_own, lambda: all_e.at[dp], below, lambda: first["e3"] + z, lambda: z > 0)
        mail.post(lambda: e_own, lambda: all_e.at[dp], x_peer, lambda: first["e4"] + z)
        pltpu.make_async_copy(e_own, all_e.at[dp], local.at[1]).start()

    def e_forward(k):
        for up in (True, False):
            here = reach[up, k]
            place = spots[up, k]

            def take(place=place):
                mail.arrived(all_e.at[place * 2 + x], first["e3"] + place, (place * 2 + x, ex))

            def view(place=place):
                return all_e.at[place * 2 + x]

            mail.only(lambda here=here: here, take)
            if up:
                mail.post(
                    view, view, above, lambda place=place: first["e3"] + place, lambda here=here: here & (z < 3)
                )
            else:
                mail.post(
                    view, view, below, lambda place=place: first["e3"] + place, lambda here=here: here & (z > 0)
                )
            mail.post(view, view, x_peer, lambda place=place: first["e4"] + place, lambda here=here: here)

    def a_share():
        for (a, k), to in plane.items():
            number = 2 * to[1] + to[0] % 2
            mail.post(
                lambda number=number: grad_maps.at[number], lambda: a_in.at[x * 4 + ex], to, first["a1"] + a * 4 + k
            )
        a_in[x * 4 + ex] = grad_maps[2 * ex + x]

    def a_partial():
        for a, k in plane:
            source = (other(dp, 1) if a else dp, (ex + 4 - k) % 4)
            at = (source[0] % 2) * 4 + source[1]
            mail.arrived(a_in.at[at], first["a1"] + a * 4 + k, source)
        rows = a_in[...].reshape(128, -1)
        senders = takers[:, pl.ds(pl.multiple_of(z * 128, 128), 128)]
        a_part[...] = mm(placed(senders, 128), rows).astype(BF)
        for k, to in later.items():
            mail.post(
                lambda to=to: a_part.at[pl.ds(pl.multiple_of(to * 32, 32), 32)], lambda: a_z.at[z],
                (along_z[k], ex), first["a2"] + k,
            )
        a_z[z] = a_part[pl.ds(pl.multiple_of(z * 32, 32), 32), :]

    def piece(number, place):
        return all_a.at[number, pl.ds(pl.multiple_of(place * 32, 32), 32)]

    mine = 2 * ex + x

    def a_total():
        for k in range(1, 4):
            source = (z + 4 - k) % 4
            mail.arrived(a_z.at[source], first["a2"] + k, (source * 2 + x, ex))
        a_own[...] = sum(a_z[i].astype(F32) for i in range(4)).astype(BF)
        for k in range(1, 4):
            mail.post(lambda: a_own, lambda: piece(mine, z), (along_z[k], ex), first["a3"] + k)
        pltpu.make_async_copy(a_own, piece(mine, z), local.at[2]).start()

    def a_gather():
        pltpu.make_async_copy(a_own, piece(mine, z), local.at[2]).wait()
        for k in range(1, 4):
            source = (z + 4 - k) % 4
            mail.arrived(piece(mine, source), first["a3"] + k, (source * 2 + x, ex))

        def send(number, peer, slot):
            here = functools.partial(lambda number: all_a.at[number], number)
            mail.post(here, here, peer, slot)

        of_y, of_x = 2 * other(ex, 2) + x, 2 * ex + 1 - x
        of_xy = 2 * other(ex, 2) + 1 - x
        send(mine, x_peer, first["ax"])
        send(mine, y_peer, first["ay"])
        send(mine, s_peer, first["a_s"])
        mail.arrived(all_a.at[of_x], first["ax"], x_peer)
        send(of_x, y_peer, first["ay"] + 1)
        send(of_x, s_peer, first["a_s"] + 1)
        mail.arrived(all_a.at[of_y], first["ay"], y_peer)
        send(of_y, s_peer, first["a_s"] + 2)
        mail.arrived(all_a.at[of_xy], first["ay"] + 1, y_peer)
        send(of_xy, s_peer, first["a_s"] + 3)

    def end():
        sib = other(ex, 1)
        numbers = (2 * sib + x, 2 * sib + 1 - x, 2 * other(sib, 2) + x, 2 * other(sib, 2) + 1 - x)
        for i, number in enumerate(numbers):
            mail.arrived(all_a.at[number], first["a_s"] + i, s_peer)
        for k in range(4):
            mail.arrived(all_e.at[2 * k + 1 - x], first["e4"] + k, x_peer)
        pltpu.make_async_copy(e_own, all_e.at[dp], local.at[1]).wait()
        mail.finish()

    return {
        "begin": [begin], "outer": [spread_near], 1: [spread_far], 6: [add_up], 9: [functools.partial(e_forward, 1)],
        "maps": [a_share], 101: [functools.partial(e_forward, 2)], 102: [a_partial],
        "end": [a_total, functools.partial(e_forward, 3), a_gather, end],
    }


def attention_backward_kernel(exchange, *refs):
    spans, dh1_ref, tok, gain_a, wqkv, wqk, wo, down_ref, up_s, cos, sin = refs[:11]
    xa_ref, q_ref, k_ref, v_ref, ob_ref, ua_ref, uo_ref, lse_ref = refs[11:19]
    steps = {}
    if exchange:
        grad_tok, grad_maps, own = refs[22], refs[25], refs[37:]
        sums = (*refs[19:22], *refs[23:25])
        bias, dob, datt, duo, lse_t, center_t, dq, dk, dv, dlin, dua = refs[26:37]
        own, held = own[:10], own[10:]
        width = wo.shape[0]
        loads = (
            dh1_ref, up_s, wo, down_ref, ob_ref, lse_ref, q_ref, k_ref, v_ref, cos, sin, ua_ref, xa_ref, uo_ref,
            wqk, wqkv.at[:, pl.ds(2 * width, width)], tok,
        )
        load = Staged([*zip(loads, held), (held[17], grad_tok)], held[18])
        (
            dh1_ref, up_s, wo, down_ref, ob_ref, lse_ref, q_ref, k_ref, v_ref, cos, sin, ua_ref, xa_ref, uo_ref,
            wqk, wv, tok,
        ) = held[:17]
        grad_tok = held[17]
        steps = summing_steps((*sums, *own), grad_maps)
    else:
        grad_tok, grad_maps = refs[19:21]
        wv = wqkv.at[:, pl.ds(2 * wo.shape[0], wo.shape[0])]
        bias, dob, datt, duo, lse_t, center_t, dq, dk, dv, dlin, dua = refs[21:]
    length, width = tok.shape
    groups = width // GROUP

    def run(point):
        for step in steps.get(point, ()):
            step()

    run("begin")
    if exchange:
        load.start(range(17))
    for half in range(length // HALF):
        bias[half] = span_bias(spans[half] - half * HALF, True)
    if exchange:
        load.wait(range(6))
    of_head = one_hot(iota((128, width), 1) // HD == iota((128, width), 0))

    def outer(block, carry):
        at = pl.ds(pl.multiple_of(block * 256, 256), 256)
        d = dh1_ref[at, :].astype(BF)
        datt[at, :] = d
        u = mm_t(d, up_s[:, pl.ds(3 * width, width)]).astype(BF)
        duo[at, :] = u
        do = (mm_t(d, wo[...]) + mm_t(u, down_ref[1])).astype(BF)
        dob[at, :] = do
        both = do.astype(F32) * ob_ref[at, :].astype(F32)
        high = both.astype(BF)
        low = (both - high.astype(F32)).astype(BF)
        center_t[:, at] = mm_t(of_head, high) + mm_t(of_head, low)
        lse_t[:, at] = lse_ref[at, :].T
        if steps:
            pl.when(block == 0)(functools.partial(run, "outer"))
        return carry

    lax.fori_loop(0, length // 256, outer, 0)
    if exchange:
        load.wait(range(6, 9))
    dq[...] = jnp.zeros(dq.shape, F32)
    dk[...] = jnp.zeros(dk.shape, F32)
    dv[...] = jnp.zeros(dv.shape, F32)
    lane = iota((1, GROUP), 1)

    def attend(head, carry):
        g, h = head // 4, head % 4
        lanes = pl.ds(pl.multiple_of(g * GROUP, GROUP), GROUP)
        qk_own = jnp.where((lane % 128) // 32 == h, 1.0, 0.0).astype(BF)
        v_own = jnp.where(lane // 64 == h, 1.0, 0.0).astype(BF)
        lse = lse_t[pl.ds(head, 1), :]
        center = center_t[pl.ds(head, 1), :]
        for half in range(length // HALF):
            at = pl.ds(half * HALF, HALF)
            late = pl.ds(half * HALF, length - half * HALF)
            kh = k_ref[at, lanes] * qk_own
            vh = v_ref[at, lanes] * v_own
            q = q_ref[late, lanes] * BF(0.125)
            do = dob[late, lanes]
            s = mm_t(kh, q) - lse[:, half * HALF :]
            if half * HALF + HALF < length:
                s = jnp.concatenate([s[:, :HALF] + bias[half], s[:, HALF:]], axis=1)
            else:
                s = s + bias[half]
            prob = jnp.exp(s)
            dp = mm_t(vh, do)
            ds = (prob * (dp - center[:, half * HALF :])).astype(BF)
            dv[at, lanes] += mm(prob.astype(BF), do * v_own)
            dk[at, lanes] += mm(ds, q * qk_own)
            dq[late, lanes] += t_mm(ds, kh)
        for point in steps:
            if isinstance(point, int) and point < 100:
                pl.when(head == point)(functools.partial(run, point))
        return carry

    lax.fori_loop(0, HEADS, attend, 0)
    if exchange:
        load.wait(range(9, 17))

    def turn_back(block, carry):
        at = pl.ds(pl.multiple_of(block * 256, 256), 256)
        c, s = cos[at, :], -sin[at, :]
        for g in range(groups):
            lanes = pl.ds(g * GROUP, GROUP)
            dlin[at, lanes] = rope(dq[at, lanes] * 0.125, c, s).astype(BF)
            dlin[at, pl.ds(width + g * GROUP, GROUP)] = rope(dk[at, lanes], c, s).astype(BF)
        dlin[at, pl.ds(2 * width, width)] = dv[at, :].astype(BF)
        dua[at, :] = mm_t(dlin[at, :], up_s[:, pl.ds(0, 3 * width)]).astype(BF)
        return carry

    lax.fori_loop(0, length // 256, turn_back, 0)
    order = head_order(True)
    grads = t_mm(dua[...], xa_ref[...]).astype(BF)
    for p in range(3):
        grad_maps[p] = grads[p * RANK : (p + 1) * RANK]
    grad_maps[3] = t_mm(duo[...], ob_ref[...]).astype(BF)[:RANK]
    for p in range(3):
        grads = t_mm(ua_ref[...], dlin[:, pl.ds(p * width, width)]).astype(BF)[p * RANK : (p + 1) * RANK]
        if p < 2:
            grads = jnp.concatenate(
                [mm(grads[:, g * GROUP : (g + 1) * GROUP], order) for g in range(groups)], axis=1
            ).astype(BF)
        grad_maps[4 + p] = grads
    grad_maps[7] = t_mm(uo_ref[...], datt[...]).astype(BF)[:RANK]
    run("maps")

    def inner(block, carry):
        at = pl.ds(pl.multiple_of(block * 256, 256), 256)
        d, u = dlin[at, :], dua[at, :]
        dx = mm_t(d[:, : 2 * width], wqk[...]) + mm_t(d[:, 2 * width :], wv[...])
        dx = (dx + mm_t(u, down_ref[0])) * gain_a[...][None]
        h0 = tok[at, :].astype(F32)
        r = lax.rsqrt(jnp.mean(h0 * h0, axis=1, keepdims=True) + EPS)
        pull = r * dx - h0 * (r * r * r * jnp.mean(dx * h0, axis=1, keepdims=True))
        grad_tok[at, :] = (dh1_ref[at, :] + pull).astype(BF)
        for point in steps:
            if isinstance(point, int) and point >= 100:
                pl.when(block == point - 100)(functools.partial(run, point))
        return carry

    lax.fori_loop(0, length // 256, inner, 0)
    if exchange:
        load.start([17])
    run("end")
    if exchange:
        load.wait([17])


def attention_backward(
    spans, dh1, tok, gain_a, wqkv, wqk, wo, down_s, up_s, xa, q, k, v, ob, ua, uo, lse, maps=None, own_maps=None, takers=None
):
    length, width = tok.shape
    cos, sin = rope_tables(length)
    vmem, smem = pl.BlockSpec(memory_space=pltpu.VMEM), pl.BlockSpec(memory_space=pltpu.SMEM)
    anys = pl.BlockSpec(memory_space=pl.ANY)
    args = (spans, dh1, tok, gain_a, wqkv, wqk, wo, down_s, up_s, cos, sin, xa, q, k, v, ob, ua, uo, lse)
    in_specs = [smem] + [vmem] * 18
    compact = ((8, RANK, width), BF)
    shapes, out_specs, scratch = [((length, width), BF)], [vmem], []
    if maps is None:
        shapes.append(compact)
        out_specs.append(vmem)
    else:
        share = maps.shape[2] // 8
        in_specs = [smem] + [vmem if a.ndim == 1 else anys for a in args[1:]] + [anys, anys, vmem]
        held = [dh1, up_s, wo, down_s, ob, lse, q, k, v, cos, sin, ua, xa, uo, wqk, wo, tok, tok]
        held = [pltpu.VMEM(a.shape, a.dtype) for a in held]
        args += (maps, own_maps, takers)
        out_specs = [anys]
        shapes += [((8, 128, share), BF), ((8, 128, width), BF)]
        out_specs += [anys] * 2
        scratch.append(compact)
    scratch += [
        ((length // HALF, HALF, HALF), F32),
        ((length, width), BF),
        ((length, width), BF),
        ((length, 128), BF),
        ((128, length), F32),
        ((128, length), F32),
        ((length, width), F32),
        ((length, width), F32),
        ((length, width), F32),
        ((length, 3 * width), BF),
        ((length, 128), BF),
    ]
    params = dict(vmem_limit_bytes=62 * MIB)
    semaphores = []
    if maps is not None:
        scratch += [
            (maps.shape, BF),
            ((8, 4, RANK, share), BF),
            ((128, share), BF),
            ((8, RANK, width), BF),
            ((128, width), BF),
            ((4, 32, width), BF),
            ((32, width), BF),
        ]
        semaphores = [pltpu.SemaphoreType.DMA((64,)), pltpu.SemaphoreType.DMA((64,)), pltpu.SemaphoreType.DMA((3,))]
        semaphores += [*held, pltpu.SemaphoreType.DMA((18,))]
        params.update(collective_id=1, has_side_effects=True)
    return pl.pallas_call(
        functools.partial(attention_backward_kernel, maps is not None),
        out_shape=[jax.ShapeDtypeStruct(s, t) for s, t in shapes],
        in_specs=in_specs,
        out_specs=out_specs,
        scratch_shapes=[pltpu.VMEM(s, t) for s, t in scratch] + semaphores,
        compiler_params=pltpu.CompilerParams(**params),
        name="attention_backward",
    )(*args)


def unpack_kernel(all_e, all_a, a_attention, b_qkv, b_out, a_gate_up, b_gate_up, a_down, b_down):
    width, hidden, share = b_out.shape[1], a_down.shape[1], all_e.shape[2]
    for p in range(4):
        a_attention[p] = all_a[p].astype(F32).T
    for p in range(3):
        b_qkv[p] = all_a[4 + p].astype(F32)
    b_out[...] = all_a[7].astype(F32)

    def pieces(start, number):
        at = start
        while at < start + number:
            stop = min(start + number, (at // share + 1) * share)
            part = all_e[at // share, :, at % share : at % share + stop - at]
            yield at - start, part.astype(F32)
            at = stop

    for p in range(2):
        for at, part in pieces(p * width, width):
            a_gate_up[0, p, pl.ds(at, part.shape[1]), :] = part.T
        for at, part in pieces(2 * width + p * hidden, hidden):
            b_gate_up[0, p, :, pl.ds(at, part.shape[1])] = part
    for at, part in pieces(2 * width + 2 * hidden, hidden):
        a_down[0, pl.ds(at, part.shape[1]), :] = part.T
    for at, part in pieces(2 * width + 3 * hidden, width):
        b_down[0, :, pl.ds(at, part.shape[1])] = part


def unpack(all_e, all_a, hidden):
    width = all_a.shape[2]
    shapes = [
        (4, width, 128), (3, 128, width), (128, width),
        (1, 2, width, 128), (1, 2, 128, hidden), (1, hidden, 128), (1, 128, width),
    ]
    return pl.pallas_call(
        unpack_kernel,
        out_shape=[jax.ShapeDtypeStruct(s, F32) for s in shapes],
        in_specs=[pl.BlockSpec(memory_space=pltpu.VMEM)] * 2,
        out_specs=[pl.BlockSpec(memory_space=pltpu.VMEM)] * 7,
        compiler_params=pltpu.CompilerParams(vmem_limit_bytes=40 * MIB),
        name="unpack",
    )(all_e, all_a)


def split(x):
    high = x.astype(BF)
    return high, (x - high.astype(F32)).astype(BF)


def route(lin_ref, carried, routes, numbers, info_t, place_t):
    kinds, length = carried.shape
    target = iota((kinds, length), 0)
    logits = lin_ref[...].T[:kinds] + carried[...]
    picks = [target == routes[k : k + 1, :] for k in range(2)]
    chosen = [jnp.sum(jnp.where(p, logits, 0.0), axis=0, keepdims=True) for p in picks]
    top = jnp.maximum(*chosen)
    parts = [jnp.exp(c - top) for c in chosen]
    total = parts[0] + parts[1]
    info_t[...] = jnp.zeros(info_t.shape, F32)
    info_t[:kinds, :] = jnp.where(picks[0], parts[0] / total, jnp.where(picks[1], parts[1] / total, 0.0))
    wide = iota((128, length), 0)
    named = [(wide == routes[k : k + 1, :]) & (wide < numbers) for k in range(2)]
    member = one_hot(named[0] | named[1])
    for block in range(length // 256):
        before = one_hot(iota((256, length), 1) < iota((256, length), 0) + block * 256)
        place_t[:, pl.ds(block * 256, 256)] = mm_t(member, before)
    place_t[...] = jnp.where(named[0] | named[1], place_t[...], -1.0)
    return named, member


def padded_rows(part, before=0):
    columns = part.shape[1]
    parts = [jnp.zeros((before, columns), BF), part, jnp.zeros((128 - RANK - before, columns), BF)]
    return jnp.concatenate(parts if before else parts[1:], axis=0)


def take_rows(n, places, gates, xb, cot):
    own = iota((n, xb.shape[0]), 0).astype(F32) == places
    taken = one_hot(own)
    x = mm(taken, xb[...]).astype(BF)
    c = mm(taken, cot[...]).astype(BF)
    g = jnp.sum(jnp.where(own, gates, 0.0), axis=1, keepdims=True)
    return x, c, g, (g * c.astype(F32)).astype(BF)


def hidden_tile(x, dy, ug, dud, w_gate, w_up, w_down, b_gate, b_up, a_dn):
    gate = mm(x, w_gate) + mm(ug, b_gate)
    up = mm(x, w_up) + mm(ug, b_up)
    sig = 1.0 / (1.0 + jnp.exp(-gate))
    act = gate * sig
    hid = (act * up).astype(BF)
    dhid = mm_t(dy, w_down) + mm(dud, a_dn)
    dup = (dhid * act).astype(BF)
    dgate = (dhid * up * (sig + act * (1.0 - sig))).astype(BF)
    y = mm(hid, w_down)
    ud = mm_t(hid, a_dn)
    dx = mm_t(dgate, w_gate) + mm_t(dup, w_up)
    dug = mm_t(dgate, b_gate) + mm_t(dup, b_up)
    ug_t = ug.T
    grads = mm(ug_t[:RANK], dgate), mm(ug_t[RANK : 2 * RANK], dup), mm(dud.T[:RANK], hid)
    return (y, ud, dx, dug), [g.astype(BF) for g in grads]


def close_rows(expert, sums, x, c, g, dy, a_gu, b_dn):
    y, ud, dx, dug = sums
    ud, dug = ud.astype(BF), dug.astype(BF)
    y = y + mm(ud, b_dn)
    high, low = split(jnp.sum(c.astype(F32) * y.astype(BF).astype(F32), axis=1, keepdims=True))
    lane = iota((1, 128), 1)
    high, low = high.astype(F32), low.astype(F32)
    both = (
        (g * y).astype(BF),
        (dx + mm(dug, a_gu)).astype(BF),
        jnp.where(lane == expert, high, jnp.where(lane == expert + 64, low, 0.0)).astype(BF),
    )
    to_a = mm(dug.T[: 2 * RANK], x).astype(BF)
    return both, (to_a[:RANK], to_a[RANK:], mm(ud.T[:RANK], dy).astype(BF))


def experts_kernel(
    own_first, order, xb, h1_ref, lin_ref, cot, routes, carried, gain_m, wr, vectors, own_both,
    w_gate, w_up, w_down, maps,
    result, dh1_ref, grads,
    count, info, info_t, place_t, both, x_s, c_s, dy_s, g_s, y_acc, dx_acc, ug_s, ud_acc, dud_s, dug_acc, a_gu, b_dn, acc,
):
    step, j = pl.program_id(0), pl.program_id(1)
    steps, tiles = pl.num_programs(0), pl.num_programs(1)
    e = order[step]
    length, width = xb.shape
    kinds = carried.shape[0]
    numbers = kinds - 4
    tile = w_gate.shape[2]
    hidden = (maps.shape[2] - 3 * width) // 3
    rows_of = 128
    skip = HALF if own_first else 0

    if grads.shape[2] > maps.shape[2]:
        grads[0, :, maps.shape[2] :] = jnp.zeros((RANK, grads.shape[2] - maps.shape[2]), BF)

    @pl.when((step == 0) & (j == 0))
    def _():
        named, member = route(lin_ref, carried, routes, numbers, info_t, place_t)
        number = iota((128, 1), 0)
        counts = jnp.sum(member.astype(F32), axis=1, keepdims=True)
        padded = jnp.floor((counts + (rows_of - 1)) * (1.0 / rows_of))
        if own_first:
            padded = jnp.where(number == lax.axis_index("expert"), 0.0, padded)
        earlier = one_hot(iota((128, 128), 1) < iota((128, 128), 0))
        starts = rows_of * mm(earlier, jnp.broadcast_to(padded, (128, 128)).astype(BF))[:, :1]
        slots = starts + skip
        if own_first:
            slots = jnp.where(number == lax.axis_index("expert"), 0.0, slots)
        at_slot = place_t[...] + slots
        for k in range(2):
            spot = jnp.sum(jnp.where(named[k], at_slot + 1.0, 0.0), axis=0, keepdims=True) - 1.0
            info_t[pl.ds(64 + k, 1), :] = spot
        info[...] = info_t[...].T
        for i in range(numbers):
            count[0, i] = jnp.sum(jnp.where(number == i, padded, 0.0)).astype(jnp.int32)
            count[1, i] = jnp.sum(jnp.where(number == i, starts, 0.0)).astype(jnp.int32)
        count[1, numbers] = jnp.sum(jnp.where(number < numbers, padded, 0.0)).astype(jnp.int32) * rows_of

    blocks = count[0, e]
    first = pl.multiple_of(count[1, e], rows_of)

    @pl.when((j == 0) & (blocks > 0))
    def _():
        a_gu[...] = padded_rows(maps[0, :, :width]) + padded_rows(maps[0, :, width : 2 * width], RANK)
        b_dn[...] = padded_rows(maps[0, :, 2 * width + 3 * hidden :])

    @pl.when((j == 0) & (blocks == 0))
    def _():
        grads[...] = jnp.zeros(grads.shape, BF)

    def work(n):
        rows = pl.ds(0, n)

        @pl.when(j == 0)
        def _():
            x, c, g, dy = take_rows(n, place_t[pl.ds(e, 1), :], info_t[pl.ds(e, 1), :], xb, cot)
            x_s[rows, :] = x
            c_s[rows, :] = c
            dy_s[rows, :] = dy
            g_s[rows, :] = jnp.broadcast_to(g, (n, 128))
            ug_s[rows, :] = mm_t(x, a_gu[...]).astype(BF)
            dud_s[rows, :] = mm_t(dy, b_dn[...]).astype(BF)

        at = pl.multiple_of(j * tile, tile)
        starts = [2 * width + i * hidden + at for i in range(3)]
        sums, parts = hidden_tile(
            x_s[rows, :], dy_s[rows, :], ug_s[rows, :], dud_s[rows, :], w_gate[0], w_up[0], w_down[0],
            padded_rows(maps[0, :, pl.ds(starts[0], tile)]),
            padded_rows(maps[0, :, pl.ds(starts[1], tile)], RANK),
            padded_rows(maps[0, :, pl.ds(starts[2], tile)]),
        )
        for start, part in zip(starts, parts):
            grads[0, :, pl.ds(start, tile)] = part
        kept = (y_acc, ud_acc, dx_acc, dug_acc)

        @pl.when(j == 0)
        def _():
            for ref, value in zip(kept, sums):
                ref[rows, :] = value

        @pl.when(j > 0)
        def _():
            for ref, value in zip(kept, sums):
                ref[rows, :] += value

        @pl.when(j == tiles - 1)
        def _():
            out, parts = close_rows(
                e, [ref[rows, :] for ref in kept], x_s[rows, :], c_s[rows, :], g_s[rows, :][:, :1], dy_s[rows, :],
                a_gu[...], b_dn[...],
            )
            to = pl.ds(first, n)
            both[to, :width], both[to, width : 2 * width], both[to, 2 * width :] = out
            grads[0, :, :width], grads[0, :, width : 2 * width] = parts[:2]
            grads[0, :, 2 * width + 3 * hidden : 3 * width + 3 * hidden] = parts[2]

    for number in range(1, 512 // rows_of + 1):
        pl.when(blocks == number)(functools.partial(work, number * rows_of))

    @pl.when((step == steps - 1) & (j == tiles - 1))
    def _():
        used = count[1, numbers]
        both[pl.ds(pl.multiple_of(used, rows_of), HALF), :] = jnp.zeros((HALF, both.shape[1]), BF)
        lane = iota((1, 128), 1)

        def combine(block, carry):
            at = pl.ds(pl.multiple_of(block * 256, 256), 256)
            g = info[at, :]
            spots = g[:, 64:66]

            def taken(start):
                slot = (iota((256, HALF), 1) + start).astype(F32)
                return one_hot((slot == spots[:, :1]) | (slot == spots[:, 1:2]))

            if own_first:
                acc[...] = mm(taken(0), own_both[...])
            else:
                acc[...] = jnp.zeros(acc.shape, F32)

            def add(part, carry):
                k0 = pl.multiple_of(part * HALF, HALF)
                acc[...] += mm(taken(k0 + skip), both[pl.ds(k0, HALF), :])
                return carry

            lax.fori_loop(0, (used + HALF - 1) // HALF, add, 0)
            h1 = h1_ref[at, :]
            ct = cot[at, :].astype(F32)
            r = lax.rsqrt(jnp.mean(h1 * h1, axis=1, keepdims=True) + EPS)
            gain = gain_m[...][None]
            n2 = h1 * r * gain
            lin = lin_ref[at, :]
            gc = g[:, numbers + 1 : numbers + 2]
            g_fix = [g[:, numbers + 2 + i : numbers + 3 + i] for i in range(2)]
            mixes = []
            for i in range(2):
                a, b = lin[:, kinds + 2 * i : kinds + 2 * i + 1], lin[:, kinds + 2 * i + 1 : kinds + 2 * i + 2]
                top = jnp.maximum(a, b)
                a, b = jnp.exp(a - top), jnp.exp(b - top)
                mixes.append((a / (a + b), b / (a + b)))
            vecs = [vectors[i : i + 1, :] for i in range(2)]
            to_n2 = gc + g_fix[0] * mixes[0][0] + g_fix[1] * mixes[1][0]
            out = h1 + acc[:, :width] + to_n2 * n2
            out = out + (g_fix[0] * mixes[0][1]) * vecs[0] + (g_fix[1] * mixes[1][1]) * vecs[1]
            result[at, :] = out.astype(BF)
            a = jnp.sum(ct * n2, axis=1, keepdims=True)
            bs = [jnp.sum(ct * v, axis=1, keepdims=True) for v in vecs]
            packed = acc[:, 2 * width :]
            dg = jnp.where(lane < numbers, packed + pltpu.roll(packed, 64, 1), 0.0)
            dg = jnp.where(lane == numbers + 1, a, dg)
            for i in range(2):
                dg = jnp.where(lane == numbers + 2 + i, mixes[i][0] * a + mixes[i][1] * bs[i], dg)
            g = jnp.where(lane < kinds, g, 0.0)
            dlin = g * (dg - jnp.sum(g * dg, axis=1, keepdims=True))
            for i in range(2):
                pull = mixes[i][0] * mixes[i][1] * (g_fix[i] * (a - bs[i]))
                dlin = jnp.where(lane == kinds + 2 * i, pull, jnp.where(lane == kinds + 2 * i + 1, -pull, dlin))
            high, low = split(dlin)
            dn2 = acc[:, width : 2 * width] + (mm(high, wr[...]) + mm(low, wr[...])) + ct * to_n2
            dn2 = dn2 * gain
            back = r * dn2 - h1 * (r * r * r * jnp.mean(dn2 * h1, axis=1, keepdims=True))
            dh1_ref[at, :] = ct + back
            return carry

        lax.fori_loop(0, length // 256, combine, 0)


def experts_both_ways(xb, h1, lin, cot, routes, carried, gain_m, wr, vectors, w_gu, w_dn, maps, copies, own_both=None):
    length, width = xb.shape
    experts, hidden = w_dn.shape[0], w_dn.shape[1]
    tile = hidden // 2
    tiles = hidden // tile
    most = 2 * length + experts * 128
    total = 3 * width + 3 * hidden
    padded = -(-total // (copies * 128)) * copies * 128

    def whole(a):
        return pl.BlockSpec(a.shape, lambda e, j, order: (0,) * a.ndim, pipeline_mode=pl.Buffered(1))

    own_first = own_both is not None
    if own_first:
        order = (lax.axis_index("expert") + jnp.arange(1, experts, dtype=jnp.int32)) % experts
    else:
        order = jnp.arange(experts, dtype=jnp.int32)
        own_both = jnp.zeros((16, 128), BF)
    resident = (xb, h1, lin, cot, routes, carried, gain_m, wr, vectors, own_both)
    return pl.pallas_call(
        functools.partial(experts_kernel, own_first),
        out_shape=[
            jax.ShapeDtypeStruct((length, width), BF),
            jax.ShapeDtypeStruct((length, width), F32),
            jax.ShapeDtypeStruct((experts, RANK, padded), BF),
        ],
        grid_spec=pltpu.PrefetchScalarGridSpec(
            num_scalar_prefetch=1,
            grid=(order.shape[0], tiles),
            in_specs=[whole(a) for a in resident]
            + [
                pl.BlockSpec((1, width, tile), lambda e, j, order: (order[e], 0, j)),
                pl.BlockSpec((1, width, tile), lambda e, j, order: (order[e], 0, tiles + j)),
                pl.BlockSpec((1, tile, width), lambda e, j, order: (order[e], j, 0)),
                pl.BlockSpec((1, RANK, total), lambda e, j, order: (order[e], 0, 0)),
            ],
            out_specs=[
                pl.BlockSpec((length, width), lambda e, j, order: (0, 0), pipeline_mode=pl.Buffered(1)),
                pl.BlockSpec((length, width), lambda e, j, order: (0, 0), pipeline_mode=pl.Buffered(1)),
                pl.BlockSpec((1, RANK, padded), lambda e, j, order: (order[e], 0, 0)),
            ],
            scratch_shapes=[
            pltpu.SMEM((2, experts + 1), jnp.int32),
            pltpu.VMEM((length, 128), F32),
            pltpu.VMEM((128, length), F32),
            pltpu.VMEM((128, length), F32),
            pltpu.VMEM((most + HALF, 2 * width + 128), BF),
            pltpu.VMEM((512, width), BF),
            pltpu.VMEM((512, width), BF),
            pltpu.VMEM((512, width), BF),
            pltpu.VMEM((512, 128), F32),
            pltpu.VMEM((512, width), F32),
            pltpu.VMEM((512, width), F32),
            pltpu.VMEM((512, 128), BF),
            pltpu.VMEM((512, 128), F32),
            pltpu.VMEM((512, 128), BF),
            pltpu.VMEM((512, 128), F32),
            pltpu.VMEM((128, width), BF),
            pltpu.VMEM((128, width), BF),
            pltpu.VMEM((256, 2 * width + 128), F32),
        ],
        ),
        compiler_params=pltpu.CompilerParams(vmem_limit_bytes=60 * MIB),
        name="experts_both_ways",
    )(order, *resident, w_gu, w_gu, w_dn, maps)


def gather_experts(weights, senders):
    w_gu, w_dn, gu_down, gu_up, dn_down, dn_up = weights
    maps = jnp.concatenate(
        [gu_down[0, 0].T, gu_down[0, 1].T, gu_up[0, 0], gu_up[0, 1], dn_down[0].T, dn_up[0]], axis=1
    )
    to = (senders[:, None] * RANK + jnp.arange(RANK)[None, :]).reshape(-1)
    rows = mm((to[:, None] == jnp.arange(128)[None, :]).astype(BF), maps).astype(BF)
    rows = rows.reshape(senders.shape[0], RANK, -1)
    return (
        lax.all_gather(w_gu, "expert", axis=0, tiled=True),
        lax.all_gather(w_dn, "expert", axis=0, tiled=True),
        lax.all_to_all(rows, "expert", split_axis=0, concat_axis=0, tiled=True),
    )


BOTH = ("dp", "expert")


def sum_expert_maps(compact, spread):
    copies = lax.axis_size("dp")
    experts, rank, columns = compact.shape
    each = columns // copies
    parts = compact.reshape(experts, rank, copies, each).transpose(2, 0, 1, 3).reshape(copies * experts, rank, each)
    got = lax.all_to_all(parts, BOTH, split_axis=0, concat_axis=0, tiled=True)
    own = mm(spread, got.reshape(-1, each)).astype(BF)
    return lax.all_gather(own, "dp", axis=1, tiled=True)


def sum_attention_maps(compact, spread):
    devices = lax.axis_size("dp") * lax.axis_size("expert")
    maps, rank, width = compact.shape
    cuts = devices // maps
    parts = compact.reshape(maps, rank, cuts, width // cuts).transpose(0, 2, 1, 3).reshape(devices, rank, width // cuts)
    got = lax.all_to_all(parts, BOTH, split_axis=0, concat_axis=0, tiled=True)
    own = mm(spread, got.reshape(devices * rank, width // cuts)).astype(BF)
    whole = lax.all_gather(own[None], BOTH, axis=0, tiled=True)
    return whole.reshape(maps, cuts, 128, width // cuts).transpose(0, 2, 1, 3).reshape(maps, 128, width).astype(F32)


def body(
    exchange,
    tokens, cotangent, attention_norm_gain, query_key_value_weight, attention_output_weight,
    adapter_attention_down_maps, adapter_query_key_value_up_maps, adapter_output_up_map,
    experts_norm_gain, router_weight, constant_expert_mixing, constant_expert_vectors,
    expert_gate_up_weight, expert_down_weight, adapter_expert_gate_up_down_maps, adapter_expert_gate_up_up_maps,
    adapter_expert_down_down_maps, adapter_expert_down_up_maps,
    routes, router_logits_carried, picture_span_starts, sequence_adapter_index,
):
    groups = lax.axis_size("expert")
    width = tokens.shape[1]
    hidden = expert_down_weight.shape[1]
    first = lax.axis_index("dp") * groups
    senders = lax.dynamic_slice_in_dim(sequence_adapter_index, first, groups, 0)
    spans = picture_span_starts.reshape(-1)
    own = (
        expert_gate_up_weight, expert_down_weight, adapter_expert_gate_up_down_maps,
        adapter_expert_gate_up_up_maps, adapter_expert_down_down_maps, adapter_expert_down_up_maps,
    )
    outs = attention_forward(
        tokens, attention_norm_gain, query_key_value_weight, adapter_attention_down_maps, adapter_query_key_value_up_maps,
        attention_output_weight, adapter_output_up_map, experts_norm_gain, router_weight.T, constant_expert_mixing.T,
        spans, sequence_adapter_index,
        (*own, cotangent, routes.T, router_logits_carried.T) if exchange else (),
    )
    xa, q, k, v, ob, ua, uo, lse, h1, xb, lin, wqk, down_s, up_s, wr = outs[:15]
    weights = outs[15:18] if exchange else gather_experts(own, senders)
    result, dh1, expert_maps = experts_both_ways(
        xb, h1, lin, cotangent, routes.T, router_logits_carried.T, experts_norm_gain, wr, constant_expert_vectors, *weights,
        lax.axis_size("dp"), outs[18] if exchange else None,
    )
    backward = functools.partial(
        attention_backward, spans, dh1, tokens, attention_norm_gain, query_key_value_weight, wqk, attention_output_weight, down_s, up_s,
        xa, q, k, v, ob, ua, uo, lse,
    )
    if exchange:
        takers = jnp.repeat(sequence_adapter_index, RANK)[None]
        grad_tokens, all_e, all_a = backward(expert_maps, outs[19], takers)
        return (result, grad_tokens, *unpack(all_e, all_a, hidden))
    grad_tokens, attention_maps = backward()
    to = (sequence_adapter_index[:, None] * RANK + jnp.arange(RANK)[None, :]).reshape(-1)
    spread = (jnp.arange(128)[:, None] == to[None, :]).astype(BF)
    of_expert = sum_expert_maps(expert_maps, spread).astype(F32)
    of_attention = sum_attention_maps(attention_maps, spread)
    ends = [0, width, 2 * width, 2 * width + hidden, 2 * width + 2 * hidden, 2 * width + 3 * hidden, 3 * width + 3 * hidden]
    gud0, gud1, guu0, guu1, dnd, dnu = (of_expert[:, a:b] for a, b in zip(ends, ends[1:]))
    return (
        result,
        grad_tokens,
        of_attention[:4].transpose(0, 2, 1),
        of_attention[4:7],
        of_attention[7],
        jnp.stack([gud0.T, gud1.T])[None],
        jnp.stack([guu0, guu1])[None],
        dnd.T[None],
        dnu[None],
    )


def solution(mesh):
    tokens, own = P(("dp", "expert"), None), P("expert", None, None)
    own4 = P("expert", None, None, None)
    in_specs = (tokens, tokens) + (P(),) * 10 + (own, own, own4, own4, own, own) + (tokens,) * 3 + (P(),)
    out_specs = (tokens, tokens, P(), P(), P(), own4, own4, own, own)
    exchange = dict(mesh.shape) == {"dp": 8, "expert": 4}
    return jax.shard_map(functools.partial(body, exchange), mesh=mesh, in_specs=in_specs, out_specs=out_specs, check_vma=False)
```

```python
import functools

import jax
import jax.numpy as jnp
import numpy as np
from jax import lax
from jax.experimental import pallas as pl
from jax.experimental.pallas import tpu as pltpu
from jax.sharding import PartitionSpec as P

HEADS = 12
HD = 64
RANK = 16
PIC = 256
GROUP = 256
HALF = 512
EPS = 1e-06
NEG = -1e30
BF = jnp.bfloat16
F32 = jnp.float32
MIB = 1024 * 1024


def mm(a, b):
    return jnp.dot(a, b, preferred_element_type=F32)


def mm_t(a, b):
    return lax.dot_general(a, b, (((1,), (1,)), ((), ())), preferred_element_type=F32)


def t_mm(a, b):
    return lax.dot_general(a, b, (((0,), (0,)), ((), ())), preferred_element_type=F32)


def iota(shape, dim):
    return lax.broadcasted_iota(jnp.int32, shape, dim)


def one_hot(condition):
    return jnp.where(condition, 1.0, 0.0).astype(BF)


def picker(adapter, place, rows=128, columns=128):
    row, column = iota((rows, columns), 0), iota((rows, columns), 1)
    return one_hot((row - adapter * RANK == column - place * RANK) & (column // RANK == place))


def placer(adapter, place, rows=128, columns=128):
    row, column = iota((rows, columns), 0), iota((rows, columns), 1)
    return one_hot((column - adapter * RANK == row - place * RANK) & (row // RANK == place))


def head_order(back):
    row, column = iota((GROUP, GROUP), 0), iota((GROUP, GROUP), 1)
    a, b = (column, row) if back else (row, column)
    return one_hot(a == (b % 128 // 32) * 64 + b // 128 * 32 + b % 32)


def rope_tables(length):
    spacing = 10000.0 ** (-np.arange(0, HD, 2, dtype=np.float32) / np.float32(HD))
    angles = np.arange(length, dtype=np.float32)[:, None] * spacing.astype(np.float32)[None, :]
    angles = np.tile(angles, (1, 4))
    return np.cos(angles).astype(np.float32), np.sin(angles).astype(np.float32)


def rope(pair, cosine, sine):
    low, high = pair[:, :128], pair[:, 128:]
    return jnp.concatenate([low * cosine - high * sine, high * cosine + low * sine], axis=1)


def span_bias(start, transposed):
    a, b = iota((HALF, HALF), 0), iota((HALF, HALF), 1)
    query, key = (b, a) if transposed else (a, b)
    inside = (query >= start) & (query < start + PIC) & (key >= start) & (key < start + PIC)
    return jnp.where((key <= query) | inside, 0.0, NEG)


UNITS = 32
CHUNKS = ((0, 1), (1, 2), (3, 1), (4, 2))
EXTRA = ((0, 2), (2, 2))
MESH = pl.DeviceIdType.MESH


def other(index, step):
    return index + step - 2 * step * ((index // step) % 2)


def sending_steps(own, outs, scratch):
    adapters, w_gu, w_dn, gu_down, gu_up, dn_down, dn_up = own
    all_gu, all_dn, all_maps = outs
    bounce_gu, bounce_dn, compact, send, recv, local = scratch
    sources, targets, bounce = (w_gu, w_dn), (all_gu, all_dn), (bounce_gu, bounce_dn)
    dp, ex = lax.axis_index("dp"), lax.axis_index("expert")
    sibling, far = other(ex, 1), other(ex, 2)
    peers = {
        "x": (other(dp, 1), ex), "z": (other(dp, 2), ex), "y": (dp, far), "s": (dp, sibling), "d": (dp, other(far, 1)),
    }
    x, z = dp % 2, (dp // 2) % 2
    quarter = {"y": z * 2 + x, "x": z * 2 + 1 - x, "z": (1 - z) * 2 + x, "d": (1 - z) * 2 + 1 - x}
    kind = (x + z) % 2
    slots = {}
    for name in ("y", "x", "z", "d"):
        for chunk in CHUNKS:
            slots[name, chunk] = len(slots)
    for name in ("e", "o"):
        for chunk in EXTRA:
            slots[name, chunk] = len(slots)
    count = len(slots)
    started = []

    def views(refs, expert, key):
        name, (first, number) = key
        if name in quarter:
            first = quarter[name] * 6 + first
        else:
            first = 24 + 4 * (kind if name == "e" else 1 - kind) + first
        columns, rows = refs[0].shape[-1] // UNITS, refs[1].shape[-2] // UNITS
        return (
            refs[0].at[expert, :, pl.ds(pl.multiple_of(first * columns, columns), number * columns)],
            refs[1].at[expert, pl.ds(pl.multiple_of(first * rows, rows), number * rows), :],
        )

    def copies(source, target, peer, slot):
        for i in range(len(source())):
            number = len(started)

            def made(i=i, number=number):
                return pltpu.make_async_remote_copy(
                    src_ref=source()[i], dst_ref=target()[i], send_sem=send.at[number], recv_sem=recv.at[slot, i],
                    device_id=peers[peer], device_id_type=MESH,
                )

            made().start()
            started.append(made)

    def arrived(view, slot, i):
        pltpu.make_async_remote_copy(
            src_ref=view, dst_ref=view, send_sem=send.at[0], recv_sem=recv.at[slot, i],
            device_id=peers["s"], device_id_type=MESH,
        ).wait_recv()

    def begin():
        barrier = pltpu.get_barrier_semaphore()
        for peer in peers.values():
            pl.semaphore_signal(barrier, inc=1, device_id=peer, device_id_type=MESH)
        pl.semaphore_wait(barrier, len(peers))
        for name, chunks in (("y", CHUNKS), ("e", EXTRA)):
            for chunk in chunks:
                key = name, chunk
                copies(
                    functools.partial(views, sources, 0, key), functools.partial(views, targets, ex, key), "y", slots[key]
                )
        copies(lambda: [s.at[0] for s in sources], lambda: [t.at[ex] for t in targets], "s", 2 * count)
        for i in range(2):
            pltpu.make_async_copy(sources[i].at[0], bounce[i], local.at[i]).start()

    def select():
        row, column = iota((64, 128), 0), iota((64, 128), 1)
        first = sum(jnp.where(row // RANK == i, adapters[dp * 4 + i], 0) for i in range(4))
        rows = one_hot(column == first * RANK + row % RANK)
        width, hidden = gu_down.shape[2], dn_down.shape[1]
        parts = [
            (0, mm_t(rows, gu_down[0, 0])),
            (width, mm_t(rows, gu_down[0, 1])),
            (2 * width, mm(rows, gu_up[0, 0])),
            (2 * width + hidden, mm(rows, gu_up[0, 1])),
            (2 * width + 2 * hidden, mm_t(rows, dn_down[0])),
            (2 * width + 3 * hidden, mm(rows, dn_up[0])),
        ]
        for at, part in parts:
            for i in range(4):
                compact[i, :, pl.ds(at, part.shape[1])] = part[i * RANK : (i + 1) * RANK].astype(BF)

    def send_maps():
        for i, (peer, to) in enumerate((("s", sibling), ("y", far), ("d", other(far, 1)))):
            copies(lambda to=to: [compact.at[to]], lambda: [all_maps.at[ex]], peer, 2 * count + 1 + i)
        pltpu.make_async_copy(compact.at[ex], all_maps.at[ex], local.at[2]).start()

    def turn():
        for i in range(2):
            pltpu.make_async_copy(sources[i].at[0], bounce[i], local.at[i]).wait()
            pltpu.make_async_copy(bounce[i], targets[i].at[ex], local.at[i]).start()

    along_x = (CHUNKS[0], CHUNKS[3])

    def got(name, chunk):
        key = name, chunk
        to = []
        if name == "y":
            to = [("x", slots["x", chunk]), ("z", slots["z", chunk])]
        if name == "x" and chunk not in along_x:
            to = [("z", slots["d", chunk])]
        if name == "z" and chunk in along_x:
            to = [("x", slots["d", chunk])]
        if name == "e":
            to = [("x" if chunk == EXTRA[0] else "z", slots["o", chunk])]

        def step():
            mine = functools.partial(views, targets, far, key)
            for i in range(2):
                arrived(mine()[i], slots[key], i)
            for peer, slot in to:
                copies(mine, mine, peer, slot)
            copies(mine, mine, "s", count + slots[key])

        return step

    def change():
        for i in range(2):
            pltpu.make_async_copy(bounce[i], targets[i].at[ex], local.at[i]).wait()
            arrived(targets[i].at[sibling], 2 * count, i)
            pltpu.make_async_copy(targets[i].at[sibling], bounce[i], local.at[i]).start()
        pltpu.make_async_copy(compact.at[ex], all_maps.at[ex], local.at[2]).wait()
        arrived(all_maps.at[sibling], 2 * count + 1, 0)
        pltpu.make_async_copy(all_maps.at[sibling], compact.at[ex], local.at[2]).start()

    def changed():
        for i in range(2):
            pltpu.make_async_copy(targets[i].at[sibling], bounce[i], local.at[i]).wait()
        pltpu.make_async_copy(all_maps.at[sibling], compact.at[ex], local.at[2]).wait()

    def end():
        for made in started:
            made().wait_send()
        for i, source in enumerate((far, other(far, 1))):
            arrived(all_maps.at[source], 2 * count + 2 + i, 0)
        for key, slot in slots.items():
            view = views(targets, other(far, 1), key)
            for i in range(2):
                arrived(view[i], count + slot, i)

    c, e = CHUNKS, EXTRA
    return {
        "begin": [begin],
        "loaded": [select],
        "ready": [turn, got("y", c[0])],
        "projected": [got("x", c[0]), got("z", c[0]), got("y", c[1])],
        3: [got("y", c[2])],
        6: [got("z", c[1]), got("x", c[1])],
        8: [got("y", c[3]), got("d", c[0])],
        10: [got("x", c[2]), got("z", c[2])],
        "finished": [send_maps, got("z", c[3]), got("e", e[0])],
        200: [got("x", c[3])],
        "change": [change],
        "changed": [got("e", e[1]), got("d", c[1]), changed],
        212: [got("d", c[2])],
        "end": [got("o", e[0]), got("d", c[3]), got("o", e[1]), end],
    }


def attention_forward_kernel(exchange, *refs):
    spans, adapters, tok, gain_a, wqkv, down, up, wo, up_out, gain_m, router, mixing, cos, sin = refs[:14]
    refs = refs[14:]
    own = ()
    if exchange:
        own, refs = (adapters, *refs[:9]), refs[9:]
    xa_ref, q_ref, k_ref, v_ref, ob_ref, ua_ref, uo_ref, lse_ref, h1_ref, xb_ref, lin_ref, wqk_ref, down_ref, up_s, wr = refs[:15]
    refs = refs[15:]
    steps = {}
    if exchange:
        cot, routes, carried = own[-3:]
        own_outs, routing, refs = refs[:3], refs[5:7], refs[:5] + refs[7:]
        semaphores = refs[6:12]
        own_both, own_grads, bias = refs[3:6]
        bounce_gu, bounce_dn, compact = refs[6:9]
        x_s, c_s, dy_s, y_acc, ud_acc, dx_acc, dug_acc = refs[12:19]
        held, refs = refs[19:], ()
        loads = (tok, down, up, up_out, *own[3:7], wqkv, cos, sin, wo, cot)
        load = Staged(list(zip(loads, held)), held[-2])
        tok, down, up, up_out, *maps, wqkv, cos, sin, wo, cot = held[: len(loads)]
        outs = (xa_ref, q_ref, k_ref, v_ref, ob_ref, ua_ref, uo_ref, lse_ref, h1_ref, xb_ref, lin_ref, wqk_ref, down_ref, up_s, wr)
        kept_outs = held[len(loads) : len(loads) + len(outs)]
        info_t, place_t = held[len(loads) + len(outs) : len(loads) + len(outs) + 2]
        store = Staged(list(zip((*kept_outs, info_t, place_t), (*outs, *routing))), held[-1])
        xa_ref, q_ref, k_ref, v_ref, ob_ref, ua_ref, uo_ref, lse_ref, h1_ref, xb_ref, lin_ref, wqk_ref, down_ref, up_s, wr = kept_outs
        steps = sending_steps((*own[:3], *maps), own_outs, semaphores)
    else:
        (bias,) = refs
    length, width = tok.shape
    groups = width // GROUP
    adapter = adapters[lax.axis_index("dp") * lax.axis_size("expert") + lax.axis_index("expert")]

    def run(point):
        for step in steps.get(point, ()):
            step()

    run("begin")
    if exchange:
        load.start()
        load.wait()
        run("loaded")
    order = head_order(False)
    down_s = sum(mm(down[p], picker(adapter, p)) for p in range(3)).astype(BF)
    down_o = mm(down[3], picker(adapter, 0)).astype(BF)
    up_o = mm(placer(adapter, 0), up_out[...]).astype(BF)
    row, column = iota((128, router.shape[0]), 0), iota((128, router.shape[0]), 1)
    wr[...] = mm(one_hot(row == column), router[...]).astype(BF)
    row, column = iota((128, mixing.shape[0]), 0), iota((128, mixing.shape[0]), 1)
    wr[...] += mm(one_hot(row == column + router.shape[0]), mixing[...]).astype(BF)
    down_ref[0] = down_s
    down_ref[1] = down_o
    up_s[:, pl.ds(3 * width, width)] = up_o
    for p in range(3):
        rows = mm(placer(adapter, p), up[p]).astype(BF)
        for g in range(groups):
            block = rows[:, g * GROUP : (g + 1) * GROUP]
            if p < 2:
                block = mm(block, order).astype(BF)
            up_s[:, pl.ds(p * width + g * GROUP, GROUP)] = block
    for g in range(2 * groups):
        at = pl.ds(g * GROUP, GROUP)
        wqk_ref[:, at] = mm(wqkv[:, at], order).astype(BF)
    for half in range(length // HALF):
        bias[half] = span_bias(spans[half] - half * HALF, False)
    run("ready")

    def project(block, carry):
        at = pl.ds(pl.multiple_of(block * 256, 256), 256)
        h0 = tok[at, :].astype(F32)
        x = h0 * lax.rsqrt(jnp.mean(h0 * h0, axis=1, keepdims=True) + EPS) * gain_a[...][None]
        x = x.astype(BF)
        xa_ref[at, :] = x
        u = mm(x, down_s).astype(BF)
        ua_ref[at, :] = u
        c, s = cos[at, :], sin[at, :]
        for p, out in enumerate((q_ref, k_ref)):
            for g in range(groups):
                lanes = pl.ds(p * width + g * GROUP, GROUP)
                lin = mm(x, wqk_ref[:, lanes]) + mm(u, up_s[:, lanes])
                out[at, pl.ds(g * GROUP, GROUP)] = rope(lin, c, s).astype(BF)
        lanes = pl.ds(2 * width, width)
        v_ref[at, :] = (mm(x, wqkv[:, lanes]) + mm(u, up_s[:, lanes])).astype(BF)
        return carry

    lax.fori_loop(0, length // 256, project, 0)
    run("projected")

    lane = iota((1, GROUP), 1)
    lse_ref[...] = jnp.zeros(lse_ref.shape, F32)
    ob_f = ob_ref

    def attend(head, carry):
        g, h = head // 4, head % 4
        lanes = pl.ds(pl.multiple_of(g * GROUP, GROUP), GROUP)
        qk_own = jnp.where((lane % 128) // 32 == h, 1.0, 0.0).astype(BF)
        v_own = jnp.where(lane // 64 == h, 1.0, 0.0)
        kh = k_ref[:, lanes] * qk_own
        vh = v_ref[:, lanes] * v_own.astype(BF)
        for half in range(length // HALF):
            at = pl.ds(half * HALF, HALF)
            q = q_ref[at, lanes] * BF(0.125)
            keys = (half + 1) * HALF
            diag = mm_t(q, kh[half * HALF : keys]) + bias[half]
            top = jnp.max(diag, axis=1, keepdims=True)
            if half:
                past = mm_t(q, kh[: half * HALF])
                top = jnp.maximum(top, jnp.max(past, axis=1, keepdims=True))
            e = jnp.exp(diag - top)
            total = jnp.sum(e, axis=1, keepdims=True)
            o = mm(e.astype(BF), vh[half * HALF : keys])
            if half:
                e = jnp.exp(past - top)
                total = total + jnp.sum(e, axis=1, keepdims=True)
                o = o + mm(e.astype(BF), vh[: half * HALF])
            o = o * pl.reciprocal(total, approx=False)
            lse = top + jnp.log(total)
            lse_ref[at, :] = jnp.where(iota((1, 128), 1) == head, lse, lse_ref[at, :])
            old = jnp.where(v_own > 0.5, 0.0, ob_f[at, lanes].astype(F32))
            ob_f[at, lanes] = jnp.where(v_own > 0.5, o, old).astype(BF)
        for point in steps:
            if isinstance(point, int) and point < 100:
                pl.when(head == point)(functools.partial(run, point))
        return carry

    lax.fori_loop(0, HEADS, attend, 0)

    def finish(block, carry):
        at = pl.ds(pl.multiple_of(block * 256, 256), 256)
        o = ob_ref[at, :]
        u = mm(o, down_o).astype(BF)
        uo_ref[at, :] = u
        h1 = tok[at, :].astype(F32) + (mm(o, wo[...]) + mm(u, up_o))
        h1_ref[at, :] = h1
        x = h1 * lax.rsqrt(jnp.mean(h1 * h1, axis=1, keepdims=True) + EPS) * gain_m[...][None]
        x = x.astype(BF)
        xb_ref[at, :] = x
        lin_ref[at, :] = mm_t(x, wr[...])
        return carry

    lax.fori_loop(0, length // 256, finish, 0)
    if exchange:
        store.start(range(15))
        run("finished")
        ex = lax.axis_index("expert")
        hidden = bounce_dn.shape[0]
        rest = own_grads.shape[2] - 3 * width - 3 * hidden
        own_grads[:, :, 3 * width + 3 * hidden :] = jnp.zeros((2, RANK, rest), BF)
        route(lin_ref, carried, routes, carried.shape[0] - 4, info_t, place_t)
        store.start([15, 16])
        run(200)
        tile = 512
        kept = (y_acc, ud_acc, dx_acc, dug_acc)
        for which, expert in enumerate((ex, other(ex, 1))):
            rows = pl.ds(which * HALF, HALF)
            x, c, g, dy = take_rows(HALF, place_t[pl.ds(expert, 1), :], info_t[pl.ds(expert, 1), :], xb_ref, cot)
            x_s[...], c_s[...], dy_s[...] = x, c, dy
            if which:
                run("changed")
            a_gu = padded_rows(compact[ex, :, :width]) + padded_rows(compact[ex, :, width : 2 * width], RANK)
            b_dn = padded_rows(compact[ex, :, 2 * width + 3 * hidden :])
            ug, dud = mm_t(x, a_gu).astype(BF), mm_t(dy, b_dn).astype(BF)
            for ref in kept:
                ref[...] = jnp.zeros(ref.shape, F32)

            def one_tile(j, carry, which=which, ug=ug, dud=dud):
                at = pl.multiple_of(j * tile, tile)
                starts = [2 * width + i * hidden + at for i in range(3)]
                sums, parts = hidden_tile(
                    x_s[...], dy_s[...], ug, dud,
                    bounce_gu[:, pl.ds(at, tile)], bounce_gu[:, pl.ds(hidden + at, tile)], bounce_dn[pl.ds(at, tile), :],
                    padded_rows(compact[ex, :, pl.ds(starts[0], tile)]),
                    padded_rows(compact[ex, :, pl.ds(starts[1], tile)], RANK),
                    padded_rows(compact[ex, :, pl.ds(starts[2], tile)]),
                )
                for start, part in zip(starts, parts):
                    own_grads[which, :, pl.ds(start, tile)] = part
                for ref, value in zip(kept, sums):
                    ref[...] += value
                for point in steps:
                    if isinstance(point, int) and point > 200 + 10 * which and point < 210 + 10 * which:
                        pl.when(j == point - 201 - 10 * which)(functools.partial(run, point))
                return carry

            lax.fori_loop(0, hidden // tile, one_tile, 0)
            out, parts = close_rows(expert, [ref[...] for ref in kept], x_s[...], c_s[...], g, dy_s[...], a_gu, b_dn)
            if not which:
                run("change")
            own_both[rows, :width], own_both[rows, width : 2 * width], own_both[rows, 2 * width :] = out
            own_grads[which, :, :width], own_grads[which, :, width : 2 * width] = parts[:2]
            own_grads[which, :, 2 * width + 3 * hidden : 3 * width + 3 * hidden] = parts[2]
        store.wait()
    run("end")


def attention_forward(tok, gain_a, wqkv, down, up, wo, up_out, gain_m, router, mixing, spans, adapters, own=()):
    length, width = tok.shape
    cos, sin = rope_tables(length)
    shapes = [
        ((length, width), BF),
        ((length, width), BF),
        ((length, width), BF),
        ((length, width), BF),
        ((length, width), BF),
        ((length, 128), BF),
        ((length, 128), BF),
        ((length, 128), F32),
        ((length, width), F32),
        ((length, width), BF),
        ((length, 128), F32),
        ((width, 2 * width), BF),
        ((2, width, 128), BF),
        ((128, 4 * width), BF),
        ((128, width), BF),
    ]
    vmem, smem = pl.BlockSpec(memory_space=pltpu.VMEM), pl.BlockSpec(memory_space=pltpu.SMEM)
    anys = pl.BlockSpec(memory_space=pl.ANY)
    in_specs, out_specs = [smem, smem] + [vmem] * 12, [vmem] * len(shapes)
    scratch = [pltpu.VMEM((length // HALF, HALF, HALF), F32)]
    params = dict(vmem_limit_bytes=62 * MIB)
    args = (spans, adapters, tok, gain_a, wqkv, down, up, wo, up_out, gain_m, router, mixing, cos, sin)
    if own:
        w_gu, w_dn = own[:2]
        columns = 3 * width + 3 * w_dn.shape[1]
        in_specs = [smem, smem] + [vmem if i in (1, 7, 8, 9) else anys for i in range(12)]
        in_specs += [anys] * 7 + [vmem] * 2
        args += own
        held = [args[i] for i in (2, 5, 6, 8, 16, 17, 18, 19, 4, 12, 13, 7, 20)]
        held = [pltpu.VMEM(a.shape, a.dtype) for a in held] + [pltpu.VMEM(a, t) for a, t in shapes]
        padded = -(-columns // 1024) * 1024
        shapes += [
            ((4, *w_gu.shape[1:]), BF),
            ((4, *w_dn.shape[1:]), BF),
            ((4, RANK, columns), BF),
            ((2 * HALF, 2 * width + 128), BF),
            ((2, RANK, padded), BF),
            ((128, length), F32),
            ((128, length), F32),
        ]
        held += [pltpu.VMEM(a, t) for a, t in shapes[-2:]]
        out_specs = [anys] * (len(out_specs) + 3) + [vmem] * 2 + [anys] * 2
        scratch += [
            pltpu.VMEM(w_gu.shape[1:], BF),
            pltpu.VMEM(w_dn.shape[1:], BF),
            pltpu.VMEM((4, RANK, columns), BF),
            pltpu.SemaphoreType.DMA((96,)),
            pltpu.SemaphoreType.DMA((48, 2)),
            pltpu.SemaphoreType.DMA((3,)),
            pltpu.VMEM((HALF, width), BF),
            pltpu.VMEM((HALF, width), BF),
            pltpu.VMEM((HALF, width), BF),
            pltpu.VMEM((HALF, width), F32),
            pltpu.VMEM((HALF, 128), F32),
            pltpu.VMEM((HALF, width), F32),
            pltpu.VMEM((HALF, 128), F32),
        ]
        scratch += held + [pltpu.SemaphoreType.DMA((16,)), pltpu.SemaphoreType.DMA((20,))]
        params.update(collective_id=0, has_side_effects=True)
    return pl.pallas_call(
        functools.partial(attention_forward_kernel, bool(own)),
        out_shape=[jax.ShapeDtypeStruct(s, t) for s, t in shapes],
        in_specs=in_specs,
        out_specs=out_specs,
        scratch_shapes=scratch,
        compiler_params=pltpu.CompilerParams(**params),
        name="attention_forward",
    )(*args)


class Staged:
    def __init__(self, pairs, sems):
        self.pairs, self.sems = pairs, sems

    def copy(self, i):
        return pltpu.make_async_copy(self.pairs[i][0], self.pairs[i][1], self.sems.at[i])

    def start(self, numbers=None):
        for i in range(len(self.pairs)) if numbers is None else numbers:
            self.copy(i).start()

    def wait(self, numbers=None):
        for i in range(len(self.pairs)) if numbers is None else numbers:
            self.copy(i).wait()


class Mail:
    def __init__(self, send, recv):
        self.send, self.recv, self.started = send, recv, []

    def post(self, source, target, peer, slot, when=None):
        number = len(self.started)

        def made():
            return pltpu.make_async_remote_copy(
                src_ref=source(), dst_ref=target(), send_sem=self.send.at[number],
                recv_sem=self.recv.at[slot() if callable(slot) else slot],
                device_id=peer, device_id_type=MESH,
            )

        self.only(when, lambda: made().start())
        self.started.append((made, when))

    def only(self, when, do):
        if when is None:
            do()
        else:
            pl.when(when())(do)

    def arrived(self, view, slot, peer):
        pltpu.make_async_remote_copy(
            src_ref=view, dst_ref=view, send_sem=self.send.at[0], recv_sem=self.recv.at[slot],
            device_id=peer, device_id_type=MESH,
        ).wait_recv()

    def finish(self):
        for made, when in self.started:
            self.only(when, lambda made=made: made().wait_send())


def meet(peers):
    barrier = pltpu.get_barrier_semaphore()
    for peer in peers:
        pl.semaphore_signal(barrier, inc=1, device_id=peer, device_id_type=MESH)
    pl.semaphore_wait(barrier, len(peers))


def summing_steps(refs, grad_maps):
    maps_in, own_maps, takers, all_e, all_a, e_got, e_two, e_own, a_in, a_part, a_z, a_own, send, recv, local = refs
    mail = Mail(send, recv)
    dp, ex = lax.axis_index("dp"), lax.axis_index("expert")
    x, z = dp % 2, dp // 2
    share = e_two.shape[3]
    group = {k: (ex + k) % 4 for k in range(1, 4)}
    later = {k: (z + k) % 4 for k in range(1, 4)}
    along = {k: (dp + k) % 8 for k in range(1, 8)}
    along_z = {k: ((z + k) % 4) * 2 + x for k in range(1, 4)}
    plane = {(a, k): (other(dp, 1) if a else dp, (ex + k) % 4) for a in range(2) for k in range(4) if (a, k) != (0, 0)}
    x_peer, y_peer, s_peer = (other(dp, 1), ex), (dp, other(ex, 2)), (dp, other(ex, 1))
    others = (other(ex, 1), other(ex, 2), other(other(ex, 1), 2))
    spots = {(up, k): ((z + 4 - k) if up else (z + k)) % 4 for up in (True, False) for k in range(1, 4)}
    reach = {(up, k): (z >= k) if up else (z + k < 4) for up in (True, False) for k in range(1, 4)}
    above, below = (((z + 1) % 4) * 2 + x, ex), (((z + 3) % 4) * 2 + x, ex)
    near = 2 * (ex // 2)
    away = 2 - near
    free = [0]

    def slots(n):
        free[0] += n
        return free[0] - n

    first = {n: slots(c) for n, c in dict(e1=4, e2=8, e5=8, e3=4, e4=4, a1=8, a2=4, a3=4, ay=2, ax=1, a_s=4).items()}

    def begin():
        meet([(dp, group[k]) for k in group] + [(along[k], ex) for k in along] + [plane[1, k] for k in range(1, 4)])
        for i, to in enumerate(others):
            mail.post(
                lambda i=i, to=to: maps_in.at[to] if i else own_maps.at[1], lambda: e_got.at[ex], (dp, to), first["e1"] + i
            )
        pltpu.make_async_copy(own_maps.at[0], e_got.at[ex], local.at[0]).start()

    def columns(refs, pair, to):
        return refs.at[pl.ds(pair, 2), :, pl.ds(pl.multiple_of(to * share, 128), share)]

    def spread_out(pair, slot):
        for k, to in along.items():
            mail.post(
                lambda to=to: columns(e_got, pair, to), lambda: e_two.at[dp, pl.ds(pair, 2)], (to, ex), first[slot] + k
            )
        e_two[dp, pl.ds(pair, 2)] = e_got[pl.ds(pair, 2), :, pl.ds(pl.multiple_of(dp * share, 128), share)]

    def spread_near():
        mail.arrived(e_got.at[others[0]], first["e1"], s_peer)
        pltpu.make_async_copy(own_maps.at[0], e_got.at[ex], local.at[0]).wait()
        spread_out(near, "e2")

    def spread_far():
        for i in (1, 2):
            mail.arrived(e_got.at[others[i]], first["e1"] + i, (dp, others[i]))
        spread_out(away, "e5")

    def placed(sender, columns):
        row, column = iota((128, columns), 0), iota((128, columns), 1)
        return one_hot(row - sender * RANK == column % RANK)

    def add_up():
        for k in along:
            source = (dp + 8 - k) % 8
            mail.arrived(e_two.at[source, pl.ds(near, 2)], first["e2"] + k, (source, ex))
            mail.arrived(e_two.at[source, pl.ds(away, 2)], first["e5"] + k, (source, ex))
        rows = e_two[...].reshape(-1, share)
        e_own[...] = mm(placed(takers[...], rows.shape[0]), rows).astype(BF)
        mail.post(lambda: e_own, lambda: all_e.at[dp], above, lambda: first["e3"] + z, lambda: z < 3)
        mail.post(lambda: e_own, lambda: all_e.at[dp], below, lambda: first["e3"] + z, lambda: z > 0)
        mail.post(lambda: e_own, lambda: all_e.at[dp], x_peer, lambda: first["e4"] + z)
        pltpu.make_async_copy(e_own, all_e.at[dp], local.at[1]).start()

    def e_forward(k):
        for up in (True, False):
            here = reach[up, k]
            place = spots[up, k]

            def take(place=place):
                mail.arrived(all_e.at[place * 2 + x], first["e3"] + place, (place * 2 + x, ex))

            def view(place=place):
                return all_e.at[place * 2 + x]

            mail.only(lambda here=here: here, take)
            if up:
                mail.post(
                    view, view, above, lambda place=place: first["e3"] + place, lambda here=here: here & (z < 3)
                )
            else:
                mail.post(
                    view, view, below, lambda place=place: first["e3"] + place, lambda here=here: here & (z > 0)
                )
            mail.post(view, view, x_peer, lambda place=place: first["e4"] + place, lambda here=here: here)

    def a_share():
        for (a, k), to in plane.items():
            number = 2 * to[1] + to[0] % 2
            mail.post(
                lambda number=number: grad_maps.at[number], lambda: a_in.at[x * 4 + ex], to, first["a1"] + a * 4 + k
            )
        a_in[x * 4 + ex] = grad_maps[2 * ex + x]

    def a_partial():
        for a, k in plane:
            source = (other(dp, 1) if a else dp, (ex + 4 - k) % 4)
            at = (source[0] % 2) * 4 + source[1]
            mail.arrived(a_in.at[at], first["a1"] + a * 4 + k, source)
        rows = a_in[...].reshape(128, -1)
        senders = takers[:, pl.ds(pl.multiple_of(z * 128, 128), 128)]
        a_part[...] = mm(placed(senders, 128), rows).astype(BF)
        for k, to in later.items():
            mail.post(
                lambda to=to: a_part.at[pl.ds(pl.multiple_of(to * 32, 32), 32)], lambda: a_z.at[z],
                (along_z[k], ex), first["a2"] + k,
            )
        a_z[z] = a_part[pl.ds(pl.multiple_of(z * 32, 32), 32), :]

    def piece(number, place):
        return all_a.at[number, pl.ds(pl.multiple_of(place * 32, 32), 32)]

    mine = 2 * ex + x

    def a_total():
        for k in range(1, 4):
            source = (z + 4 - k) % 4
            mail.arrived(a_z.at[source], first["a2"] + k, (source * 2 + x, ex))
        a_own[...] = sum(a_z[i].astype(F32) for i in range(4)).astype(BF)
        for k in range(1, 4):
            mail.post(lambda: a_own, lambda: piece(mine, z), (along_z[k], ex), first["a3"] + k)
        pltpu.make_async_copy(a_own, piece(mine, z), local.at[2]).start()

    def a_gather():
        pltpu.make_async_copy(a_own, piece(mine, z), local.at[2]).wait()
        for k in range(1, 4):
            source = (z + 4 - k) % 4
            mail.arrived(piece(mine, source), first["a3"] + k, (source * 2 + x, ex))

        def send(number, peer, slot):
            here = functools.partial(lambda number: all_a.at[number], number)
            mail.post(here, here, peer, slot)

        of_y, of_x = 2 * other(ex, 2) + x, 2 * ex + 1 - x
        of_xy = 2 * other(ex, 2) + 1 - x
        send(mine, x_peer, first["ax"])
        send(mine, y_peer, first["ay"])
        send(mine, s_peer, first["a_s"])
        mail.arrived(all_a.at[of_x], first["ax"], x_peer)
        send(of_x, y_peer, first["ay"] + 1)
        send(of_x, s_peer, first["a_s"] + 1)
        mail.arrived(all_a.at[of_y], first["ay"], y_peer)
        send(of_y, s_peer, first["a_s"] + 2)
        mail.arrived(all_a.at[of_xy], first["ay"] + 1, y_peer)
        send(of_xy, s_peer, first["a_s"] + 3)

    def end():
        sib = other(ex, 1)
        numbers = (2 * sib + x, 2 * sib + 1 - x, 2 * other(sib, 2) + x, 2 * other(sib, 2) + 1 - x)
        for i, number in enumerate(numbers):
            mail.arrived(all_a.at[number], first["a_s"] + i, s_peer)
        for k in range(4):
            mail.arrived(all_e.at[2 * k + 1 - x], first["e4"] + k, x_peer)
        pltpu.make_async_copy(e_own, all_e.at[dp], local.at[1]).wait()
        mail.finish()

    return {
        "begin": [begin], "outer": [spread_near], 1: [spread_far], 6: [add_up], 9: [functools.partial(e_forward, 1)],
        "maps": [a_share], 101: [functools.partial(e_forward, 2)], 102: [a_partial],
        "end": [a_total, functools.partial(e_forward, 3), a_gather, end],
    }


def attention_backward_kernel(exchange, numbers, *refs):
    spans, h1_ref, tok, gain_a, wqkv, wqk, wo, down_ref, up_s, cos, sin = refs[:11]
    xa_ref, q_ref, k_ref, v_ref, ob_ref, ua_ref, uo_ref, lse_ref = refs[11:19]
    mixed, cot, lin_ref, info, vectors, gain_m, wr = refs[19:26]
    steps = {}
    if exchange:
        grad_out, result_out, grad_maps, own = refs[29], refs[30], refs[33], refs[46:]
        dh1_ref, bias, dob, datt, duo, lse_t, center_t, dq, dk, dv, dlin, dua = refs[34:46]
        own, held = own[:10], own[10:]
        width = wo.shape[0]
        loads = (
            up_s, wo, down_ref, ob_ref, lse_ref, lin_ref, info, wr, q_ref, k_ref, v_ref, cos, sin, ua_ref, xa_ref, uo_ref,
            wqk, wqkv.at[:, pl.ds(2 * width, width)], tok,
        )
        grad_tok, result = held[19:21]
        pairs = [
            (h1_ref, dq), (mixed, dlin.at[:, pl.ds(0, mixed.shape[1])]), (cot, grad_tok), *zip(loads, held),
            (grad_tok, grad_out), (result, result_out),
        ]
        load = Staged(pairs, held[21])
        h1_ref, mixed, cot = dq, dlin, grad_tok
        (
            up_s, wo, down_ref, ob_ref, lse_ref, lin_ref, info, wr, q_ref, k_ref, v_ref, cos, sin, ua_ref, xa_ref, uo_ref,
            wqk, wv, tok,
        ) = held[:19]
        steps = summing_steps((*refs[26:29], *refs[31:33], *own), grad_maps)
    else:
        grad_tok, result, grad_maps = refs[26:29]
        wv = wqkv.at[:, pl.ds(2 * wo.shape[0], wo.shape[0])]
        dh1_ref, bias, dob, datt, duo, lse_t, center_t, dq, dk, dv, dlin, dua = refs[29:]
    length, width = tok.shape
    groups = width // GROUP

    def run(point):
        for step in steps.get(point, ()):
            step()

    run("begin")
    if exchange:
        load.start(range(22))
    for half in range(length // HALF):
        bias[half] = span_bias(spans[half] - half * HALF, True)
    if exchange:
        load.wait(range(11))
    of_head = one_hot(iota((128, width), 1) // HD == iota((128, width), 0))

    def outer(block, carry):
        at = pl.ds(pl.multiple_of(block * 256, 256), 256)
        h1 = h1_ref[at, :]
        g = info[at, :]
        lane = iota((1, 128), 1)
        kinds = numbers + 4
        ct = cot[at, :].astype(F32)
        r = lax.rsqrt(jnp.mean(h1 * h1, axis=1, keepdims=True) + EPS)
        gain = gain_m[...][None]
        n2 = h1 * r * gain
        lin = lin_ref[at, :]
        gc = g[:, numbers + 1 : numbers + 2]
        g_fix = [g[:, numbers + 2 + i : numbers + 3 + i] for i in range(2)]
        mixes = []
        for i in range(2):
            a, b = lin[:, kinds + 2 * i : kinds + 2 * i + 1], lin[:, kinds + 2 * i + 1 : kinds + 2 * i + 2]
            top = jnp.maximum(a, b)
            a, b = jnp.exp(a - top), jnp.exp(b - top)
            mixes.append((a / (a + b), b / (a + b)))
        vecs = [vectors[i : i + 1, :] for i in range(2)]
        to_n2 = gc + g_fix[0] * mixes[0][0] + g_fix[1] * mixes[1][0]
        out = h1 + mixed[at, :width].astype(F32) + to_n2 * n2
        out = out + (g_fix[0] * mixes[0][1]) * vecs[0] + (g_fix[1] * mixes[1][1]) * vecs[1]
        result[at, :] = out.astype(BF)
        a = jnp.sum(ct * n2, axis=1, keepdims=True)
        bs = [jnp.sum(ct * v, axis=1, keepdims=True) for v in vecs]
        packed = mixed[at, 2 * width : 2 * width + 128].astype(F32)
        dg = jnp.where(lane < numbers, packed + pltpu.roll(packed, 64, 1), 0.0)
        dg = jnp.where(lane == numbers + 1, a, dg)
        for i in range(2):
            dg = jnp.where(lane == numbers + 2 + i, mixes[i][0] * a + mixes[i][1] * bs[i], dg)
        g = jnp.where(lane < kinds, g, 0.0)
        dlin = g * (dg - jnp.sum(g * dg, axis=1, keepdims=True))
        for i in range(2):
            pull = mixes[i][0] * mixes[i][1] * (g_fix[i] * (a - bs[i]))
            dlin = jnp.where(lane == kinds + 2 * i, pull, jnp.where(lane == kinds + 2 * i + 1, -pull, dlin))
        high, low = split(dlin)
        dn2 = mixed[at, width : 2 * width].astype(F32) + (mm(high, wr[...]) + mm(low, wr[...])) + ct * to_n2
        dn2 = dn2 * gain
        back = r * dn2 - h1 * (r * r * r * jnp.mean(dn2 * h1, axis=1, keepdims=True))
        dh1 = ct + back
        dh1_ref[at, :] = dh1
        d = dh1.astype(BF)
        datt[at, :] = d
        u = mm_t(d, up_s[:, pl.ds(3 * width, width)]).astype(BF)
        duo[at, :] = u
        do = (mm_t(d, wo[...]) + mm_t(u, down_ref[1])).astype(BF)
        dob[at, :] = do
        both = do.astype(F32) * ob_ref[at, :].astype(F32)
        high = both.astype(BF)
        low = (both - high.astype(F32)).astype(BF)
        center_t[:, at] = mm_t(of_head, high) + mm_t(of_head, low)
        lse_t[:, at] = lse_ref[at, :].T
        if steps:
            pl.when(block == 0)(functools.partial(run, "outer"))
        return carry

    lax.fori_loop(0, length // 256, outer, 0)
    if exchange:
        load.start([23])
        load.wait(range(11, 14))
    dq[...] = jnp.zeros(dq.shape, F32)
    dk[...] = jnp.zeros(dk.shape, F32)
    dv[...] = jnp.zeros(dv.shape, F32)
    lane = iota((1, GROUP), 1)

    def attend(head, carry):
        g, h = head // 4, head % 4
        lanes = pl.ds(pl.multiple_of(g * GROUP, GROUP), GROUP)
        qk_own = jnp.where((lane % 128) // 32 == h, 1.0, 0.0).astype(BF)
        v_own = jnp.where(lane // 64 == h, 1.0, 0.0).astype(BF)
        lse = lse_t[pl.ds(head, 1), :]
        center = center_t[pl.ds(head, 1), :]
        for half in range(length // HALF):
            at = pl.ds(half * HALF, HALF)
            late = pl.ds(half * HALF, length - half * HALF)
            kh = k_ref[at, lanes] * qk_own
            vh = v_ref[at, lanes] * v_own
            q = q_ref[late, lanes] * BF(0.125)
            do = dob[late, lanes]
            s = mm_t(kh, q) - lse[:, half * HALF :]
            if half * HALF + HALF < length:
                s = jnp.concatenate([s[:, :HALF] + bias[half], s[:, HALF:]], axis=1)
            else:
                s = s + bias[half]
            prob = jnp.exp(s)
            dp = mm_t(vh, do)
            ds = (prob * (dp - center[:, half * HALF :])).astype(BF)
            dv[at, lanes] += mm(prob.astype(BF), do * v_own)
            dk[at, lanes] += mm(ds, q * qk_own)
            dq[late, lanes] += t_mm(ds, kh)
        for point in steps:
            if isinstance(point, int) and point < 100:
                pl.when(head == point)(functools.partial(run, point))
        return carry

    lax.fori_loop(0, HEADS, attend, 0)
    if exchange:
        load.wait(range(14, 22))

    def turn_back(block, carry):
        at = pl.ds(pl.multiple_of(block * 256, 256), 256)
        c, s = cos[at, :], -sin[at, :]
        for g in range(groups):
            lanes = pl.ds(g * GROUP, GROUP)
            dlin[at, lanes] = rope(dq[at, lanes] * 0.125, c, s).astype(BF)
            dlin[at, pl.ds(width + g * GROUP, GROUP)] = rope(dk[at, lanes], c, s).astype(BF)
        dlin[at, pl.ds(2 * width, width)] = dv[at, :].astype(BF)
        dua[at, :] = mm_t(dlin[at, :], up_s[:, pl.ds(0, 3 * width)]).astype(BF)
        return carry

    lax.fori_loop(0, length // 256, turn_back, 0)
    order = head_order(True)
    grads = t_mm(dua[...], xa_ref[...]).astype(BF)
    for p in range(3):
        grad_maps[p] = grads[p * RANK : (p + 1) * RANK]
    grad_maps[3] = t_mm(duo[...], ob_ref[...]).astype(BF)[:RANK]
    for p in range(3):
        grads = t_mm(ua_ref[...], dlin[:, pl.ds(p * width, width)]).astype(BF)[p * RANK : (p + 1) * RANK]
        if p < 2:
            grads = jnp.concatenate(
                [mm(grads[:, g * GROUP : (g + 1) * GROUP], order) for g in range(groups)], axis=1
            ).astype(BF)
        grad_maps[4 + p] = grads
    grad_maps[7] = t_mm(uo_ref[...], datt[...]).astype(BF)[:RANK]
    run("maps")

    def inner(block, carry):
        at = pl.ds(pl.multiple_of(block * 256, 256), 256)
        d, u = dlin[at, :], dua[at, :]
        dx = mm_t(d[:, : 2 * width], wqk[...]) + mm_t(d[:, 2 * width :], wv[...])
        dx = (dx + mm_t(u, down_ref[0])) * gain_a[...][None]
        h0 = tok[at, :].astype(F32)
        r = lax.rsqrt(jnp.mean(h0 * h0, axis=1, keepdims=True) + EPS)
        pull = r * dx - h0 * (r * r * r * jnp.mean(dx * h0, axis=1, keepdims=True))
        grad_tok[at, :] = (dh1_ref[at, :] + pull).astype(BF)
        for point in steps:
            if isinstance(point, int) and point >= 100:
                pl.when(block == point - 100)(functools.partial(run, point))
        return carry

    lax.fori_loop(0, length // 256, inner, 0)
    if exchange:
        load.start([22])
    run("end")
    if exchange:
        load.wait([22, 23])


def attention_backward(
    numbers, spans, h1, tok, gain_a, wqkv, wqk, wo, down_s, up_s, xa, q, k, v, ob, ua, uo, lse,
    mixed, cot, lin, info, vectors, gain_m, wr, maps=None, own_maps=None, takers=None,
):
    length, width = tok.shape
    cos, sin = rope_tables(length)
    vmem, smem = pl.BlockSpec(memory_space=pltpu.VMEM), pl.BlockSpec(memory_space=pltpu.SMEM)
    anys = pl.BlockSpec(memory_space=pl.ANY)
    args = (
        spans, h1, tok, gain_a, wqkv, wqk, wo, down_s, up_s, cos, sin, xa, q, k, v, ob, ua, uo, lse,
        mixed, cot, lin, info, vectors, gain_m, wr,
    )
    in_specs = [smem] + [vmem] * 25
    compact = ((8, RANK, width), BF)
    shapes, out_specs, scratch = [((length, width), BF)] * 2, [vmem] * 2, []
    if maps is None:
        shapes.append(compact)
        out_specs.append(vmem)
    else:
        share = maps.shape[2] // 8
        in_specs = [smem] + [vmem if a.size < 2048 else anys for a in args[1:]] + [anys, anys, vmem]
        held = [up_s, wo, down_s, ob, lse, lin, info, wr, q, k, v, cos, sin, ua, xa, uo, wqk, wo, tok, tok, tok]
        held = [pltpu.VMEM(a.shape, a.dtype) for a in held]
        args += (maps, own_maps, takers)
        out_specs = [anys] * 2
        shapes += [((8, 128, share), BF), ((8, 128, width), BF)]
        out_specs += [anys] * 2
        scratch.append(compact)
    scratch += [
        ((length, width), F32),
        ((length // HALF, HALF, HALF), F32),
        ((length, width), BF),
        ((length, width), BF),
        ((length, 128), BF),
        ((128, length), F32),
        ((128, length), F32),
        ((length, width), F32),
        ((length, width), F32),
        ((length, width), F32),
        ((length, 3 * width), BF),
        ((length, 128), BF),
    ]
    params = dict(vmem_limit_bytes=62 * MIB)
    semaphores = []
    if maps is not None:
        scratch += [
            (maps.shape, BF),
            ((8, 4, RANK, share), BF),
            ((128, share), BF),
            ((8, RANK, width), BF),
            ((128, width), BF),
            ((4, 32, width), BF),
            ((32, width), BF),
        ]
        semaphores = [pltpu.SemaphoreType.DMA((64,)), pltpu.SemaphoreType.DMA((64,)), pltpu.SemaphoreType.DMA((3,))]
        semaphores += [*held, pltpu.SemaphoreType.DMA((24,))]
        params.update(collective_id=1, has_side_effects=True)
    return pl.pallas_call(
        functools.partial(attention_backward_kernel, maps is not None, numbers),
        out_shape=[jax.ShapeDtypeStruct(s, t) for s, t in shapes],
        in_specs=in_specs,
        out_specs=out_specs,
        scratch_shapes=[pltpu.VMEM(s, t) for s, t in scratch] + semaphores,
        compiler_params=pltpu.CompilerParams(**params),
        name="attention_backward",
    )(*args)


def unpack_kernel(all_e, all_a, a_attention, b_qkv, b_out, a_gate_up, b_gate_up, a_down, b_down):
    width, hidden, share = b_out.shape[1], a_down.shape[1], all_e.shape[2]
    for p in range(4):
        a_attention[p] = all_a[p].astype(F32).T
    for p in range(3):
        b_qkv[p] = all_a[4 + p].astype(F32)
    b_out[...] = all_a[7].astype(F32)

    def pieces(start, number):
        at = start
        while at < start + number:
            stop = min(start + number, (at // share + 1) * share)
            part = all_e[at // share, :, at % share : at % share + stop - at]
            yield at - start, part.astype(F32)
            at = stop

    for p in range(2):
        for at, part in pieces(p * width, width):
            a_gate_up[0, p, pl.ds(at, part.shape[1]), :] = part.T
        for at, part in pieces(2 * width + p * hidden, hidden):
            b_gate_up[0, p, :, pl.ds(at, part.shape[1])] = part
    for at, part in pieces(2 * width + 2 * hidden, hidden):
        a_down[0, pl.ds(at, part.shape[1]), :] = part.T
    for at, part in pieces(2 * width + 3 * hidden, width):
        b_down[0, :, pl.ds(at, part.shape[1])] = part


def unpack(all_e, all_a, hidden):
    width = all_a.shape[2]
    shapes = [
        (4, width, 128), (3, 128, width), (128, width),
        (1, 2, width, 128), (1, 2, 128, hidden), (1, hidden, 128), (1, 128, width),
    ]
    return pl.pallas_call(
        unpack_kernel,
        out_shape=[jax.ShapeDtypeStruct(s, F32) for s in shapes],
        in_specs=[pl.BlockSpec(memory_space=pltpu.VMEM)] * 2,
        out_specs=[pl.BlockSpec(memory_space=pltpu.VMEM)] * 7,
        compiler_params=pltpu.CompilerParams(vmem_limit_bytes=40 * MIB),
        name="unpack",
    )(all_e, all_a)


def split(x):
    high = x.astype(BF)
    return high, (x - high.astype(F32)).astype(BF)


def route(lin_ref, carried, routes, numbers, info_t, place_t):
    kinds, length = carried.shape
    target = iota((kinds, length), 0)
    logits = lin_ref[...].T[:kinds] + carried[...]
    picks = [target == routes[k : k + 1, :] for k in range(2)]
    chosen = [jnp.sum(jnp.where(p, logits, 0.0), axis=0, keepdims=True) for p in picks]
    top = jnp.maximum(*chosen)
    parts = [jnp.exp(c - top) for c in chosen]
    total = parts[0] + parts[1]
    info_t[...] = jnp.zeros(info_t.shape, F32)
    info_t[:kinds, :] = jnp.where(picks[0], parts[0] / total, jnp.where(picks[1], parts[1] / total, 0.0))
    wide = iota((128, length), 0)
    named = [(wide == routes[k : k + 1, :]) & (wide < numbers) for k in range(2)]
    member = one_hot(named[0] | named[1])
    for block in range(length // 256):
        before = one_hot(iota((256, length), 1) < iota((256, length), 0) + block * 256)
        place_t[:, pl.ds(block * 256, 256)] = mm_t(member, before)
    place_t[...] = jnp.where(named[0] | named[1], place_t[...], -1.0)


def padded_rows(part, before=0):
    columns = part.shape[1]
    parts = [jnp.zeros((before, columns), BF), part, jnp.zeros((128 - RANK - before, columns), BF)]
    return jnp.concatenate(parts if before else parts[1:], axis=0)


def take_rows(n, places, gates, xb, cot):
    own = iota((n, xb.shape[0]), 0).astype(F32) == places
    taken = one_hot(own)
    x = mm(taken, xb[...]).astype(BF)
    c = mm(taken, cot[...]).astype(BF)
    g = jnp.sum(jnp.where(own, gates, 0.0), axis=1, keepdims=True)
    return x, c, g, (g * c.astype(F32)).astype(BF)


def hidden_tile(x, dy, ug, dud, w_gate, w_up, w_down, b_gate, b_up, a_dn):
    gate = mm(x, w_gate) + mm(ug, b_gate)
    up = mm(x, w_up) + mm(ug, b_up)
    sig = 1.0 / (1.0 + jnp.exp(-gate))
    act = gate * sig
    hid = (act * up).astype(BF)
    dhid = mm_t(dy, w_down) + mm(dud, a_dn)
    dup = (dhid * act).astype(BF)
    dgate = (dhid * up * (sig + act * (1.0 - sig))).astype(BF)
    y = mm(hid, w_down)
    ud = mm_t(hid, a_dn)
    dx = mm_t(dgate, w_gate) + mm_t(dup, w_up)
    dug = mm_t(dgate, b_gate) + mm_t(dup, b_up)
    ug_t = ug.T
    grads = mm(ug_t[:RANK], dgate), mm(ug_t[RANK : 2 * RANK], dup), mm(dud.T[:RANK], hid)
    return (y, ud, dx, dug), [g.astype(BF) for g in grads]


def close_rows(expert, sums, x, c, g, dy, a_gu, b_dn):
    y, ud, dx, dug = sums
    ud, dug = ud.astype(BF), dug.astype(BF)
    y = y + mm(ud, b_dn)
    high, low = split(jnp.sum(c.astype(F32) * y.astype(BF).astype(F32), axis=1, keepdims=True))
    lane = iota((1, 128), 1)
    high, low = high.astype(F32), low.astype(F32)
    both = (
        (g * y).astype(BF),
        (dx + mm(dug, a_gu)).astype(BF),
        jnp.where(lane == expert, high, jnp.where(lane == expert + 64, low, 0.0)).astype(BF),
    )
    to_a = mm(dug.T[: 2 * RANK], x).astype(BF)
    return both, (to_a[:RANK], to_a[RANK:], mm(ud.T[:RANK], dy).astype(BF))


def experts_kernel(
    own_first, order, xb, cot, routes, given, given_too, own_both,
    w_gate, w_up, w_down, maps,
    mixed, info, grads,
    count, info_t, place_t, both, x_s, c_s, dy_s, g_s, y_acc, dx_acc, ug_s, ud_acc, dud_s, dug_acc, a_gu, b_dn, acc,
):
    step, j = pl.program_id(0), pl.program_id(1)
    steps, tiles = pl.num_programs(0), pl.num_programs(1)
    e = order[step]
    length, width = xb.shape
    numbers = count.shape[1] - 1
    tile = w_gate.shape[2]
    hidden = (maps.shape[2] - 3 * width) // 3
    rows_of = 128
    skip = 2 * HALF if own_first else 0

    if grads.shape[2] > maps.shape[2]:
        grads[0, :, maps.shape[2] :] = jnp.zeros((RANK, grads.shape[2] - maps.shape[2]), BF)

    @pl.when((step == 0) & (j == 0))
    def _():
        if own_first:
            info_t[...], place_t[...] = given[...], given_too[...]
        else:
            route(given, given_too, routes, numbers, info_t, place_t)
        wide = iota((128, length), 0)
        named = [(wide == routes[k : k + 1, :]) & (wide < numbers) for k in range(2)]
        number = iota((128, 1), 0)
        counts = jnp.max(place_t[...], axis=1, keepdims=True) + 1.0
        padded = jnp.floor((counts + (rows_of - 1)) * (1.0 / rows_of))
        if own_first:
            ex = lax.axis_index("expert")
            padded = jnp.where((number == ex) | (number == other(ex, 1)), 0.0, padded)
        earlier = one_hot(iota((128, 128), 1) < iota((128, 128), 0))
        starts = rows_of * mm(earlier, jnp.broadcast_to(padded, (128, 128)).astype(BF))[:, :1]
        slots = starts + skip
        if own_first:
            slots = jnp.where(number == ex, 0.0, jnp.where(number == other(ex, 1), 1.0 * HALF, slots))
        at_slot = place_t[...] + slots
        for k in range(2):
            spot = jnp.sum(jnp.where(named[k], at_slot + 1.0, 0.0), axis=0, keepdims=True) - 1.0
            info_t[pl.ds(64 + k, 1), :] = spot
        info[...] = info_t[...].T
        for i in range(numbers):
            count[0, i] = jnp.sum(jnp.where(number == i, padded, 0.0)).astype(jnp.int32)
            count[1, i] = jnp.sum(jnp.where(number == i, starts, 0.0)).astype(jnp.int32)
        count[1, numbers] = jnp.sum(jnp.where(number < numbers, padded, 0.0)).astype(jnp.int32) * rows_of

    blocks = count[0, e]
    first = pl.multiple_of(count[1, e], rows_of)

    @pl.when((j == 0) & (blocks > 0))
    def _():
        a_gu[...] = padded_rows(maps[0, :, :width]) + padded_rows(maps[0, :, width : 2 * width], RANK)
        b_dn[...] = padded_rows(maps[0, :, 2 * width + 3 * hidden :])

    @pl.when((j == 0) & (blocks == 0))
    def _():
        grads[...] = jnp.zeros(grads.shape, BF)

    def work(n):
        rows = pl.ds(0, n)

        @pl.when(j == 0)
        def _():
            x, c, g, dy = take_rows(n, place_t[pl.ds(e, 1), :], info_t[pl.ds(e, 1), :], xb, cot)
            x_s[rows, :] = x
            c_s[rows, :] = c
            dy_s[rows, :] = dy
            g_s[rows, :] = jnp.broadcast_to(g, (n, 128))
            ug_s[rows, :] = mm_t(x, a_gu[...]).astype(BF)
            dud_s[rows, :] = mm_t(dy, b_dn[...]).astype(BF)

        at = pl.multiple_of(j * tile, tile)
        starts = [2 * width + i * hidden + at for i in range(3)]
        sums, parts = hidden_tile(
            x_s[rows, :], dy_s[rows, :], ug_s[rows, :], dud_s[rows, :], w_gate[0], w_up[0], w_down[0],
            padded_rows(maps[0, :, pl.ds(starts[0], tile)]),
            padded_rows(maps[0, :, pl.ds(starts[1], tile)], RANK),
            padded_rows(maps[0, :, pl.ds(starts[2], tile)]),
        )
        for start, part in zip(starts, parts):
            grads[0, :, pl.ds(start, tile)] = part
        kept = (y_acc, ud_acc, dx_acc, dug_acc)

        @pl.when(j == 0)
        def _():
            for ref, value in zip(kept, sums):
                ref[rows, :] = value

        @pl.when(j > 0)
        def _():
            for ref, value in zip(kept, sums):
                ref[rows, :] += value

        @pl.when(j == tiles - 1)
        def _():
            out, parts = close_rows(
                e, [ref[rows, :] for ref in kept], x_s[rows, :], c_s[rows, :], g_s[rows, :][:, :1], dy_s[rows, :],
                a_gu[...], b_dn[...],
            )
            to = pl.ds(first, n)
            both[to, :width], both[to, width : 2 * width], both[to, 2 * width :] = out
            grads[0, :, :width], grads[0, :, width : 2 * width] = parts[:2]
            grads[0, :, 2 * width + 3 * hidden : 3 * width + 3 * hidden] = parts[2]

    for number in range(1, 512 // rows_of + 1):
        pl.when(blocks == number)(functools.partial(work, number * rows_of))

    @pl.when((step == steps - 1) & (j == tiles - 1))
    def _():
        used = count[1, numbers]
        both[pl.ds(pl.multiple_of(used, rows_of), HALF), :] = jnp.zeros((HALF, both.shape[1]), BF)
        def combine(block, carry):
            at = pl.ds(pl.multiple_of(block * 256, 256), 256)
            g = info[at, :]
            spots = g[:, 64:66]

            def taken(start):
                slot = (iota((256, HALF), 1) + start).astype(F32)
                return one_hot((slot == spots[:, :1]) | (slot == spots[:, 1:2]))

            if own_first:
                acc[...] = mm(taken(0), own_both[:HALF, :]) + mm(taken(HALF), own_both[HALF:, :])
            else:
                acc[...] = jnp.zeros(acc.shape, F32)

            def add(part, carry):
                k0 = pl.multiple_of(part * HALF, HALF)
                acc[...] += mm(taken(k0 + skip), both[pl.ds(k0, HALF), :])
                return carry

            lax.fori_loop(0, (used + HALF - 1) // HALF, add, 0)
            mixed[at, :] = acc[...].astype(BF)
            return carry

        lax.fori_loop(0, length // 256, combine, 0)


def experts_both_ways(xb, cot, routes, given, given_too, w_gu, w_dn, maps, copies, own_both=None):
    length, width = xb.shape
    experts, hidden = w_dn.shape[0], w_dn.shape[1]
    tile = hidden // 2
    tiles = hidden // tile
    most = 2 * length + experts * 128
    total = 3 * width + 3 * hidden
    padded = -(-total // (copies * 128)) * copies * 128

    def whole(a):
        return pl.BlockSpec(a.shape, lambda e, j, order: (0,) * a.ndim, pipeline_mode=pl.Buffered(1))

    own_first = own_both is not None
    if own_first:
        order = other(2 * (lax.axis_index("expert") // 2), 2) + jnp.arange(2, dtype=jnp.int32)
    else:
        order = jnp.arange(experts, dtype=jnp.int32)
        own_both = jnp.zeros((16, 128), BF)
    resident = (xb, cot, routes, given, given_too, own_both)
    return pl.pallas_call(
        functools.partial(experts_kernel, own_first),
        out_shape=[
            jax.ShapeDtypeStruct((length, 2 * width + 128), BF),
            jax.ShapeDtypeStruct((length, 128), F32),
            jax.ShapeDtypeStruct((experts, RANK, padded), BF),
        ],
        grid_spec=pltpu.PrefetchScalarGridSpec(
            num_scalar_prefetch=1,
            grid=(order.shape[0], tiles),
            in_specs=[whole(a) for a in resident]
            + [
                pl.BlockSpec((1, width, tile), lambda e, j, order: (order[e], 0, j)),
                pl.BlockSpec((1, width, tile), lambda e, j, order: (order[e], 0, tiles + j)),
                pl.BlockSpec((1, tile, width), lambda e, j, order: (order[e], j, 0)),
                pl.BlockSpec((1, RANK, total), lambda e, j, order: (order[e], 0, 0)),
            ],
            out_specs=[
                pl.BlockSpec((length, 2 * width + 128), lambda e, j, order: (0, 0), pipeline_mode=pl.Buffered(1)),
                pl.BlockSpec((length, 128), lambda e, j, order: (0, 0), pipeline_mode=pl.Buffered(1)),
                pl.BlockSpec((1, RANK, padded), lambda e, j, order: (order[e], 0, 0)),
            ],
            scratch_shapes=[
            pltpu.SMEM((2, experts + 1), jnp.int32),
            pltpu.VMEM((128, length), F32),
            pltpu.VMEM((128, length), F32),
            pltpu.VMEM((most + HALF, 2 * width + 128), BF),
            pltpu.VMEM((512, width), BF),
            pltpu.VMEM((512, width), BF),
            pltpu.VMEM((512, width), BF),
            pltpu.VMEM((512, 128), F32),
            pltpu.VMEM((512, width), F32),
            pltpu.VMEM((512, width), F32),
            pltpu.VMEM((512, 128), BF),
            pltpu.VMEM((512, 128), F32),
            pltpu.VMEM((512, 128), BF),
            pltpu.VMEM((512, 128), F32),
            pltpu.VMEM((128, width), BF),
            pltpu.VMEM((128, width), BF),
            pltpu.VMEM((256, 2 * width + 128), F32),
        ],
        ),
        compiler_params=pltpu.CompilerParams(vmem_limit_bytes=60 * MIB),
        name="experts_both_ways",
    )(order, *resident, w_gu, w_gu, w_dn, maps)


def gather_experts(weights, senders):
    w_gu, w_dn, gu_down, gu_up, dn_down, dn_up = weights
    maps = jnp.concatenate(
        [gu_down[0, 0].T, gu_down[0, 1].T, gu_up[0, 0], gu_up[0, 1], dn_down[0].T, dn_up[0]], axis=1
    )
    to = (senders[:, None] * RANK + jnp.arange(RANK)[None, :]).reshape(-1)
    rows = mm((to[:, None] == jnp.arange(128)[None, :]).astype(BF), maps).astype(BF)
    rows = rows.reshape(senders.shape[0], RANK, -1)
    return (
        lax.all_gather(w_gu, "expert", axis=0, tiled=True),
        lax.all_gather(w_dn, "expert", axis=0, tiled=True),
        lax.all_to_all(rows, "expert", split_axis=0, concat_axis=0, tiled=True),
    )


BOTH = ("dp", "expert")


def sum_expert_maps(compact, spread):
    copies = lax.axis_size("dp")
    experts, rank, columns = compact.shape
    each = columns // copies
    parts = compact.reshape(experts, rank, copies, each).transpose(2, 0, 1, 3).reshape(copies * experts, rank, each)
    got = lax.all_to_all(parts, BOTH, split_axis=0, concat_axis=0, tiled=True)
    own = mm(spread, got.reshape(-1, each)).astype(BF)
    return lax.all_gather(own, "dp", axis=1, tiled=True)


def sum_attention_maps(compact, spread):
    devices = lax.axis_size("dp") * lax.axis_size("expert")
    maps, rank, width = compact.shape
    cuts = devices // maps
    parts = compact.reshape(maps, rank, cuts, width // cuts).transpose(0, 2, 1, 3).reshape(devices, rank, width // cuts)
    got = lax.all_to_all(parts, BOTH, split_axis=0, concat_axis=0, tiled=True)
    own = mm(spread, got.reshape(devices * rank, width // cuts)).astype(BF)
    whole = lax.all_gather(own[None], BOTH, axis=0, tiled=True)
    return whole.reshape(maps, cuts, 128, width // cuts).transpose(0, 2, 1, 3).reshape(maps, 128, width).astype(F32)


def body(
    exchange,
    tokens, cotangent, attention_norm_gain, query_key_value_weight, attention_output_weight,
    adapter_attention_down_maps, adapter_query_key_value_up_maps, adapter_output_up_map,
    experts_norm_gain, router_weight, constant_expert_mixing, constant_expert_vectors,
    expert_gate_up_weight, expert_down_weight, adapter_expert_gate_up_down_maps, adapter_expert_gate_up_up_maps,
    adapter_expert_down_down_maps, adapter_expert_down_up_maps,
    routes, router_logits_carried, picture_span_starts, sequence_adapter_index,
):
    groups = lax.axis_size("expert")
    width = tokens.shape[1]
    hidden = expert_down_weight.shape[1]
    first = lax.axis_index("dp") * groups
    senders = lax.dynamic_slice_in_dim(sequence_adapter_index, first, groups, 0)
    spans = picture_span_starts.reshape(-1)
    own = (
        expert_gate_up_weight, expert_down_weight, adapter_expert_gate_up_down_maps,
        adapter_expert_gate_up_up_maps, adapter_expert_down_down_maps, adapter_expert_down_up_maps,
    )
    outs = attention_forward(
        tokens, attention_norm_gain, query_key_value_weight, adapter_attention_down_maps, adapter_query_key_value_up_maps,
        attention_output_weight, adapter_output_up_map, experts_norm_gain, router_weight.T, constant_expert_mixing.T,
        spans, sequence_adapter_index,
        (*own, cotangent, routes.T, router_logits_carried.T) if exchange else (),
    )
    xa, q, k, v, ob, ua, uo, lse, h1, xb, lin, wqk, down_s, up_s, wr = outs[:15]
    weights = outs[15:18] if exchange else gather_experts(own, senders)
    given = outs[20:22] if exchange else (lin, router_logits_carried.T)
    mixed, info, expert_maps = experts_both_ways(
        xb, cotangent, routes.T, *given, *weights, lax.axis_size("dp"), outs[18] if exchange else None
    )
    backward = functools.partial(
        attention_backward, weights[1].shape[0], spans, h1, tokens, attention_norm_gain, query_key_value_weight, wqk,
        attention_output_weight, down_s, up_s, xa, q, k, v, ob, ua, uo, lse,
        mixed, cotangent, lin, info, constant_expert_vectors, experts_norm_gain, wr,
    )
    if exchange:
        takers = jnp.repeat(sequence_adapter_index, RANK)[None]
        grad_tokens, result, all_e, all_a = backward(expert_maps, outs[19], takers)
        return (result, grad_tokens, *unpack(all_e, all_a, hidden))
    grad_tokens, result, attention_maps = backward()
    to = (sequence_adapter_index[:, None] * RANK + jnp.arange(RANK)[None, :]).reshape(-1)
    spread = (jnp.arange(128)[:, None] == to[None, :]).astype(BF)
    of_expert = sum_expert_maps(expert_maps, spread).astype(F32)
    of_attention = sum_attention_maps(attention_maps, spread)
    ends = [0, width, 2 * width, 2 * width + hidden, 2 * width + 2 * hidden, 2 * width + 3 * hidden, 3 * width + 3 * hidden]
    gud0, gud1, guu0, guu1, dnd, dnu = (of_expert[:, a:b] for a, b in zip(ends, ends[1:]))
    return (
        result,
        grad_tokens,
        of_attention[:4].transpose(0, 2, 1),
        of_attention[4:7],
        of_attention[7],
        jnp.stack([gud0.T, gud1.T])[None],
        jnp.stack([guu0, guu1])[None],
        dnd.T[None],
        dnu[None],
    )


def solution(mesh):
    tokens, own = P(("dp", "expert"), None), P("expert", None, None)
    own4 = P("expert", None, None, None)
    in_specs = (tokens, tokens) + (P(),) * 10 + (own, own, own4, own4, own, own) + (tokens,) * 3 + (P(),)
    out_specs = (tokens, tokens, P(), P(), P(), own4, own4, own, own)
    exchange = dict(mesh.shape) == {"dp": 8, "expert": 4}
    return jax.shard_map(functools.partial(body, exchange), mesh=mesh, in_specs=in_specs, out_specs=out_specs, check_vma=False)
```

```python
import functools

import jax
import jax.numpy as jnp
import numpy as np
from jax import lax
from jax.experimental import pallas as pl
from jax.experimental.pallas import tpu as pltpu
from jax.sharding import PartitionSpec as P

HEADS = 12
HD = 64
RANK = 16
PIC = 256
GROUP = 256
HALF = 512
EPS = 1e-06
NEG = -1e30
BF = jnp.bfloat16
F32 = jnp.float32
MIB = 1024 * 1024


def mm(a, b):
    return jnp.dot(a, b, preferred_element_type=F32)


def mm_t(a, b):
    return lax.dot_general(a, b, (((1,), (1,)), ((), ())), preferred_element_type=F32)


def t_mm(a, b):
    return lax.dot_general(a, b, (((0,), (0,)), ((), ())), preferred_element_type=F32)


def iota(shape, dim):
    return lax.broadcasted_iota(jnp.int32, shape, dim)


def one_hot(condition):
    return jnp.where(condition, 1.0, 0.0).astype(BF)


def picker(adapter, place, rows=128, columns=128):
    row, column = iota((rows, columns), 0), iota((rows, columns), 1)
    return one_hot((row - adapter * RANK == column - place * RANK) & (column // RANK == place))


def placer(adapter, place, rows=128, columns=128):
    row, column = iota((rows, columns), 0), iota((rows, columns), 1)
    return one_hot((column - adapter * RANK == row - place * RANK) & (row // RANK == place))


def head_order(back):
    row, column = iota((GROUP, GROUP), 0), iota((GROUP, GROUP), 1)
    a, b = (column, row) if back else (row, column)
    return one_hot(a == (b % 128 // 32) * 64 + b // 128 * 32 + b % 32)


def rope_tables(length):
    spacing = 10000.0 ** (-np.arange(0, HD, 2, dtype=np.float32) / np.float32(HD))
    angles = np.arange(length, dtype=np.float32)[:, None] * spacing.astype(np.float32)[None, :]
    angles = np.tile(angles, (1, 4))
    return np.cos(angles).astype(np.float32), np.sin(angles).astype(np.float32)


def rope(pair, cosine, sine):
    low, high = pair[:, :128], pair[:, 128:]
    return jnp.concatenate([low * cosine - high * sine, high * cosine + low * sine], axis=1)


def span_bias(start, transposed):
    a, b = iota((HALF, HALF), 0), iota((HALF, HALF), 1)
    query, key = (b, a) if transposed else (a, b)
    inside = (query >= start) & (query < start + PIC) & (key >= start) & (key < start + PIC)
    return jnp.where((key <= query) | inside, 0.0, NEG)


UNITS = 32
CHUNKS = ((0, 1), (1, 2), (3, 1), (4, 2))
EXTRA = ((0, 2), (2, 2))
MESH = pl.DeviceIdType.MESH


def other(index, step):
    return index + step - 2 * step * ((index // step) % 2)


def sending_steps(own, outs, scratch):
    adapters, w_gu, w_dn, gu_down, gu_up, dn_down, dn_up = own
    all_gu, all_dn, all_maps = outs
    bounce_gu, bounce_dn, compact, send, recv, local = scratch
    sources, targets, bounce = (w_gu, w_dn), (all_gu, all_dn), (bounce_gu, bounce_dn)
    dp, ex = lax.axis_index("dp"), lax.axis_index("expert")
    sibling, far = other(ex, 1), other(ex, 2)
    peers = {
        "x": (other(dp, 1), ex), "z": (other(dp, 2), ex), "y": (dp, far), "s": (dp, sibling), "d": (dp, other(far, 1)),
    }
    x, z = dp % 2, (dp // 2) % 2
    quarter = {"y": z * 2 + x, "x": z * 2 + 1 - x, "z": (1 - z) * 2 + x, "d": (1 - z) * 2 + 1 - x}
    kind = (x + z) % 2
    slots = {}
    for name in ("y", "x", "z", "d"):
        for chunk in CHUNKS:
            slots[name, chunk] = len(slots)
    for name in ("e", "o"):
        for chunk in EXTRA:
            slots[name, chunk] = len(slots)
    count = len(slots)
    started = []

    def views(refs, expert, key):
        name, (first, number) = key
        if name in quarter:
            first = quarter[name] * 6 + first
        else:
            first = 24 + 4 * (kind if name == "e" else 1 - kind) + first
        columns, rows = refs[0].shape[-1] // UNITS, refs[1].shape[-2] // UNITS
        return (
            refs[0].at[expert, :, pl.ds(pl.multiple_of(first * columns, columns), number * columns)],
            refs[1].at[expert, pl.ds(pl.multiple_of(first * rows, rows), number * rows), :],
        )

    def copies(source, target, peer, slot):
        for i in range(len(source())):
            number = len(started)

            def made(i=i, number=number):
                return pltpu.make_async_remote_copy(
                    src_ref=source()[i], dst_ref=target()[i], send_sem=send.at[number], recv_sem=recv.at[slot, i],
                    device_id=peers[peer], device_id_type=MESH,
                )

            made().start()
            started.append(made)

    def arrived(view, slot, i):
        pltpu.make_async_remote_copy(
            src_ref=view, dst_ref=view, send_sem=send.at[0], recv_sem=recv.at[slot, i],
            device_id=peers["s"], device_id_type=MESH,
        ).wait_recv()

    def begin():
        barrier = pltpu.get_barrier_semaphore()
        for peer in peers.values():
            pl.semaphore_signal(barrier, inc=1, device_id=peer, device_id_type=MESH)
        pl.semaphore_wait(barrier, len(peers))
        for name, chunks in (("y", CHUNKS), ("e", EXTRA)):
            for chunk in chunks:
                key = name, chunk
                copies(
                    functools.partial(views, sources, 0, key), functools.partial(views, targets, ex, key), "y", slots[key]
                )
        copies(lambda: [s.at[0] for s in sources], lambda: [t.at[ex] for t in targets], "s", 2 * count)
        for i in range(2):
            pltpu.make_async_copy(sources[i].at[0], bounce[i], local.at[i]).start()

    def select():
        row, column = iota((64, 128), 0), iota((64, 128), 1)
        first = sum(jnp.where(row // RANK == i, adapters[dp * 4 + i], 0) for i in range(4))
        rows = one_hot(column == first * RANK + row % RANK)
        width, hidden = gu_down.shape[2], dn_down.shape[1]
        parts = [
            (0, mm_t(rows, gu_down[0, 0])),
            (width, mm_t(rows, gu_down[0, 1])),
            (2 * width, mm(rows, gu_up[0, 0])),
            (2 * width + hidden, mm(rows, gu_up[0, 1])),
            (2 * width + 2 * hidden, mm_t(rows, dn_down[0])),
            (2 * width + 3 * hidden, mm(rows, dn_up[0])),
        ]
        for at, part in parts:
            for i in range(4):
                compact[i, :, pl.ds(at, part.shape[1])] = part[i * RANK : (i + 1) * RANK].astype(BF)

    def send_maps():
        for i, (peer, to) in enumerate((("s", sibling), ("y", far), ("d", other(far, 1)))):
            copies(lambda to=to: [compact.at[to]], lambda: [all_maps.at[ex]], peer, 2 * count + 1 + i)
        pltpu.make_async_copy(compact.at[ex], all_maps.at[ex], local.at[2]).start()

    def turn():
        for i in range(2):
            pltpu.make_async_copy(sources[i].at[0], bounce[i], local.at[i]).wait()
            pltpu.make_async_copy(bounce[i], targets[i].at[ex], local.at[i]).start()

    along_x = (CHUNKS[0], CHUNKS[3])

    def got(name, chunk):
        key = name, chunk
        to = []
        if name == "y":
            to = [("x", slots["x", chunk]), ("z", slots["z", chunk])]
        if name == "x" and chunk not in along_x:
            to = [("z", slots["d", chunk])]
        if name == "z" and chunk in along_x:
            to = [("x", slots["d", chunk])]
        if name == "e":
            to = [("x" if chunk == EXTRA[0] else "z", slots["o", chunk])]

        def step():
            mine = functools.partial(views, targets, far, key)
            for i in range(2):
                arrived(mine()[i], slots[key], i)
            for peer, slot in to:
                copies(mine, mine, peer, slot)
            copies(mine, mine, "s", count + slots[key])

        return step

    def change():
        for i in range(2):
            pltpu.make_async_copy(bounce[i], targets[i].at[ex], local.at[i]).wait()
            arrived(targets[i].at[sibling], 2 * count, i)
            pltpu.make_async_copy(targets[i].at[sibling], bounce[i], local.at[i]).start()
        pltpu.make_async_copy(compact.at[ex], all_maps.at[ex], local.at[2]).wait()
        arrived(all_maps.at[sibling], 2 * count + 1, 0)
        pltpu.make_async_copy(all_maps.at[sibling], compact.at[ex], local.at[2]).start()

    def changed():
        for i in range(2):
            pltpu.make_async_copy(targets[i].at[sibling], bounce[i], local.at[i]).wait()
        pltpu.make_async_copy(all_maps.at[sibling], compact.at[ex], local.at[2]).wait()

    def end():
        for made in started:
            made().wait_send()
        for i, source in enumerate((far, other(far, 1))):
            arrived(all_maps.at[source], 2 * count + 2 + i, 0)
        for key, slot in slots.items():
            view = views(targets, other(far, 1), key)
            for i in range(2):
                arrived(view[i], count + slot, i)

    c, e = CHUNKS, EXTRA
    return {
        "begin": [begin],
        "loaded": [select],
        "ready": [turn, got("y", c[0])],
        "projected": [got("x", c[0]), got("z", c[0]), got("y", c[1])],
        3: [got("y", c[2])],
        6: [got("z", c[1]), got("x", c[1])],
        8: [got("y", c[3]), got("d", c[0])],
        10: [got("x", c[2]), got("z", c[2])],
        "finished": [send_maps, got("z", c[3]), got("e", e[0])],
        200: [got("x", c[3])],
        "change": [change],
        "changed": [got("e", e[1]), got("d", c[1]), changed],
        212: [got("d", c[2])],
        "end": [got("o", e[0]), got("d", c[3]), got("o", e[1]), end],
    }


def attention_forward_kernel(exchange, *refs):
    spans, adapters, tok, gain_a, wqkv, down, up, wo, up_out, gain_m, router, mixing, cos, sin = refs[:14]
    refs = refs[14:]
    own = ()
    if exchange:
        own, refs = (adapters, *refs[:9]), refs[9:]
    xa_ref, q_ref, k_ref, v_ref, ob_ref, ua_ref, uo_ref, lse_ref, h1_ref, xb_ref, lin_ref, wqk_ref, down_ref, up_s, wr = refs[:15]
    refs = refs[15:]
    steps = {}
    if exchange:
        cot, routes, carried = own[-3:]
        own_outs, routing, refs = refs[:3], refs[5:7], refs[:5] + refs[7:]
        semaphores = refs[6:12]
        own_both, own_grads, bias = refs[3:6]
        bounce_gu, bounce_dn, compact = refs[6:9]
        x_s, c_s, dy_s, y_acc, ud_acc, dx_acc, dug_acc = refs[12:19]
        held, refs = refs[19:], ()
        loads = (tok, down, up, up_out, *own[3:7], wqkv, cos, sin, wo, cot)
        load = Staged(list(zip(loads, held)), held[-2])
        tok, down, up, up_out, *maps, wqkv, cos, sin, wo, cot = held[: len(loads)]
        outs = (xa_ref, q_ref, k_ref, v_ref, ob_ref, ua_ref, uo_ref, lse_ref, h1_ref, xb_ref, lin_ref, wqk_ref, down_ref, up_s, wr)
        kept_outs = held[len(loads) : len(loads) + len(outs)]
        info_t, place_t = held[len(loads) + len(outs) : len(loads) + len(outs) + 2]
        store = Staged(list(zip((*kept_outs, info_t, place_t), (*outs, *routing))), held[-1])
        xa_ref, q_ref, k_ref, v_ref, ob_ref, ua_ref, uo_ref, lse_ref, h1_ref, xb_ref, lin_ref, wqk_ref, down_ref, up_s, wr = kept_outs
        steps = sending_steps((*own[:3], *maps), own_outs, semaphores)
    else:
        (bias,) = refs
    length, width = tok.shape
    groups = width // GROUP
    adapter = adapters[lax.axis_index("dp") * lax.axis_size("expert") + lax.axis_index("expert")]

    def run(point):
        for step in steps.get(point, ()):
            step()

    run("begin")
    if exchange:
        load.start()
        load.wait()
        run("loaded")
    order = head_order(False)
    down_s = sum(mm(down[p], picker(adapter, p)) for p in range(3)).astype(BF)
    down_o = mm(down[3], picker(adapter, 0)).astype(BF)
    up_o = mm(placer(adapter, 0), up_out[...]).astype(BF)
    row, column = iota((128, router.shape[0]), 0), iota((128, router.shape[0]), 1)
    wr[...] = mm(one_hot(row == column), router[...]).astype(BF)
    row, column = iota((128, mixing.shape[0]), 0), iota((128, mixing.shape[0]), 1)
    wr[...] += mm(one_hot(row == column + router.shape[0]), mixing[...]).astype(BF)
    down_ref[0] = down_s
    down_ref[1] = down_o
    up_s[:, pl.ds(3 * width, width)] = up_o
    for p in range(3):
        rows = mm(placer(adapter, p), up[p]).astype(BF)
        for g in range(groups):
            block = rows[:, g * GROUP : (g + 1) * GROUP]
            if p < 2:
                block = mm(block, order).astype(BF)
            up_s[:, pl.ds(p * width + g * GROUP, GROUP)] = block
    for g in range(2 * groups):
        at = pl.ds(g * GROUP, GROUP)
        wqk_ref[:, at] = mm(wqkv[:, at], order).astype(BF)
    for half in range(length // HALF):
        bias[half] = span_bias(spans[half] - half * HALF, False)
    run("ready")

    def project(block, carry):
        at = pl.ds(pl.multiple_of(block * 512, 512), 512)
        h0 = tok[at, :].astype(F32)
        x = h0 * lax.rsqrt(jnp.mean(h0 * h0, axis=1, keepdims=True) + EPS) * gain_a[...][None]
        x = x.astype(BF)
        xa_ref[at, :] = x
        u = mm(x, down_s).astype(BF)
        ua_ref[at, :] = u
        c, s = cos[at, :], sin[at, :]
        for p, out in enumerate((q_ref, k_ref)):
            for g in range(groups):
                lanes = pl.ds(p * width + g * GROUP, GROUP)
                lin = mm(x, wqk_ref[:, lanes]) + mm(u, up_s[:, lanes])
                out[at, pl.ds(g * GROUP, GROUP)] = rope(lin, c, s).astype(BF)
        lanes = pl.ds(2 * width, width)
        v_ref[at, :] = (mm(x, wqkv[:, lanes]) + mm(u, up_s[:, lanes])).astype(BF)
        return carry

    lax.fori_loop(0, length // 512, project, 0)
    run("projected")

    lane = iota((1, GROUP), 1)
    lse_ref[...] = jnp.zeros(lse_ref.shape, F32)
    ob_f = ob_ref

    def attend(head, carry):
        g, h = head // 4, head % 4
        lanes = pl.ds(pl.multiple_of(g * GROUP, GROUP), GROUP)
        qk_own = jnp.where((lane % 128) // 32 == h, 1.0, 0.0).astype(BF)
        v_own = jnp.where(lane // 64 == h, 1.0, 0.0)
        kh = k_ref[:, lanes] * qk_own
        vh = v_ref[:, lanes] * v_own.astype(BF)
        for half in range(length // HALF):
            at = pl.ds(half * HALF, HALF)
            q = q_ref[at, lanes] * BF(0.125)
            keys = (half + 1) * HALF
            diag = mm_t(q, kh[half * HALF : keys]) + bias[half]
            top = jnp.max(diag, axis=1, keepdims=True)
            if half:
                past = mm_t(q, kh[: half * HALF])
                top = jnp.maximum(top, jnp.max(past, axis=1, keepdims=True))
            e = jnp.exp(diag - top)
            total = jnp.sum(e, axis=1, keepdims=True)
            o = mm(e.astype(BF), vh[half * HALF : keys])
            if half:
                e = jnp.exp(past - top)
                total = total + jnp.sum(e, axis=1, keepdims=True)
                o = o + mm(e.astype(BF), vh[: half * HALF])
            o = o * pl.reciprocal(total, approx=False)
            lse = top + jnp.log(total)
            lse_ref[at, :] = jnp.where(iota((1, 128), 1) == head, lse, lse_ref[at, :])
            old = jnp.where(v_own > 0.5, 0.0, ob_f[at, lanes].astype(F32))
            ob_f[at, lanes] = jnp.where(v_own > 0.5, o, old).astype(BF)
        for point in steps:
            if isinstance(point, int) and point < 100:
                pl.when(head == point)(functools.partial(run, point))
        return carry

    lax.fori_loop(0, HEADS, attend, 0)

    def finish(block, carry):
        at = pl.ds(pl.multiple_of(block * 512, 512), 512)
        o = ob_ref[at, :]
        u = mm(o, down_o).astype(BF)
        uo_ref[at, :] = u
        h1 = tok[at, :].astype(F32) + (mm(o, wo[...]) + mm(u, up_o))
        h1_ref[at, :] = h1
        x = h1 * lax.rsqrt(jnp.mean(h1 * h1, axis=1, keepdims=True) + EPS) * gain_m[...][None]
        x = x.astype(BF)
        xb_ref[at, :] = x
        lin_ref[at, :] = mm_t(x, wr[...])
        return carry

    lax.fori_loop(0, length // 512, finish, 0)
    if exchange:
        store.start(range(15))
        run("finished")
        ex = lax.axis_index("expert")
        hidden = bounce_dn.shape[0]
        rest = own_grads.shape[2] - 3 * width - 3 * hidden
        own_grads[:, :, 3 * width + 3 * hidden :] = jnp.zeros((2, RANK, rest), BF)
        route(lin_ref, carried, routes, carried.shape[0] - 4, info_t, place_t)
        store.start([15, 16])
        run(200)
        tile = 512
        kept = (y_acc, ud_acc, dx_acc, dug_acc)
        for which, expert in enumerate((ex, other(ex, 1))):
            rows = pl.ds(which * HALF, HALF)
            x, c, g, dy = take_rows(HALF, place_t[pl.ds(expert, 1), :], info_t[pl.ds(expert, 1), :], xb_ref, cot)
            x_s[...], c_s[...], dy_s[...] = x, c, dy
            if which:
                run("changed")
            a_gu = padded_rows(compact[ex, :, :width]) + padded_rows(compact[ex, :, width : 2 * width], RANK)
            b_dn = padded_rows(compact[ex, :, 2 * width + 3 * hidden :])
            ug, dud = mm_t(x, a_gu).astype(BF), mm_t(dy, b_dn).astype(BF)
            for ref in kept:
                ref[...] = jnp.zeros(ref.shape, F32)

            def one_tile(j, carry, which=which, ug=ug, dud=dud):
                at = pl.multiple_of(j * tile, tile)
                starts = [2 * width + i * hidden + at for i in range(3)]
                sums, parts = hidden_tile(
                    x_s[...], dy_s[...], ug, dud,
                    bounce_gu[:, pl.ds(at, tile)], bounce_gu[:, pl.ds(hidden + at, tile)], bounce_dn[pl.ds(at, tile), :],
                    padded_rows(compact[ex, :, pl.ds(starts[0], tile)]),
                    padded_rows(compact[ex, :, pl.ds(starts[1], tile)], RANK),
                    padded_rows(compact[ex, :, pl.ds(starts[2], tile)]),
                )
                for start, part in zip(starts, parts):
                    own_grads[which, :, pl.ds(start, tile)] = part
                for ref, value in zip(kept, sums):
                    ref[...] += value
                for point in steps:
                    if isinstance(point, int) and point > 200 + 10 * which and point < 210 + 10 * which:
                        pl.when(j == point - 201 - 10 * which)(functools.partial(run, point))
                return carry

            lax.fori_loop(0, hidden // tile, one_tile, 0)
            out, parts = close_rows(expert, [ref[...] for ref in kept], x_s[...], c_s[...], g, dy_s[...], a_gu, b_dn)
            if not which:
                run("change")
            own_both[rows, :width], own_both[rows, width : 2 * width], own_both[rows, 2 * width :] = out
            own_grads[which, :, :width], own_grads[which, :, width : 2 * width] = parts[:2]
            own_grads[which, :, 2 * width + 3 * hidden : 3 * width + 3 * hidden] = parts[2]
        store.wait()
    run("end")


def attention_forward(tok, gain_a, wqkv, down, up, wo, up_out, gain_m, router, mixing, spans, adapters, own=()):
    length, width = tok.shape
    cos, sin = rope_tables(length)
    shapes = [
        ((length, width), BF),
        ((length, width), BF),
        ((length, width), BF),
        ((length, width), BF),
        ((length, width), BF),
        ((length, 128), BF),
        ((length, 128), BF),
        ((length, 128), F32),
        ((length, width), F32),
        ((length, width), BF),
        ((length, 128), F32),
        ((width, 2 * width), BF),
        ((2, width, 128), BF),
        ((128, 4 * width), BF),
        ((128, width), BF),
    ]
    vmem, smem = pl.BlockSpec(memory_space=pltpu.VMEM), pl.BlockSpec(memory_space=pltpu.SMEM)
    anys = pl.BlockSpec(memory_space=pl.ANY)
    in_specs, out_specs = [smem, smem] + [vmem] * 12, [vmem] * len(shapes)
    scratch = [pltpu.VMEM((length // HALF, HALF, HALF), F32)]
    params = dict(vmem_limit_bytes=62 * MIB)
    args = (spans, adapters, tok, gain_a, wqkv, down, up, wo, up_out, gain_m, router, mixing, cos, sin)
    if own:
        w_gu, w_dn = own[:2]
        columns = 3 * width + 3 * w_dn.shape[1]
        in_specs = [smem, smem] + [vmem if i in (1, 7, 8, 9) else anys for i in range(12)]
        in_specs += [anys] * 7 + [vmem] * 2
        args += own
        held = [args[i] for i in (2, 5, 6, 8, 16, 17, 18, 19, 4, 12, 13, 7, 20)]
        held = [pltpu.VMEM(a.shape, a.dtype) for a in held] + [pltpu.VMEM(a, t) for a, t in shapes]
        padded = -(-columns // 1024) * 1024
        shapes += [
            ((4, *w_gu.shape[1:]), BF),
            ((4, *w_dn.shape[1:]), BF),
            ((4, RANK, columns), BF),
            ((2 * HALF, 2 * width + 128), BF),
            ((2, RANK, padded), BF),
            ((128, length), F32),
            ((128, length), F32),
        ]
        held += [pltpu.VMEM(a, t) for a, t in shapes[-2:]]
        out_specs = [anys] * (len(out_specs) + 3) + [vmem] * 2 + [anys] * 2
        scratch += [
            pltpu.VMEM(w_gu.shape[1:], BF),
            pltpu.VMEM(w_dn.shape[1:], BF),
            pltpu.VMEM((4, RANK, columns), BF),
            pltpu.SemaphoreType.DMA((96,)),
            pltpu.SemaphoreType.DMA((48, 2)),
            pltpu.SemaphoreType.DMA((3,)),
            pltpu.VMEM((HALF, width), BF),
            pltpu.VMEM((HALF, width), BF),
            pltpu.VMEM((HALF, width), BF),
            pltpu.VMEM((HALF, width), F32),
            pltpu.VMEM((HALF, 128), F32),
            pltpu.VMEM((HALF, width), F32),
            pltpu.VMEM((HALF, 128), F32),
        ]
        scratch += held + [pltpu.SemaphoreType.DMA((16,)), pltpu.SemaphoreType.DMA((20,))]
        params.update(collective_id=0, has_side_effects=True)
    return pl.pallas_call(
        functools.partial(attention_forward_kernel, bool(own)),
        out_shape=[jax.ShapeDtypeStruct(s, t) for s, t in shapes],
        in_specs=in_specs,
        out_specs=out_specs,
        scratch_shapes=scratch,
        compiler_params=pltpu.CompilerParams(**params),
        name="attention_forward",
    )(*args)


class Staged:
    def __init__(self, pairs, sems):
        self.pairs, self.sems = pairs, sems

    def copy(self, i):
        return pltpu.make_async_copy(self.pairs[i][0], self.pairs[i][1], self.sems.at[i])

    def start(self, numbers=None):
        for i in range(len(self.pairs)) if numbers is None else numbers:
            self.copy(i).start()

    def wait(self, numbers=None):
        for i in range(len(self.pairs)) if numbers is None else numbers:
            self.copy(i).wait()


class Mail:
    def __init__(self, send, recv):
        self.send, self.recv, self.started = send, recv, []

    def post(self, source, target, peer, slot, when=None):
        number = len(self.started)

        def made():
            return pltpu.make_async_remote_copy(
                src_ref=source(), dst_ref=target(), send_sem=self.send.at[number],
                recv_sem=self.recv.at[slot() if callable(slot) else slot],
                device_id=peer, device_id_type=MESH,
            )

        self.only(when, lambda: made().start())
        self.started.append((made, when))

    def only(self, when, do):
        if when is None:
            do()
        else:
            pl.when(when())(do)

    def arrived(self, view, slot, peer):
        pltpu.make_async_remote_copy(
            src_ref=view, dst_ref=view, send_sem=self.send.at[0], recv_sem=self.recv.at[slot],
            device_id=peer, device_id_type=MESH,
        ).wait_recv()

    def finish(self):
        for made, when in self.started:
            self.only(when, lambda made=made: made().wait_send())


def meet(peers):
    barrier = pltpu.get_barrier_semaphore()
    for peer in peers:
        pl.semaphore_signal(barrier, inc=1, device_id=peer, device_id_type=MESH)
    pl.semaphore_wait(barrier, len(peers))


def summing_steps(refs, grad_maps):
    maps_in, own_maps, takers, all_e, all_a, e_got, e_two, e_own, a_in, a_part, a_z, a_own, send, recv, local = refs
    mail = Mail(send, recv)
    dp, ex = lax.axis_index("dp"), lax.axis_index("expert")
    x, z = dp % 2, dp // 2
    share = e_two.shape[3]
    group = {k: (ex + k) % 4 for k in range(1, 4)}
    later = {k: (z + k) % 4 for k in range(1, 4)}
    along = {k: (dp + k) % 8 for k in range(1, 8)}
    along_z = {k: ((z + k) % 4) * 2 + x for k in range(1, 4)}
    plane = {(a, k): (other(dp, 1) if a else dp, (ex + k) % 4) for a in range(2) for k in range(4) if (a, k) != (0, 0)}
    x_peer, y_peer, s_peer = (other(dp, 1), ex), (dp, other(ex, 2)), (dp, other(ex, 1))
    others = (other(ex, 1), other(ex, 2), other(other(ex, 1), 2))
    spots = {(up, k): ((z + 4 - k) if up else (z + k)) % 4 for up in (True, False) for k in range(1, 4)}
    reach = {(up, k): (z >= k) if up else (z + k < 4) for up in (True, False) for k in range(1, 4)}
    above, below = (((z + 1) % 4) * 2 + x, ex), (((z + 3) % 4) * 2 + x, ex)
    near = 2 * (ex // 2)
    away = 2 - near
    free = [0]

    def slots(n):
        free[0] += n
        return free[0] - n

    first = {n: slots(c) for n, c in dict(e1=4, e2=8, e5=8, e3=4, e4=4, a1=8, a2=4, a3=4, ay=2, ax=1, a_s=4).items()}

    def begin():
        meet([(dp, group[k]) for k in group] + [(along[k], ex) for k in along] + [plane[1, k] for k in range(1, 4)])
        for i, to in enumerate(others):
            mail.post(
                lambda i=i, to=to: maps_in.at[to] if i else own_maps.at[1], lambda: e_got.at[ex], (dp, to), first["e1"] + i
            )
        pltpu.make_async_copy(own_maps.at[0], e_got.at[ex], local.at[0]).start()

    def columns(refs, pair, to):
        return refs.at[pl.ds(pair, 2), :, pl.ds(pl.multiple_of(to * share, 128), share)]

    def spread_out(pair, slot):
        for k, to in along.items():
            mail.post(
                lambda to=to: columns(e_got, pair, to), lambda: e_two.at[dp, pl.ds(pair, 2)], (to, ex), first[slot] + k
            )
        e_two[dp, pl.ds(pair, 2)] = e_got[pl.ds(pair, 2), :, pl.ds(pl.multiple_of(dp * share, 128), share)]

    def spread_near():
        mail.arrived(e_got.at[others[0]], first["e1"], s_peer)
        pltpu.make_async_copy(own_maps.at[0], e_got.at[ex], local.at[0]).wait()
        spread_out(near, "e2")

    def spread_far():
        for i in (1, 2):
            mail.arrived(e_got.at[others[i]], first["e1"] + i, (dp, others[i]))
        spread_out(away, "e5")

    def placed(sender, columns):
        row, column = iota((128, columns), 0), iota((128, columns), 1)
        return one_hot(row - sender * RANK == column % RANK)

    def add_up():
        for k in along:
            source = (dp + 8 - k) % 8
            mail.arrived(e_two.at[source, pl.ds(near, 2)], first["e2"] + k, (source, ex))
            mail.arrived(e_two.at[source, pl.ds(away, 2)], first["e5"] + k, (source, ex))
        rows = e_two[...].reshape(-1, share)
        e_own[...] = mm(placed(takers[...], rows.shape[0]), rows).astype(BF)
        mail.post(lambda: e_own, lambda: all_e.at[dp], above, lambda: first["e3"] + z, lambda: z < 3)
        mail.post(lambda: e_own, lambda: all_e.at[dp], below, lambda: first["e3"] + z, lambda: z > 0)
        mail.post(lambda: e_own, lambda: all_e.at[dp], x_peer, lambda: first["e4"] + z)
        pltpu.make_async_copy(e_own, all_e.at[dp], local.at[1]).start()

    def e_forward(k):
        for up in (True, False):
            here = reach[up, k]
            place = spots[up, k]

            def take(place=place):
                mail.arrived(all_e.at[place * 2 + x], first["e3"] + place, (place * 2 + x, ex))

            def view(place=place):
                return all_e.at[place * 2 + x]

            mail.only(lambda here=here: here, take)
            if up:
                mail.post(
                    view, view, above, lambda place=place: first["e3"] + place, lambda here=here: here & (z < 3)
                )
            else:
                mail.post(
                    view, view, below, lambda place=place: first["e3"] + place, lambda here=here: here & (z > 0)
                )
            mail.post(view, view, x_peer, lambda place=place: first["e4"] + place, lambda here=here: here)

    def a_share():
        for (a, k), to in plane.items():
            number = 2 * to[1] + to[0] % 2
            mail.post(
                lambda number=number: grad_maps.at[number], lambda: a_in.at[x * 4 + ex], to, first["a1"] + a * 4 + k
            )
        a_in[x * 4 + ex] = grad_maps[2 * ex + x]

    def a_partial():
        for a, k in plane:
            source = (other(dp, 1) if a else dp, (ex + 4 - k) % 4)
            at = (source[0] % 2) * 4 + source[1]
            mail.arrived(a_in.at[at], first["a1"] + a * 4 + k, source)
        rows = a_in[...].reshape(128, -1)
        senders = takers[:, pl.ds(pl.multiple_of(z * 128, 128), 128)]
        a_part[...] = mm(placed(senders, 128), rows).astype(BF)
        for k, to in later.items():
            mail.post(
                lambda to=to: a_part.at[pl.ds(pl.multiple_of(to * 32, 32), 32)], lambda: a_z.at[z],
                (along_z[k], ex), first["a2"] + k,
            )
        a_z[z] = a_part[pl.ds(pl.multiple_of(z * 32, 32), 32), :]

    def piece(number, place):
        return all_a.at[number, pl.ds(pl.multiple_of(place * 32, 32), 32)]

    mine = 2 * ex + x

    def a_total():
        for k in range(1, 4):
            source = (z + 4 - k) % 4
            mail.arrived(a_z.at[source], first["a2"] + k, (source * 2 + x, ex))
        a_own[...] = sum(a_z[i].astype(F32) for i in range(4)).astype(BF)
        for k in range(1, 4):
            mail.post(lambda: a_own, lambda: piece(mine, z), (along_z[k], ex), first["a3"] + k)
        pltpu.make_async_copy(a_own, piece(mine, z), local.at[2]).start()

    def a_gather():
        pltpu.make_async_copy(a_own, piece(mine, z), local.at[2]).wait()
        for k in range(1, 4):
            source = (z + 4 - k) % 4
            mail.arrived(piece(mine, source), first["a3"] + k, (source * 2 + x, ex))

        def send(number, peer, slot):
            here = functools.partial(lambda number: all_a.at[number], number)
            mail.post(here, here, peer, slot)

        of_y, of_x = 2 * other(ex, 2) + x, 2 * ex + 1 - x
        of_xy = 2 * other(ex, 2) + 1 - x
        send(mine, x_peer, first["ax"])
        send(mine, y_peer, first["ay"])
        send(mine, s_peer, first["a_s"])
        mail.arrived(all_a.at[of_x], first["ax"], x_peer)
        send(of_x, y_peer, first["ay"] + 1)
        send(of_x, s_peer, first["a_s"] + 1)
        mail.arrived(all_a.at[of_y], first["ay"], y_peer)
        send(of_y, s_peer, first["a_s"] + 2)
        mail.arrived(all_a.at[of_xy], first["ay"] + 1, y_peer)
        send(of_xy, s_peer, first["a_s"] + 3)

    def end():
        sib = other(ex, 1)
        numbers = (2 * sib + x, 2 * sib + 1 - x, 2 * other(sib, 2) + x, 2 * other(sib, 2) + 1 - x)
        for i, number in enumerate(numbers):
            mail.arrived(all_a.at[number], first["a_s"] + i, s_peer)
        for k in range(4):
            mail.arrived(all_e.at[2 * k + 1 - x], first["e4"] + k, x_peer)
        pltpu.make_async_copy(e_own, all_e.at[dp], local.at[1]).wait()
        mail.finish()

    return {
        "begin": [begin], "outer": [spread_near], 1: [spread_far], 6: [add_up], 9: [functools.partial(e_forward, 1)],
        "maps": [a_share], 101: [functools.partial(e_forward, 2)], 102: [a_partial],
        "end": [a_total, functools.partial(e_forward, 3), a_gather, end],
    }


def attention_backward_kernel(exchange, numbers, *refs):
    spans, h1_ref, tok, gain_a, wqkv, wqk, wo, down_ref, up_s, cos, sin = refs[:11]
    xa_ref, q_ref, k_ref, v_ref, ob_ref, ua_ref, uo_ref, lse_ref = refs[11:19]
    mixed, cot, lin_ref, info, vectors, gain_m, wr = refs[19:26]
    steps = {}
    if exchange:
        grad_out, result_out, grad_maps, own = refs[29], refs[30], refs[33], refs[46:]
        dh1_ref, bias, dob, datt, duo, lse_t, center_t, dq, dk, dv, dlin, dua = refs[34:46]
        own, held = own[:10], own[10:]
        width = wo.shape[0]
        loads = (
            up_s, wo, down_ref, ob_ref, lse_ref, lin_ref, info, wr, q_ref, k_ref, v_ref, cos, sin, ua_ref, xa_ref, uo_ref,
            wqk, wqkv.at[:, pl.ds(2 * width, width)], tok,
        )
        grad_tok, result = held[19:21]
        pairs = [
            (h1_ref, dq), (mixed, dlin.at[:, pl.ds(0, mixed.shape[1])]), (cot, grad_tok), *zip(loads, held),
            (grad_tok, grad_out), (result, result_out),
        ]
        load = Staged(pairs, held[21])
        h1_ref, mixed, cot = dq, dlin, grad_tok
        (
            up_s, wo, down_ref, ob_ref, lse_ref, lin_ref, info, wr, q_ref, k_ref, v_ref, cos, sin, ua_ref, xa_ref, uo_ref,
            wqk, wv, tok,
        ) = held[:19]
        steps = summing_steps((*refs[26:29], *refs[31:33], *own), grad_maps)
    else:
        grad_tok, result, grad_maps = refs[26:29]
        wv = wqkv.at[:, pl.ds(2 * wo.shape[0], wo.shape[0])]
        dh1_ref, bias, dob, datt, duo, lse_t, center_t, dq, dk, dv, dlin, dua = refs[29:]
    length, width = tok.shape
    groups = width // GROUP

    def run(point):
        for step in steps.get(point, ()):
            step()

    run("begin")
    if exchange:
        load.start(range(22))
    for half in range(length // HALF):
        bias[half] = span_bias(spans[half] - half * HALF, True)
    if exchange:
        load.wait(range(11))
    of_head = one_hot(iota((128, width), 1) // HD == iota((128, width), 0))

    def outer(block, carry):
        at = pl.ds(pl.multiple_of(block * 256, 256), 256)
        h1 = h1_ref[at, :]
        g = info[at, :]
        lane = iota((1, 128), 1)
        kinds = numbers + 4
        ct = cot[at, :].astype(F32)
        r = lax.rsqrt(jnp.mean(h1 * h1, axis=1, keepdims=True) + EPS)
        gain = gain_m[...][None]
        n2 = h1 * r * gain
        lin = lin_ref[at, :]
        gc = g[:, numbers + 1 : numbers + 2]
        g_fix = [g[:, numbers + 2 + i : numbers + 3 + i] for i in range(2)]
        mixes = []
        for i in range(2):
            a, b = lin[:, kinds + 2 * i : kinds + 2 * i + 1], lin[:, kinds + 2 * i + 1 : kinds + 2 * i + 2]
            top = jnp.maximum(a, b)
            a, b = jnp.exp(a - top), jnp.exp(b - top)
            mixes.append((a / (a + b), b / (a + b)))
        vecs = [vectors[i : i + 1, :] for i in range(2)]
        to_n2 = gc + g_fix[0] * mixes[0][0] + g_fix[1] * mixes[1][0]
        out = h1 + mixed[at, :width].astype(F32) + to_n2 * n2
        out = out + (g_fix[0] * mixes[0][1]) * vecs[0] + (g_fix[1] * mixes[1][1]) * vecs[1]
        result[at, :] = out.astype(BF)
        a = jnp.sum(ct * n2, axis=1, keepdims=True)
        bs = [jnp.sum(ct * v, axis=1, keepdims=True) for v in vecs]
        packed = mixed[at, 2 * width : 2 * width + 128].astype(F32)
        dg = jnp.where(lane < numbers, packed + pltpu.roll(packed, 64, 1), 0.0)
        dg = jnp.where(lane == numbers + 1, a, dg)
        for i in range(2):
            dg = jnp.where(lane == numbers + 2 + i, mixes[i][0] * a + mixes[i][1] * bs[i], dg)
        g = jnp.where(lane < kinds, g, 0.0)
        dlin = g * (dg - jnp.sum(g * dg, axis=1, keepdims=True))
        for i in range(2):
            pull = mixes[i][0] * mixes[i][1] * (g_fix[i] * (a - bs[i]))
            dlin = jnp.where(lane == kinds + 2 * i, pull, jnp.where(lane == kinds + 2 * i + 1, -pull, dlin))
        high, low = split(dlin)
        dn2 = mixed[at, width : 2 * width].astype(F32) + (mm(high, wr[...]) + mm(low, wr[...])) + ct * to_n2
        dn2 = dn2 * gain
        back = r * dn2 - h1 * (r * r * r * jnp.mean(dn2 * h1, axis=1, keepdims=True))
        dh1 = ct + back
        dh1_ref[at, :] = dh1
        d = dh1.astype(BF)
        datt[at, :] = d
        u = mm_t(d, up_s[:, pl.ds(3 * width, width)]).astype(BF)
        duo[at, :] = u
        do = (mm_t(d, wo[...]) + mm_t(u, down_ref[1])).astype(BF)
        dob[at, :] = do
        both = do.astype(F32) * ob_ref[at, :].astype(F32)
        high = both.astype(BF)
        low = (both - high.astype(F32)).astype(BF)
        center_t[:, at] = mm_t(of_head, high) + mm_t(of_head, low)
        lse_t[:, at] = lse_ref[at, :].T
        if steps:
            pl.when(block == 0)(functools.partial(run, "outer"))
        return carry

    lax.fori_loop(0, length // 256, outer, 0)
    if exchange:
        load.start([23])
        load.wait(range(11, 14))
    dq[...] = jnp.zeros(dq.shape, F32)
    dk[...] = jnp.zeros(dk.shape, F32)
    dv[...] = jnp.zeros(dv.shape, F32)
    lane = iota((1, GROUP), 1)

    def attend(head, carry):
        g, h = head // 4, head % 4
        lanes = pl.ds(pl.multiple_of(g * GROUP, GROUP), GROUP)
        qk_own = jnp.where((lane % 128) // 32 == h, 1.0, 0.0).astype(BF)
        v_own = jnp.where(lane // 64 == h, 1.0, 0.0).astype(BF)
        lse = lse_t[pl.ds(head, 1), :]
        center = center_t[pl.ds(head, 1), :]
        for half in range(length // HALF):
            at = pl.ds(half * HALF, HALF)
            late = pl.ds(half * HALF, length - half * HALF)
            kh = k_ref[at, lanes] * qk_own
            vh = v_ref[at, lanes] * v_own
            q = q_ref[late, lanes] * BF(0.125)
            do = dob[late, lanes]
            s = mm_t(kh, q) - lse[:, half * HALF :]
            if half * HALF + HALF < length:
                s = jnp.concatenate([s[:, :HALF] + bias[half], s[:, HALF:]], axis=1)
            else:
                s = s + bias[half]
            prob = jnp.exp(s)
            dp = mm_t(vh, do)
            ds = (prob * (dp - center[:, half * HALF :])).astype(BF)
            dv[at, lanes] += mm(prob.astype(BF), do * v_own)
            dk[at, lanes] += mm(ds, q * qk_own)
            dq[late, lanes] += t_mm(ds, kh)
        for point in steps:
            if isinstance(point, int) and point < 100:
                pl.when(head == point)(functools.partial(run, point))
        return carry

    lax.fori_loop(0, HEADS, attend, 0)
    if exchange:
        load.wait(range(14, 22))

    def turn_back(block, carry):
        at = pl.ds(pl.multiple_of(block * 256, 256), 256)
        c, s = cos[at, :], -sin[at, :]
        for g in range(groups):
            lanes = pl.ds(g * GROUP, GROUP)
            dlin[at, lanes] = rope(dq[at, lanes] * 0.125, c, s).astype(BF)
            dlin[at, pl.ds(width + g * GROUP, GROUP)] = rope(dk[at, lanes], c, s).astype(BF)
        dlin[at, pl.ds(2 * width, width)] = dv[at, :].astype(BF)
        dua[at, :] = mm_t(dlin[at, :], up_s[:, pl.ds(0, 3 * width)]).astype(BF)
        return carry

    lax.fori_loop(0, length // 256, turn_back, 0)
    order = head_order(True)
    grads = t_mm(dua[...], xa_ref[...]).astype(BF)
    for p in range(3):
        grad_maps[p] = grads[p * RANK : (p + 1) * RANK]
    grad_maps[3] = t_mm(duo[...], ob_ref[...]).astype(BF)[:RANK]
    for p in range(3):
        grads = t_mm(ua_ref[...], dlin[:, pl.ds(p * width, width)]).astype(BF)[p * RANK : (p + 1) * RANK]
        if p < 2:
            grads = jnp.concatenate(
                [mm(grads[:, g * GROUP : (g + 1) * GROUP], order) for g in range(groups)], axis=1
            ).astype(BF)
        grad_maps[4 + p] = grads
    grad_maps[7] = t_mm(uo_ref[...], datt[...]).astype(BF)[:RANK]
    run("maps")

    def inner(block, carry):
        at = pl.ds(pl.multiple_of(block * 256, 256), 256)
        d, u = dlin[at, :], dua[at, :]
        dx = mm_t(d[:, : 2 * width], wqk[...]) + mm_t(d[:, 2 * width :], wv[...])
        dx = (dx + mm_t(u, down_ref[0])) * gain_a[...][None]
        h0 = tok[at, :].astype(F32)
        r = lax.rsqrt(jnp.mean(h0 * h0, axis=1, keepdims=True) + EPS)
        pull = r * dx - h0 * (r * r * r * jnp.mean(dx * h0, axis=1, keepdims=True))
        grad_tok[at, :] = (dh1_ref[at, :] + pull).astype(BF)
        for point in steps:
            if isinstance(point, int) and point >= 100:
                pl.when(block == point - 100)(functools.partial(run, point))
        return carry

    lax.fori_loop(0, length // 256, inner, 0)
    if exchange:
        load.start([22])
    run("end")
    if exchange:
        load.wait([22, 23])


def attention_backward(
    numbers, spans, h1, tok, gain_a, wqkv, wqk, wo, down_s, up_s, xa, q, k, v, ob, ua, uo, lse,
    mixed, cot, lin, info, vectors, gain_m, wr, maps=None, own_maps=None, takers=None,
):
    length, width = tok.shape
    cos, sin = rope_tables(length)
    vmem, smem = pl.BlockSpec(memory_space=pltpu.VMEM), pl.BlockSpec(memory_space=pltpu.SMEM)
    anys = pl.BlockSpec(memory_space=pl.ANY)
    args = (
        spans, h1, tok, gain_a, wqkv, wqk, wo, down_s, up_s, cos, sin, xa, q, k, v, ob, ua, uo, lse,
        mixed, cot, lin, info, vectors, gain_m, wr,
    )
    in_specs = [smem] + [vmem] * 25
    compact = ((8, RANK, width), BF)
    shapes, out_specs, scratch = [((length, width), BF)] * 2, [vmem] * 2, []
    if maps is None:
        shapes.append(compact)
        out_specs.append(vmem)
    else:
        share = maps.shape[2] // 8
        in_specs = [smem] + [vmem if a.size < 2048 else anys for a in args[1:]] + [anys, anys, vmem]
        held = [up_s, wo, down_s, ob, lse, lin, info, wr, q, k, v, cos, sin, ua, xa, uo, wqk, wo, tok, tok, tok]
        held = [pltpu.VMEM(a.shape, a.dtype) for a in held]
        args += (maps, own_maps, takers)
        out_specs = [anys] * 2
        shapes += [((8, 128, share), BF), ((8, 128, width), BF)]
        out_specs += [anys] * 2
        scratch.append(compact)
    scratch += [
        ((length, width), F32),
        ((length // HALF, HALF, HALF), F32),
        ((length, width), BF),
        ((length, width), BF),
        ((length, 128), BF),
        ((128, length), F32),
        ((128, length), F32),
        ((length, width), F32),
        ((length, width), F32),
        ((length, width), F32),
        ((length, 3 * width), BF),
        ((length, 128), BF),
    ]
    params = dict(vmem_limit_bytes=62 * MIB)
    semaphores = []
    if maps is not None:
        scratch += [
            (maps.shape, BF),
            ((8, 4, RANK, share), BF),
            ((128, share), BF),
            ((8, RANK, width), BF),
            ((128, width), BF),
            ((4, 32, width), BF),
            ((32, width), BF),
        ]
        semaphores = [pltpu.SemaphoreType.DMA((64,)), pltpu.SemaphoreType.DMA((64,)), pltpu.SemaphoreType.DMA((3,))]
        semaphores += [*held, pltpu.SemaphoreType.DMA((24,))]
        params.update(collective_id=1, has_side_effects=True)
    return pl.pallas_call(
        functools.partial(attention_backward_kernel, maps is not None, numbers),
        out_shape=[jax.ShapeDtypeStruct(s, t) for s, t in shapes],
        in_specs=in_specs,
        out_specs=out_specs,
        scratch_shapes=[pltpu.VMEM(s, t) for s, t in scratch] + semaphores,
        compiler_params=pltpu.CompilerParams(**params),
        name="attention_backward",
    )(*args)


def unpack_kernel(all_e, all_a, a_attention, b_qkv, b_out, a_gate_up, b_gate_up, a_down, b_down):
    width, hidden, share = b_out.shape[1], a_down.shape[1], all_e.shape[2]
    for p in range(4):
        a_attention[p] = all_a[p].astype(F32).T
    for p in range(3):
        b_qkv[p] = all_a[4 + p].astype(F32)
    b_out[...] = all_a[7].astype(F32)

    def pieces(start, number):
        at = start
        while at < start + number:
            stop = min(start + number, (at // share + 1) * share)
            part = all_e[at // share, :, at % share : at % share + stop - at]
            yield at - start, part.astype(F32)
            at = stop

    for p in range(2):
        for at, part in pieces(p * width, width):
            a_gate_up[0, p, pl.ds(at, part.shape[1]), :] = part.T
        for at, part in pieces(2 * width + p * hidden, hidden):
            b_gate_up[0, p, :, pl.ds(at, part.shape[1])] = part
    for at, part in pieces(2 * width + 2 * hidden, hidden):
        a_down[0, pl.ds(at, part.shape[1]), :] = part.T
    for at, part in pieces(2 * width + 3 * hidden, width):
        b_down[0, :, pl.ds(at, part.shape[1])] = part


def unpack(all_e, all_a, hidden):
    width = all_a.shape[2]
    shapes = [
        (4, width, 128), (3, 128, width), (128, width),
        (1, 2, width, 128), (1, 2, 128, hidden), (1, hidden, 128), (1, 128, width),
    ]
    return pl.pallas_call(
        unpack_kernel,
        out_shape=[jax.ShapeDtypeStruct(s, F32) for s in shapes],
        in_specs=[pl.BlockSpec(memory_space=pltpu.VMEM)] * 2,
        out_specs=[pl.BlockSpec(memory_space=pltpu.VMEM)] * 7,
        compiler_params=pltpu.CompilerParams(vmem_limit_bytes=40 * MIB),
        name="unpack",
    )(all_e, all_a)


def split(x):
    high = x.astype(BF)
    return high, (x - high.astype(F32)).astype(BF)


def route(lin_ref, carried, routes, numbers, info_t, place_t):
    kinds, length = carried.shape
    target = iota((kinds, length), 0)
    logits = lin_ref[...].T[:kinds] + carried[...]
    picks = [target == routes[k : k + 1, :] for k in range(2)]
    chosen = [jnp.sum(jnp.where(p, logits, 0.0), axis=0, keepdims=True) for p in picks]
    top = jnp.maximum(*chosen)
    parts = [jnp.exp(c - top) for c in chosen]
    total = parts[0] + parts[1]
    info_t[...] = jnp.zeros(info_t.shape, F32)
    info_t[:kinds, :] = jnp.where(picks[0], parts[0] / total, jnp.where(picks[1], parts[1] / total, 0.0))
    wide = iota((128, length), 0)
    named = [(wide == routes[k : k + 1, :]) & (wide < numbers) for k in range(2)]
    member = one_hot(named[0] | named[1])
    for block in range(length // 256):
        before = one_hot(iota((256, length), 1) < iota((256, length), 0) + block * 256)
        place_t[:, pl.ds(block * 256, 256)] = mm_t(member, before)
    place_t[...] = jnp.where(named[0] | named[1], place_t[...], -1.0)


def padded_rows(part, before=0):
    columns = part.shape[1]
    parts = [jnp.zeros((before, columns), BF), part, jnp.zeros((128 - RANK - before, columns), BF)]
    return jnp.concatenate(parts if before else parts[1:], axis=0)


def take_rows(n, places, gates, xb, cot):
    own = iota((n, xb.shape[0]), 0).astype(F32) == places
    taken = one_hot(own)
    x = mm(taken, xb[...]).astype(BF)
    c = mm(taken, cot[...]).astype(BF)
    g = jnp.sum(jnp.where(own, gates, 0.0), axis=1, keepdims=True)
    return x, c, g, (g * c.astype(F32)).astype(BF)


def hidden_tile(x, dy, ug, dud, w_gate, w_up, w_down, b_gate, b_up, a_dn):
    gate = mm(x, w_gate) + mm(ug, b_gate)
    up = mm(x, w_up) + mm(ug, b_up)
    sig = 1.0 / (1.0 + jnp.exp(-gate))
    act = gate * sig
    hid = (act * up).astype(BF)
    dhid = mm_t(dy, w_down) + mm(dud, a_dn)
    dup = (dhid * act).astype(BF)
    dgate = (dhid * up * (sig + act * (1.0 - sig))).astype(BF)
    y = mm(hid, w_down)
    ud = mm_t(hid, a_dn)
    dx = mm_t(dgate, w_gate) + mm_t(dup, w_up)
    dug = mm_t(dgate, b_gate) + mm_t(dup, b_up)
    ug_t = ug.T
    grads = mm(ug_t[:RANK], dgate), mm(ug_t[RANK : 2 * RANK], dup), mm(dud.T[:RANK], hid)
    return (y, ud, dx, dug), [g.astype(BF) for g in grads]


def close_rows(expert, sums, x, c, g, dy, a_gu, b_dn):
    y, ud, dx, dug = sums
    ud, dug = ud.astype(BF), dug.astype(BF)
    y = y + mm(ud, b_dn)
    high, low = split(jnp.sum(c.astype(F32) * y.astype(BF).astype(F32), axis=1, keepdims=True))
    lane = iota((1, 128), 1)
    high, low = high.astype(F32), low.astype(F32)
    both = (
        (g * y).astype(BF),
        (dx + mm(dug, a_gu)).astype(BF),
        jnp.where(lane == expert, high, jnp.where(lane == expert + 64, low, 0.0)).astype(BF),
    )
    to_a = mm(dug.T[: 2 * RANK], x).astype(BF)
    return both, (to_a[:RANK], to_a[RANK:], mm(ud.T[:RANK], dy).astype(BF))


def experts_kernel(
    own_first, order, xb, cot, routes, given, given_too, own_both,
    w_gate, w_up, w_down, maps,
    mixed, info, grads,
    count, info_t, place_t, both, x_s, c_s, dy_s, g_s, y_acc, dx_acc, ug_s, ud_acc, dud_s, dug_acc, a_gu, b_dn, acc,
):
    step, j = pl.program_id(0), pl.program_id(1)
    steps, tiles = pl.num_programs(0), pl.num_programs(1)
    e = order[step]
    length, width = xb.shape
    numbers = count.shape[1] - 1
    tile = w_gate.shape[2]
    hidden = (maps.shape[2] - 3 * width) // 3
    rows_of = 128
    skip = 2 * HALF if own_first else 0

    if grads.shape[2] > maps.shape[2]:
        grads[0, :, maps.shape[2] :] = jnp.zeros((RANK, grads.shape[2] - maps.shape[2]), BF)

    @pl.when((step == 0) & (j == 0))
    def _():
        if own_first:
            info_t[...], place_t[...] = given[...], given_too[...]
        else:
            route(given, given_too, routes, numbers, info_t, place_t)
        wide = iota((128, length), 0)
        named = [(wide == routes[k : k + 1, :]) & (wide < numbers) for k in range(2)]
        number = iota((128, 1), 0)
        counts = jnp.max(place_t[...], axis=1, keepdims=True) + 1.0
        padded = jnp.floor((counts + (rows_of - 1)) * (1.0 / rows_of))
        if own_first:
            ex = lax.axis_index("expert")
            padded = jnp.where((number == ex) | (number == other(ex, 1)), 0.0, padded)
        earlier = one_hot(iota((128, 128), 1) < iota((128, 128), 0))
        starts = rows_of * mm(earlier, jnp.broadcast_to(padded, (128, 128)).astype(BF))[:, :1]
        slots = starts + skip
        if own_first:
            slots = jnp.where(number == ex, 0.0, jnp.where(number == other(ex, 1), 1.0 * HALF, slots))
        at_slot = place_t[...] + slots
        for k in range(2):
            spot = jnp.sum(jnp.where(named[k], at_slot + 1.0, 0.0), axis=0, keepdims=True) - 1.0
            info_t[pl.ds(64 + k, 1), :] = spot
        info[...] = info_t[...].T
        for i in range(numbers):
            count[0, i] = jnp.sum(jnp.where(number == i, padded, 0.0)).astype(jnp.int32)
            count[1, i] = jnp.sum(jnp.where(number == i, starts, 0.0)).astype(jnp.int32)
        count[1, numbers] = jnp.sum(jnp.where(number < numbers, padded, 0.0)).astype(jnp.int32) * rows_of

    blocks = count[0, e]
    first = pl.multiple_of(count[1, e], rows_of)

    @pl.when((j == 0) & (blocks > 0))
    def _():
        a_gu[...] = padded_rows(maps[0, :, :width]) + padded_rows(maps[0, :, width : 2 * width], RANK)
        b_dn[...] = padded_rows(maps[0, :, 2 * width + 3 * hidden :])

    @pl.when((j == 0) & (blocks == 0))
    def _():
        grads[...] = jnp.zeros(grads.shape, BF)

    def work(n):
        rows = pl.ds(0, n)

        @pl.when(j == 0)
        def _():
            x, c, g, dy = take_rows(n, place_t[pl.ds(e, 1), :], info_t[pl.ds(e, 1), :], xb, cot)
            x_s[rows, :] = x
            c_s[rows, :] = c
            dy_s[rows, :] = dy
            g_s[rows, :] = jnp.broadcast_to(g, (n, 128))
            ug_s[rows, :] = mm_t(x, a_gu[...]).astype(BF)
            dud_s[rows, :] = mm_t(dy, b_dn[...]).astype(BF)

        at = pl.multiple_of(j * tile, tile)
        starts = [2 * width + i * hidden + at for i in range(3)]
        sums, parts = hidden_tile(
            x_s[rows, :], dy_s[rows, :], ug_s[rows, :], dud_s[rows, :], w_gate[0], w_up[0], w_down[0],
            padded_rows(maps[0, :, pl.ds(starts[0], tile)]),
            padded_rows(maps[0, :, pl.ds(starts[1], tile)], RANK),
            padded_rows(maps[0, :, pl.ds(starts[2], tile)]),
        )
        for start, part in zip(starts, parts):
            grads[0, :, pl.ds(start, tile)] = part
        kept = (y_acc, ud_acc, dx_acc, dug_acc)

        @pl.when(j == 0)
        def _():
            for ref, value in zip(kept, sums):
                ref[rows, :] = value

        @pl.when(j > 0)
        def _():
            for ref, value in zip(kept, sums):
                ref[rows, :] += value

        @pl.when(j == tiles - 1)
        def _():
            out, parts = close_rows(
                e, [ref[rows, :] for ref in kept], x_s[rows, :], c_s[rows, :], g_s[rows, :][:, :1], dy_s[rows, :],
                a_gu[...], b_dn[...],
            )
            to = pl.ds(first, n)
            both[to, :width], both[to, width : 2 * width], both[to, 2 * width :] = out
            grads[0, :, :width], grads[0, :, width : 2 * width] = parts[:2]
            grads[0, :, 2 * width + 3 * hidden : 3 * width + 3 * hidden] = parts[2]

    for number in range(1, 512 // rows_of + 1):
        pl.when(blocks == number)(functools.partial(work, number * rows_of))

    @pl.when((step == steps - 1) & (j == tiles - 1))
    def _():
        used = count[1, numbers]
        both[pl.ds(pl.multiple_of(used, rows_of), HALF), :] = jnp.zeros((HALF, both.shape[1]), BF)
        def combine(block, carry):
            at = pl.ds(pl.multiple_of(block * 256, 256), 256)
            g = info[at, :]
            spots = g[:, 64:66]

            def taken(start):
                slot = (iota((256, HALF), 1) + start).astype(F32)
                return one_hot((slot == spots[:, :1]) | (slot == spots[:, 1:2]))

            if own_first:
                acc[...] = mm(taken(0), own_both[:HALF, :]) + mm(taken(HALF), own_both[HALF:, :])
            else:
                acc[...] = jnp.zeros(acc.shape, F32)

            def add(part, carry):
                k0 = pl.multiple_of(part * HALF, HALF)
                acc[...] += mm(taken(k0 + skip), both[pl.ds(k0, HALF), :])
                return carry

            lax.fori_loop(0, (used + HALF - 1) // HALF, add, 0)
            mixed[at, :] = acc[...].astype(BF)
            return carry

        lax.fori_loop(0, length // 256, combine, 0)


def experts_both_ways(xb, cot, routes, given, given_too, w_gu, w_dn, maps, copies, own_both=None):
    length, width = xb.shape
    experts, hidden = w_dn.shape[0], w_dn.shape[1]
    tile = hidden // 2
    tiles = hidden // tile
    most = 2 * length + experts * 128
    total = 3 * width + 3 * hidden
    padded = -(-total // (copies * 128)) * copies * 128

    def whole(a):
        return pl.BlockSpec(a.shape, lambda e, j, order: (0,) * a.ndim, pipeline_mode=pl.Buffered(1))

    own_first = own_both is not None
    if own_first:
        order = other(2 * (lax.axis_index("expert") // 2), 2) + jnp.arange(2, dtype=jnp.int32)
    else:
        order = jnp.arange(experts, dtype=jnp.int32)
        own_both = jnp.zeros((16, 128), BF)
    resident = (xb, cot, routes, given, given_too, own_both)
    return pl.pallas_call(
        functools.partial(experts_kernel, own_first),
        out_shape=[
            jax.ShapeDtypeStruct((length, 2 * width + 128), BF),
            jax.ShapeDtypeStruct((length, 128), F32),
            jax.ShapeDtypeStruct((experts, RANK, padded), BF),
        ],
        grid_spec=pltpu.PrefetchScalarGridSpec(
            num_scalar_prefetch=1,
            grid=(order.shape[0], tiles),
            in_specs=[whole(a) for a in resident]
            + [
                pl.BlockSpec((1, width, tile), lambda e, j, order: (order[e], 0, j)),
                pl.BlockSpec((1, width, tile), lambda e, j, order: (order[e], 0, tiles + j)),
                pl.BlockSpec((1, tile, width), lambda e, j, order: (order[e], j, 0)),
                pl.BlockSpec((1, RANK, total), lambda e, j, order: (order[e], 0, 0)),
            ],
            out_specs=[
                pl.BlockSpec((length, 2 * width + 128), lambda e, j, order: (0, 0), pipeline_mode=pl.Buffered(1)),
                pl.BlockSpec((length, 128), lambda e, j, order: (0, 0), pipeline_mode=pl.Buffered(1)),
                pl.BlockSpec((1, RANK, padded), lambda e, j, order: (order[e], 0, 0)),
            ],
            scratch_shapes=[
            pltpu.SMEM((2, experts + 1), jnp.int32),
            pltpu.VMEM((128, length), F32),
            pltpu.VMEM((128, length), F32),
            pltpu.VMEM((most + HALF, 2 * width + 128), BF),
            pltpu.VMEM((512, width), BF),
            pltpu.VMEM((512, width), BF),
            pltpu.VMEM((512, width), BF),
            pltpu.VMEM((512, 128), F32),
            pltpu.VMEM((512, width), F32),
            pltpu.VMEM((512, width), F32),
            pltpu.VMEM((512, 128), BF),
            pltpu.VMEM((512, 128), F32),
            pltpu.VMEM((512, 128), BF),
            pltpu.VMEM((512, 128), F32),
            pltpu.VMEM((128, width), BF),
            pltpu.VMEM((128, width), BF),
            pltpu.VMEM((256, 2 * width + 128), F32),
        ],
        ),
        compiler_params=pltpu.CompilerParams(vmem_limit_bytes=60 * MIB),
        name="experts_both_ways",
    )(order, *resident, w_gu, w_gu, w_dn, maps)


def gather_experts(weights, senders):
    w_gu, w_dn, gu_down, gu_up, dn_down, dn_up = weights
    maps = jnp.concatenate(
        [gu_down[0, 0].T, gu_down[0, 1].T, gu_up[0, 0], gu_up[0, 1], dn_down[0].T, dn_up[0]], axis=1
    )
    to = (senders[:, None] * RANK + jnp.arange(RANK)[None, :]).reshape(-1)
    rows = mm((to[:, None] == jnp.arange(128)[None, :]).astype(BF), maps).astype(BF)
    rows = rows.reshape(senders.shape[0], RANK, -1)
    return (
        lax.all_gather(w_gu, "expert", axis=0, tiled=True),
        lax.all_gather(w_dn, "expert", axis=0, tiled=True),
        lax.all_to_all(rows, "expert", split_axis=0, concat_axis=0, tiled=True),
    )


BOTH = ("dp", "expert")


def sum_expert_maps(compact, spread):
    copies = lax.axis_size("dp")
    experts, rank, columns = compact.shape
    each = columns // copies
    parts = compact.reshape(experts, rank, copies, each).transpose(2, 0, 1, 3).reshape(copies * experts, rank, each)
    got = lax.all_to_all(parts, BOTH, split_axis=0, concat_axis=0, tiled=True)
    own = mm(spread, got.reshape(-1, each)).astype(BF)
    return lax.all_gather(own, "dp", axis=1, tiled=True)


def sum_attention_maps(compact, spread):
    devices = lax.axis_size("dp") * lax.axis_size("expert")
    maps, rank, width = compact.shape
    cuts = devices // maps
    parts = compact.reshape(maps, rank, cuts, width // cuts).transpose(0, 2, 1, 3).reshape(devices, rank, width // cuts)
    got = lax.all_to_all(parts, BOTH, split_axis=0, concat_axis=0, tiled=True)
    own = mm(spread, got.reshape(devices * rank, width // cuts)).astype(BF)
    whole = lax.all_gather(own[None], BOTH, axis=0, tiled=True)
    return whole.reshape(maps, cuts, 128, width // cuts).transpose(0, 2, 1, 3).reshape(maps, 128, width).astype(F32)


def body(
    exchange,
    tokens, cotangent, attention_norm_gain, query_key_value_weight, attention_output_weight,
    adapter_attention_down_maps, adapter_query_key_value_up_maps, adapter_output_up_map,
    experts_norm_gain, router_weight, constant_expert_mixing, constant_expert_vectors,
    expert_gate_up_weight, expert_down_weight, adapter_expert_gate_up_down_maps, adapter_expert_gate_up_up_maps,
    adapter_expert_down_down_maps, adapter_expert_down_up_maps,
    routes, router_logits_carried, picture_span_starts, sequence_adapter_index,
):
    groups = lax.axis_size("expert")
    width = tokens.shape[1]
    hidden = expert_down_weight.shape[1]
    first = lax.axis_index("dp") * groups
    senders = lax.dynamic_slice_in_dim(sequence_adapter_index, first, groups, 0)
    spans = picture_span_starts.reshape(-1)
    own = (
        expert_gate_up_weight, expert_down_weight, adapter_expert_gate_up_down_maps,
        adapter_expert_gate_up_up_maps, adapter_expert_down_down_maps, adapter_expert_down_up_maps,
    )
    outs = attention_forward(
        tokens, attention_norm_gain, query_key_value_weight, adapter_attention_down_maps, adapter_query_key_value_up_maps,
        attention_output_weight, adapter_output_up_map, experts_norm_gain, router_weight.T, constant_expert_mixing.T,
        spans, sequence_adapter_index,
        (*own, cotangent, routes.T, router_logits_carried.T) if exchange else (),
    )
    xa, q, k, v, ob, ua, uo, lse, h1, xb, lin, wqk, down_s, up_s, wr = outs[:15]
    weights = outs[15:18] if exchange else gather_experts(own, senders)
    given = outs[20:22] if exchange else (lin, router_logits_carried.T)
    mixed, info, expert_maps = experts_both_ways(
        xb, cotangent, routes.T, *given, *weights, lax.axis_size("dp"), outs[18] if exchange else None
    )
    backward = functools.partial(
        attention_backward, weights[1].shape[0], spans, h1, tokens, attention_norm_gain, query_key_value_weight, wqk,
        attention_output_weight, down_s, up_s, xa, q, k, v, ob, ua, uo, lse,
        mixed, cotangent, lin, info, constant_expert_vectors, experts_norm_gain, wr,
    )
    if exchange:
        takers = jnp.repeat(sequence_adapter_index, RANK)[None]
        grad_tokens, result, all_e, all_a = backward(expert_maps, outs[19], takers)
        return (result, grad_tokens, *unpack(all_e, all_a, hidden))
    grad_tokens, result, attention_maps = backward()
    to = (sequence_adapter_index[:, None] * RANK + jnp.arange(RANK)[None, :]).reshape(-1)
    spread = (jnp.arange(128)[:, None] == to[None, :]).astype(BF)
    of_expert = sum_expert_maps(expert_maps, spread).astype(F32)
    of_attention = sum_attention_maps(attention_maps, spread)
    ends = [0, width, 2 * width, 2 * width + hidden, 2 * width + 2 * hidden, 2 * width + 3 * hidden, 3 * width + 3 * hidden]
    gud0, gud1, guu0, guu1, dnd, dnu = (of_expert[:, a:b] for a, b in zip(ends, ends[1:]))
    return (
        result,
        grad_tokens,
        of_attention[:4].transpose(0, 2, 1),
        of_attention[4:7],
        of_attention[7],
        jnp.stack([gud0.T, gud1.T])[None],
        jnp.stack([guu0, guu1])[None],
        dnd.T[None],
        dnu[None],
    )


def solution(mesh):
    tokens, own = P(("dp", "expert"), None), P("expert", None, None)
    own4 = P("expert", None, None, None)
    in_specs = (tokens, tokens) + (P(),) * 10 + (own, own, own4, own4, own, own) + (tokens,) * 3 + (P(),)
    out_specs = (tokens, tokens, P(), P(), P(), own4, own4, own, own)
    exchange = dict(mesh.shape) == {"dp": 8, "expert": 4}
    return jax.shard_map(functools.partial(body, exchange), mesh=mesh, in_specs=in_specs, out_specs=out_specs, check_vma=False)
```
